32 devices in a mesh: date: 4 (over y, x), strip: 8 (over z, core).
Axes of the slice: x: 2, y: 2, z: 4, core: 2. Of those that a mesh axis runs over, the one named last changes fastest.
Arguments:
- slc: bfloat16 [2, 128, 256, 2048], P(None, 'date', None, 'strip'), may hold values from -180 to 180
- range_kernel: bfloat16 [128, 256, 256], P('date'), may hold values from -2.5 to 2.5, as said below
- azimuth_kernel: bfloat16 [128, 272, 2048], P('date', None, 'strip'), may hold values from -2.5 to 2.5, as said below
Outputs:
- coherence: float32 [16, 128, 2, 128, 128], P('date', 'strip')
The draws below stay inside these ranges and needn't reach their ends.
Inputs may be any that keep to these rules, and one draw needn't show every extreme that they name: range_kernel[d, r, s] is zero unless s - r lies in a run of 8 consecutive values that begins between -8 and 1; the run depends on r but not on d, and runs beginning at -8 and at 1 both occur. azimuth_kernel[d, k, a] is zero unless k - (a mod 256) lies in a run of 8 consecutive values that begins between 0 and 9; the run depends on a but not on d; in every strip the first pixel's run begins at 0 and the last pixel's at 9.
All inputs are finite; a program needn't handle non-finite values.
Results may differ from the reference program's by a relative error of at most 0.00051.
Values may be sent and summed in bfloat16 or wider, within the bound.
No kernel may reach another device: no remote copies, remote signals or barrier semaphores. Data moves between devices by JAX's collectives and lax.ppermute only.
A program may use at most 192 MiB of HBM per device.

```python
import math
import jax
import jax.numpy as jnp
from jax import lax

DATES = 128
RG = 256
AZ_DEV = 256
TAPS = 8
HALO = 8
WIN = 32
AZ = 2048
N_STRIP = 8


def draw_slc(key, part):
    key = jax.random.fold_in(key, 11)
    subkeys = jax.random.split(key, 5)
    common = jnp.clip(jax.random.normal(subkeys[0], (2, RG, AZ)), -5.0, 5.0)
    noise_part = jnp.clip(jax.random.normal(subkeys[1], (2, DATES, RG, AZ)), -5.0, 5.0)
    pixel_amp = jnp.exp(jax.random.uniform(subkeys[4], (RG, AZ), minval=math.log(0.3), maxval=math.log(3.0)))
    date_amp = jnp.exp(jax.random.uniform(subkeys[2], (DATES,), minval=math.log(0.5), maxval=math.log(5.0)))
    phase_angle = jax.random.uniform(subkeys[3], (DATES,), minval=-math.pi, maxval=math.pi)
    cosine = jnp.cos(phase_angle)[:, None, None]
    sine_part = jnp.sin(phase_angle)[:, None, None]
    rotated_real = common[0][None] * cosine - common[1][None] * sine_part
    rotated_imag = common[0][None] * sine_part + common[1][None] * cosine
    samples = jnp.stack([rotated_real, rotated_imag]) + 0.8 * noise_part
    return (samples * date_amp[None, :, None, None] * pixel_amp[None, None]).astype(jnp.bfloat16)


def draw_range_kernel(key, part):
    key = jax.random.fold_in(key, 23)
    subkeys = jax.random.split(key, 3)
    positions = jnp.arange(RG, dtype=jnp.int32)
    offsets = jax.random.randint(subkeys[0], (RG,), -4, 6)
    offsets = jnp.where(positions == RG // 2, -4, jnp.where(positions == RG // 2 + 1, 5, offsets))
    shared_taps = jnp.clip(jax.random.normal(subkeys[1], (RG, TAPS)), -4.0, 4.0)
    date_taps = jnp.clip(jax.random.normal(subkeys[2], (DATES, RG, TAPS)), -4.0, 4.0)
    tap_weights = 0.4 * (shared_taps[None] + 0.4 * date_taps)
    in_column = positions[None, None, :]
    out_row = positions[None, :, None]
    kernel_sum = jnp.zeros((DATES, RG, RG), jnp.float32)
    for tap_index in range(TAPS):
        target = out_row + offsets[None, :, None] + tap_index - 4
        kernel_sum = kernel_sum + jnp.where(in_column == target, tap_weights[:, :, tap_index][:, :, None], 0.0)
    return kernel_sum.astype(jnp.bfloat16)


def draw_azimuth_kernel(key, part):
    key = jax.random.fold_in(key, 37)
    subkeys = jax.random.split(key, 3)
    local_pos = jnp.arange(AZ, dtype=jnp.int32) % AZ_DEV
    offsets = jax.random.randint(subkeys[0], (AZ,), -4, 6)
    offsets = jnp.where(local_pos == 0, -4, jnp.where(local_pos == AZ_DEV - 1, 5, offsets))
    shared_taps = jnp.clip(jax.random.normal(subkeys[1], (AZ, TAPS)), -4.0, 4.0)
    date_taps = jnp.clip(jax.random.normal(subkeys[2], (DATES, AZ, TAPS)), -4.0, 4.0)
    tap_weights = 0.4 * (shared_taps[None] + 0.4 * date_taps)
    in_row = jnp.arange(AZ_DEV + 2 * HALO, dtype=jnp.int32)[None, :, None]
    start = (local_pos + HALO + offsets - 4)[None, None, :]
    kernel_sum = jnp.zeros((DATES, AZ_DEV + 2 * HALO, AZ), jnp.float32)
    for tap_index in range(TAPS):
        kernel_sum = kernel_sum + jnp.where(in_row == start + tap_index, tap_weights[:, :, tap_index][:, None, :], 0.0)
    return kernel_sum.astype(jnp.bfloat16)


def setup_inputs(seed: int = 0) -> dict:
    key_list = jax.random.split(jax.random.key(seed), 4)
    slc = draw_slc(jax.random.fold_in(key_list[3], 71), 0)
    range_kernel = draw_range_kernel(jax.random.fold_in(key_list[3], 71), 0)
    azimuth_kernel = draw_azimuth_kernel(jax.random.fold_in(key_list[3], 71), 0)
    return {"slc": slc, "range_kernel": range_kernel, "azimuth_kernel": azimuth_kernel}


epsilon = 1e-06

def coherence_of(moment, date_count):
    real_part = moment[..., :date_count, :date_count] + moment[..., date_count:, date_count:]
    imag_part = moment[..., date_count:, :date_count] - moment[..., :date_count, date_count:]
    power_sum = jnp.diagonal(real_part, axis1=-2, axis2=-1) + epsilon
    inverse_root = lax.rsqrt(power_sum)
    pair_scale = inverse_root[..., :, None] * inverse_root[..., None, :]
    return jnp.stack([real_part * pair_scale, imag_part * pair_scale], axis=-3)

def reference(slc, range_kernel, azimuth_kernel):
    slc_padded = jnp.pad(slc, ((0, 0), (0, 0), (0, 0), (HALO, HALO)))
    range_float = range_kernel.astype(jnp.float32)

    def resample_strip(strip_index):
        rim_rows = lax.dynamic_slice_in_dim(slc_padded, strip_index * AZ_DEV, AZ_DEV + 2 * HALO, 3)
        ranged = jnp.einsum('drs,cdsa->cdra', range_float, rim_rows.astype(jnp.float32)).astype(jnp.bfloat16)
        kernel = lax.dynamic_slice_in_dim(azimuth_kernel, strip_index * AZ_DEV, AZ_DEV, 2)
        return jnp.einsum('cdrp,dpa->cdra', ranged.astype(jnp.float32), kernel.astype(jnp.float32)).astype(jnp.bfloat16)
    shifted = lax.map(resample_strip, jnp.arange(N_STRIP, dtype=jnp.int32))
    shifted = jnp.moveaxis(shifted, 0, 3).reshape(2, DATES, RG, AZ)
    half_window = WIN // 2
    margin = WIN // 4
    pixel_grid = jnp.pad(shifted, ((0, 0), (0, 0), (margin, margin), (margin, margin)))
    range_blocks = RG // half_window + 1
    az_blocks = AZ // half_window + 1

    def column_moments(column):
        column_pixels = lax.dynamic_slice_in_dim(pixel_grid, column * half_window, half_window, 3)
        column_pixels = column_pixels.reshape(2, DATES, range_blocks, half_window, half_window)
        column_pixels = column_pixels.transpose(2, 0, 1, 3, 4).reshape(range_blocks, 2 * DATES, half_window * half_window)
        column_pixels = column_pixels.astype(jnp.float32)
        return jnp.einsum('bip,bjp->bij', column_pixels, column_pixels)

    def advance(previous, column):
        current = column_moments(column)
        window_moment = previous[:-1] + previous[1:] + current[:-1] + current[1:]
        return (current, coherence_of(window_moment, DATES))
    first_moments = column_moments(jnp.int32(0))
    unused, result = lax.scan(advance, first_moments, jnp.arange(1, az_blocks, dtype=jnp.int32))
    return jnp.transpose(result, (1, 0, 2, 3, 4))
```

```python
import functools

import jax
import jax.numpy as jnp
from jax import lax
from jax.experimental import pallas as pl
from jax.experimental.pallas import tpu as pltpu
from jax.sharding import PartitionSpec as P

HALO = 8
SIDE = 16
PIX = SIDE * SIDE
LANES = 128
SUB = 8
DBLK = 16
EPS = 1e-06
VMEM = 56 * 1024 * 1024

bf16 = jnp.bfloat16
f32 = jnp.float32


def params():
    return pltpu.CompilerParams(vmem_limit_bytes=VMEM)


def block_transpose(rows):
    group = lax.broadcasted_iota(jnp.int32, rows[0].shape, 1) // SIDE
    for step in (4, 2, 1):
        low = (group & step) == 0
        later = list(rows)
        for r in range(8):
            if r & step == 0:
                a, b = rows[r], rows[r + step]
                later[r] = jnp.where(low, a, pltpu.roll(b, SIDE * step, 1))
                later[r + step] = jnp.where(low, pltpu.roll(a, LANES - SIDE * step, 1), b)
        rows = later
    return rows


def interior_kernel(spans, dest_rows, me_ref, slc_ref, rk_ref, ak_ref, *refs):
    *outs, plane = refs
    step, steps = pl.program_id(0), pl.num_programs(0)
    per_step, n_rows = slc_ref.shape[1], slc_ref.shape[2]
    lines = 2 * DBLK
    partners = len(outs) // len(spans)
    row_blocks = outs[0].shape[0]
    halves = plane.shape[0]

    @pl.when(step == 0)
    def _():
        zero = jnp.zeros((halves, SUB * lines, LANES), f32)
        plane[:, : SUB * lines, :] = zero
        plane[:, (SUB + n_rows) * lines :, :] = zero

    for i in range(per_step):
        kernel = ak_ref[i].astype(f32)[HALO : HALO + n_rows]
        kernel = pltpu.roll(kernel, HALO, 1).astype(bf16)
        for c in range(2):
            ranged = jnp.dot(rk_ref[i], slc_ref[c, i], preferred_element_type=f32).astype(bf16)
            moved = jnp.dot(ranged, kernel, preferred_element_type=f32)
            line = SUB * lines + c * DBLK + step * per_step + i
            for h in range(halves):
                plane[h, pl.ds(line, n_rows, stride=lines), :] = moved[:, h * LANES : (h + 1) * LANES]

    @pl.when(step == steps - 1)
    def _():
        me = me_ref[0]
        for k in range(partners):
            base = (me ^ k) * dest_rows

            def blocks(j, carry):
                first = base + j * SIDE
                for half in range(2):
                    for h in range(halves):
                        rows = []
                        for r in range(8):
                            start = pl.multiple_of((first + half * 8 + r) * lines, lines)
                            rows.append(plane[h, pl.ds(start, lines), :].astype(bf16))
                        cols = block_transpose(rows)
                        for g in range(8):
                            column = h * 8 + g
                            for s, (lo, hi) in enumerate(spans):
                                if lo <= column < hi:
                                    out = outs[s * partners + k]
                                    for c in range(2):
                                        out[j, column - lo, c, :, half * LANES : (half + 1) * LANES] = cols[g][
                                            c * DBLK : (c + 1) * DBLK
                                        ]
                return carry

            lax.fori_loop(0, row_blocks, blocks, 0)


def interior(me, slc, rk, ak, part, spans, partners):
    n_rows, n_az = slc.shape[2], slc.shape[3]
    dest_rows = n_rows // partners
    row_blocks = dest_rows // SIDE + 1
    per_step = 2
    steps = DBLK // per_step
    shapes = [
        jax.ShapeDtypeStruct((row_blocks, hi - lo, 2, DBLK, PIX), bf16)
        for lo, hi in spans
        for _ in range(partners)
    ]
    grid = pltpu.PrefetchScalarGridSpec(
        num_scalar_prefetch=1,
        grid=(steps,),
        in_specs=[
            pl.BlockSpec((2, per_step, n_rows, n_az), lambda t, m: (0, part * steps + t, 0, 0)),
            pl.BlockSpec((per_step, n_rows, n_rows), lambda t, m: (part * steps + t, 0, 0)),
            pl.BlockSpec((per_step, ak.shape[1], n_az), lambda t, m: (part * steps + t, 0, 0)),
        ],
        out_specs=[pl.BlockSpec(s.shape, lambda t, m: (0, 0, 0, 0, 0)) for s in shapes],
        scratch_shapes=[pltpu.VMEM((n_az // LANES, (n_rows + 2 * SUB) * 2 * DBLK, LANES), f32)],
    )
    flat = pl.pallas_call(
        functools.partial(interior_kernel, spans, dest_rows),
        grid_spec=grid,
        out_shape=shapes,
        compiler_params=params(),
        cost_estimate=pl.CostEstimate(flops=DBLK * 8 * 256**3, bytes_accessed=16 << 20, transcendentals=0),
        name=f"interior_{part}",
    )(me, slc, rk, ak)
    return [flat[s * partners : (s + 1) * partners] for s in range(len(spans))]


def rim_kernel(dest_rows, me_ref, edge_ref, rk_ref, ak_ref, *refs):
    *outs, plane = refs
    step, steps = pl.program_id(0), pl.num_programs(0)
    per_step, n_rows = rk_ref.shape[0], rk_ref.shape[1]
    n_dates = outs[0].shape[2]
    lines = 2 * n_dates
    row_blocks = outs[0].shape[0]
    eighths = n_rows // 8

    @pl.when(step == 0)
    def _():
        zero = jnp.zeros((lines, LANES), f32)
        plane[:lines, :] = zero
        plane[(eighths + 1) * lines :, :] = zero

    row = lax.broadcasted_iota(jnp.int32, (n_rows, 2 * LANES), 0)
    lane = lax.broadcasted_iota(jnp.int32, (n_rows, 2 * LANES), 1)
    own = (row % 8) == (lane % LANES) // SIDE
    gather = (
        lax.broadcasted_iota(jnp.int32, (eighths, n_rows), 1) // 8
        == lax.broadcasted_iota(jnp.int32, (eighths, n_rows), 0)
    ).astype(f32).astype(bf16)
    for i in range(per_step):
        ranged = jnp.dot(rk_ref[i], edge_ref[i], preferred_element_type=f32).astype(bf16)
        moved = jnp.dot(ranged, ak_ref[i], preferred_element_type=f32)
        moved = jnp.where(own, moved, 0.0).astype(bf16)
        packed = jnp.dot(gather, moved, preferred_element_type=f32)
        for c in range(2):
            line = lines + c * n_dates + step * per_step + i
            plane[pl.ds(line, eighths, stride=lines), :] = packed[:, c * LANES : (c + 1) * LANES]

    @pl.when(step == steps - 1)
    def _():
        me = me_ref[0]
        for k in range(len(outs)):
            base = (me ^ k) * (dest_rows // 8)
            for j in range(row_blocks):
                for half in range(2):
                    start = pl.multiple_of((base + 2 * j + half) * lines, lines)
                    values = plane[pl.ds(start, lines), :].astype(bf16)
                    for c in range(2):
                        outs[k][j, c, :, half * LANES : (half + 1) * LANES] = values[
                            c * n_dates : (c + 1) * n_dates
                        ]


def rim(me, edge, rk, ak_edge, partners):
    n_dates, n_rows = rk.shape[0], rk.shape[1]
    dest_rows = n_rows // partners
    row_blocks = dest_rows // SIDE + 1
    per_step = 4
    shape = jax.ShapeDtypeStruct((row_blocks, 2, n_dates, PIX), bf16)
    grid = pltpu.PrefetchScalarGridSpec(
        num_scalar_prefetch=1,
        grid=(n_dates // per_step,),
        in_specs=[
            pl.BlockSpec((per_step, n_rows, LANES), lambda t, m: (t, 0, 0)),
            pl.BlockSpec((per_step, n_rows, n_rows), lambda t, m: (t, 0, 0)),
            pl.BlockSpec((per_step, LANES, 2 * LANES), lambda t, m: (t, 0, 0)),
        ],
        out_specs=[pl.BlockSpec(shape.shape, lambda t, m: (0, 0, 0, 0))] * partners,
        scratch_shapes=[pltpu.VMEM(((n_rows // 8 + 2) * 2 * n_dates, LANES), f32)],
    )
    return pl.pallas_call(
        functools.partial(rim_kernel, dest_rows),
        grid_spec=grid,
        out_shape=[shape] * partners,
        compiler_params=params(),
        cost_estimate=pl.CostEstimate(flops=n_dates * 256**3, bytes_accessed=10 << 20, transcendentals=0),
        name="rim",
    )(me, edge, rk, ak_edge)


def block_moment(pixels):
    n = pixels.shape[0] // 2
    m = lax.dot_general(pixels, pixels, (((1,), (1,)), ((), ())), preferred_element_type=f32)
    return m[:n, :n] + m[n:, n:], m[n:, :n] - m[:n, n:]


def store_coherence(out, index, real, imag):
    n = real.shape[0]
    eye = lax.broadcasted_iota(jnp.int32, (n, n), 0) == lax.broadcasted_iota(jnp.int32, (n, n), 1)
    diagonal = jnp.where(eye, real, 0.0)
    column = lax.rsqrt(jnp.sum(diagonal, axis=1, keepdims=True) + EPS)
    row = lax.rsqrt(jnp.sum(diagonal, axis=0, keepdims=True) + EPS)
    scale = column * row
    out[(*index, 0)] = real * scale
    out[(*index, 1)] = imag * scale


def column_sums(read, scratch, row_blocks, emit):
    before = None
    for j in range(row_blocks):
        read(j, scratch.at[j])
        now = block_moment(scratch[j])
        if before is not None:
            emit(j - 1, before[0] + now[0], before[1] + now[1])
        before = now


def rim_gram_kernel(partners, me_ref, *refs):
    own, before, after = (refs[i * partners : (i + 1) * partners] for i in range(3))
    out, pixels = refs[3 * partners :]
    row_blocks, _, n, _ = own[0].shape
    me = me_ref[0]
    total = n * partners
    for end in range(2):

        def read(j, scratch):
            for k in range(partners):
                for c in range(2):
                    left, right = (before[k], own[k]) if end == 0 else (own[k], after[k])
                    lane = lax.broadcasted_iota(jnp.int32, (n, PIX), 1)
                    value = jnp.where(lane % SIDE < 8, left[j, c], right[j, c])
                    at = pl.multiple_of(c * total + (me ^ k) * n, SIDE)
                    scratch[pl.ds(at, n), :] = value

        def emit(u, real, imag):
            out[end, u, 0] = real
            out[end, u, 1] = imag

        column_sums(read, pixels, row_blocks, emit)


def rim_gram(me, own, before, after):
    partners = len(own)
    row_blocks, _, n, _ = own[0].shape
    total = n * partners
    whole = pl.BlockSpec(memory_space=pltpu.VMEM)
    return pl.pallas_call(
        functools.partial(rim_gram_kernel, partners),
        in_specs=[pl.BlockSpec(memory_space=pltpu.SMEM)] + [whole] * (3 * partners),
        out_specs=whole,
        out_shape=jax.ShapeDtypeStruct((2, row_blocks - 1, 2, total, total), f32),
        scratch_shapes=[pltpu.VMEM((row_blocks, 2 * total, PIX), bf16)],
        compiler_params=params(),
        cost_estimate=pl.CostEstimate(flops=20 * 256**3, bytes_accessed=4 << 20, transcendentals=0),
        name="rim_gram",
    )(me, *own, *before, *after)


def gram_kernel(partners, parts, columns, closing, me_ref, *refs):
    pieces = refs[: partners * parts]
    state, end = refs[partners * parts : partners * parts + 2]
    out, state_out, held, pixels = refs[-4:]
    step = pl.program_id(0)
    row_blocks = pieces[0].shape[0]
    me = me_ref[0]
    total = pixels.shape[1] // 2

    @pl.when(step == 0)
    def _():
        held[...] = state[0]

    def work():
        def read(j, scratch):
            for k in range(partners):
                for p in range(parts):
                    for c in range(2):
                        at = pl.multiple_of(c * total + (me ^ k) * (parts * DBLK) + p * DBLK, DBLK)
                        scratch[pl.ds(at, DBLK), :] = pieces[k * parts + p][j, 0, c]

        def emit(u, real, imag):
            store_coherence(out, (u, 0), held[u, 0] + real, held[u, 1] + imag)
            held[u, 0] = real
            held[u, 1] = imag

        column_sums(read, pixels, row_blocks, emit)

    if closing:
        pl.when(step < columns)(work)

        @pl.when(step == columns)
        def _():
            for u in range(row_blocks - 1):
                store_coherence(out, (u, 0), held[u, 0] + end[0, u, 0], held[u, 1] + end[0, u, 1])
    else:
        work()

    @pl.when(step == pl.num_programs(0) - 1)
    def _():
        state_out[0] = held[...]


def gram(me, pieces, offsets, columns, first, state, state_at, ends, result, out_shape, closing):
    partners, parts = len(pieces), len(pieces[0])
    row_blocks = pieces[0][0].shape[0]
    total = out_shape.shape[-1]
    grid_steps = columns + (1 if closing else 0)

    def piece_spec(p):
        return pl.BlockSpec(
            (row_blocks, 1, 2, DBLK, PIX),
            lambda t, m: (0, offsets[p] + jnp.minimum(t, columns - 1), 0, 0, 0),
        )

    state_block = (1, row_blocks - 1, 2, total, total)
    in_specs = [piece_spec(p) for _ in range(partners) for p in range(parts)]
    in_specs += [
        pl.BlockSpec(state_block, lambda t, m: (state_at, 0, 0, 0, 0)),
        pl.BlockSpec(state_block, lambda t, m: (1, 0, 0, 0, 0)),
    ]
    operands = [x for k in pieces for x in k] + [state, ends]
    aliases = {}
    if result is not None:
        in_specs.append(pl.BlockSpec(memory_space=pl.ANY))
        aliases = {1 + len(operands): 0}
        operands.append(result)
    grid = pltpu.PrefetchScalarGridSpec(
        num_scalar_prefetch=1,
        grid=(grid_steps,),
        in_specs=in_specs,
        out_specs=[
            pl.BlockSpec((row_blocks - 1, 1, 2, total, total), lambda t, m: (0, first - 1 + t, 0, 0, 0)),
            pl.BlockSpec(state_block, lambda t, m: (0, 0, 0, 0, 0)),
        ],
        scratch_shapes=[
            pltpu.VMEM((row_blocks - 1, 2, total, total), f32),
            pltpu.VMEM((row_blocks, 2 * total, PIX), bf16),
        ],
    )
    return pl.pallas_call(
        functools.partial(gram_kernel, partners, parts, columns, closing),
        grid_spec=grid,
        out_shape=[out_shape, jax.ShapeDtypeStruct(state_block, f32)],
        input_output_aliases=aliases,
        compiler_params=params(),
        cost_estimate=pl.CostEstimate(flops=columns * 10 * 256**3, bytes_accessed=columns << 21, transcendentals=0),
        name=f"gram_{first}",
    )(me, *operands)


def shift(value, axis, by):
    n = lax.axis_size(axis)
    pairs = [(i, i + by) for i in range(n) if 0 <= i + by < n]
    return lax.ppermute(value, axis, pairs)


def exchange(blocks):
    n = lax.axis_size("date")
    got = [blocks[0]]
    for k in range(1, n):
        got.append(lax.ppermute(blocks[k], "date", [(i, i ^ k) for i in range(n)]))
    return got


def edge_operands(slc, ak):
    n_az = slc.shape[3]
    first, last = slc[..., :SUB], slc[..., n_az - SUB :]
    left, right = shift(last, "strip", 1), shift(first, "strip", -1)
    pad = jnp.zeros((*slc.shape[:3], 16), bf16)
    edge = jnp.concatenate([slc[..., n_az - 16 :], right, left, slc[..., :16], pad], axis=3)
    edge = jnp.concatenate([edge[0], edge[1]], axis=2)
    at_end = ak[:, n_az - 8 : n_az + 16, n_az - 8 :]
    at_start = ak[:, :24, :8]
    block = jnp.concatenate(
        [
            jnp.pad(at_end, ((0, 0), (0, 0), (0, 8))),
            jnp.pad(at_start, ((0, 0), (0, 0), (8, 0))),
        ],
        axis=1,
    )
    block = jnp.tile(block, (1, 1, 8))
    weights = jnp.concatenate(
        [
            jnp.pad(block, ((0, 0), (0, 16), (0, LANES))),
            jnp.pad(block, ((0, 0), (0, 16), (LANES, 0))),
        ],
        axis=1,
    )
    return edge, weights


def on_device(slc, range_kernel, azimuth_kernel):
    partners = lax.axis_size("date")
    n_dates, n_rows, n_az = slc.shape[1:]
    total = n_dates * partners
    columns = n_az // SIDE
    me = lax.axis_index("date").astype(jnp.int32).reshape(1)
    parts = n_dates // DBLK
    bounds = [1, 6, 10, 13, columns]
    spans = list(zip(bounds[:-1], bounds[1:]))

    sent = []
    for part in range(parts - 1):
        sent.append(interior(me, slc, range_kernel, azimuth_kernel, part, [(1, columns)], partners))
    early = [exchange(s[0]) for s in sent]
    edge, weights = edge_operands(slc, azimuth_kernel)
    last = interior(me, slc, range_kernel, azimuth_kernel, parts - 1, spans, partners)
    rims = exchange(rim(me, edge, range_kernel, weights, partners))
    before = [shift(x, "strip", 1) for x in rims]
    after = [shift(x, "strip", -1) for x in rims]
    late = [exchange(x) for x in last]
    ends = rim_gram(me, rims, before, after)

    dest_windows = n_rows // partners // SIDE
    out_shape = jax.ShapeDtypeStruct((dest_windows, columns, 2, total, total), f32)
    result, state = None, ends
    for s, (lo, hi) in enumerate(spans):
        pieces = [[e[k] for e in early] + [late[s][k]] for k in range(partners)]
        offsets = [lo - 1] * (parts - 1) + [0]
        result, state = gram(
            me, pieces, offsets, hi - lo, lo, state, 0, ends, result, out_shape, closing=s == len(spans) - 1
        )
    return result


def solution(mesh):
    in_specs = (P(None, "date", None, "strip"), P("date", None, None), P("date", None, "strip"))
    out_specs = P("date", "strip", None, None, None)
    return jax.shard_map(on_device, mesh=mesh, in_specs=in_specs, out_specs=out_specs, check_vma=False)
```

```python
import functools

import jax
import jax.numpy as jnp
from jax import lax
from jax.experimental import pallas as pl
from jax.experimental.pallas import tpu as pltpu
from jax.sharding import PartitionSpec as P

HALO = 8
SIDE = 16
PIX = SIDE * SIDE
LANES = 128
SUB = 8
DBLK = 16
EPS = 1e-06
VMEM = 56 * 1024 * 1024
COST = pl.CostEstimate(flops=1, bytes_accessed=1, transcendentals=0)

bf16 = jnp.bfloat16
f32 = jnp.float32


def params():
    return pltpu.CompilerParams(vmem_limit_bytes=VMEM)


def gather_groups(rows):
    group = lax.broadcasted_iota(jnp.int32, rows[0].shape, 1) // SIDE
    turned = [rows[0]] + [pltpu.roll(rows[r], SIDE * r, 1) for r in range(1, 8)]
    held = [turned[-i % 8] for i in range(8)]
    for step in (1, 2, 4):
        low = (group & step) == 0
        held = [jnp.where(low, held[i], held[(i - step) % 8]) for i in range(8)]
    return held


def interior_kernel(spans, dest_rows, part, per_step, me_ref, slc_any, rk_any, ak_any, *refs):
    own_ref, first_ref, last_ref, *refs = refs
    *refs, slc_ref, rk_ref, ak_ref, turned, plane, ranged, in_sems, out_sems = refs
    outs, stage = refs[: len(refs) - len(spans)], refs[len(refs) - len(spans) :]
    steps = DBLK // per_step
    n_rows, n_az = slc_ref.shape[2:]
    lines = 2 * DBLK
    partners = len(outs) // len(spans)
    row_blocks = outs[0].shape[0]
    halves = plane.shape[0]

    def fetch(step):
        here = pl.ds(step * per_step, per_step)
        there = pl.ds(part * DBLK + step * per_step, per_step)
        return [
            pltpu.make_async_copy(rk_any.at[there], rk_ref.at[here], in_sems.at[step, 0]),
            pltpu.make_async_copy(slc_any.at[0, there], slc_ref.at[0, here], in_sems.at[step, 1]),
            pltpu.make_async_copy(slc_any.at[1, there], slc_ref.at[1, here], in_sems.at[step, 2]),
            pltpu.make_async_copy(ak_any.at[there], ak_ref.at[here], in_sems.at[step, 3]),
        ]

    def start(step, carry):
        for copy in fetch(step):
            copy.start()
        return carry

    def wait(step):
        for copy in fetch(step):
            copy.wait()

    def along_range(step):
        for n in range(per_step):
            i = step * per_step + n
            for c in range(2):
                value = jnp.dot(rk_ref[i], slc_ref[c, i], preferred_element_type=f32)
                ranged[i, c * n_rows : (c + 1) * n_rows, :] = value.astype(bf16)

    def prepare(step):
        for n in range(per_step):
            i = step * per_step + n
            kernel = ak_ref[i].astype(f32)[HALO : HALO + n_rows]
            turned[i] = pltpu.roll(kernel, HALO, 1).astype(bf16)

    def along_azimuth(step):
        for n in range(per_step):
            i = step * per_step + n
            moved = jnp.dot(ranged[i], turned[i], preferred_element_type=f32)
            for c in range(2):
                line = SUB * lines + c * DBLK + i
                for h in range(halves):
                    plane[h, pl.ds(line, n_rows, stride=lines), :] = moved[
                        c * n_rows : (c + 1) * n_rows, h * LANES : (h + 1) * LANES
                    ]

    lax.fori_loop(0, steps, start, 0)
    zero = jnp.zeros((SUB * lines, LANES), f32)
    for h in range(halves):
        plane[h, : SUB * lines, :] = zero
        plane[h, (SUB + n_rows) * lines :, :] = zero
    wait(0)
    along_range(0)
    prepare(0)

    def resample(step, carry):
        later = jnp.minimum(step + 1, steps - 1)
        pl.when(step + 1 < steps)(lambda: wait(later))
        along_azimuth(step)
        along_range(later)
        prepare(later)
        return carry

    lax.fori_loop(0, steps, resample, 0)

    me = me_ref[0]
    copies = [
        pltpu.make_async_copy(stage[n // partners].at[n % partners], outs[n], out_sems.at[n]) for n in range(len(outs))
    ]

    for k in [*range(1, partners), 0]:
        base = (me ^ k) * dest_rows

        def blocks(j, carry):
            for half in range(2):
                for h in range(halves):
                    rows = []
                    for r in range(8):
                        at = pl.multiple_of((base + j * SIDE + half * 8 + r) * lines, lines)
                        rows.append(plane[h, pl.ds(at, lines), :].astype(bf16))
                    cols = gather_groups(rows)
                    for g in range(8):
                        column = h * 8 + g
                        for s, (lo, hi) in enumerate(spans):
                            if lo <= column < hi:
                                for c in range(2):
                                    stage[s][k, j, column - lo, c, :, half * LANES : (half + 1) * LANES] = cols[g][
                                        c * DBLK : (c + 1) * DBLK
                                    ]
            return carry

        lax.fori_loop(0, row_blocks, blocks, 0)
        for s in range(len(spans)):
            copies[s * partners + k].start()

    pick_row = lax.broadcasted_iota(jnp.int32, (2 * SIDE, n_az), 0)
    pick_col = lax.broadcasted_iota(jnp.int32, (2 * SIDE, n_az), 1)
    pick = (pick_col == jnp.where(pick_row < SIDE, pick_row, pick_row + n_az - 2 * SIDE)).astype(f32).astype(bf16)

    def edges(step, carry):
        for n in range(4):
            i = step * 4 + n
            both = lax.dot_general(pick, ranged[i], (((1,), (1,)), ((), ())), preferred_element_type=f32)
            parts = [both[:, c * n_rows : (c + 1) * n_rows] for c in range(2)]
            for c in range(2):
                own_ref[i, c] = parts[c].astype(bf16)
            first_ref[i] = jnp.concatenate([p[:SUB] for p in parts], axis=0).astype(bf16)
            last_ref[i] = jnp.concatenate([p[2 * SIDE - SUB :] for p in parts], axis=0).astype(bf16)
        return carry

    lax.fori_loop(0, DBLK // 4, edges, 0)
    for copy in copies:
        copy.wait()


def interior(me, slc, rk, ak, part, spans, partners):
    n_rows, n_az = slc.shape[2], slc.shape[3]
    dest_rows = n_rows // partners
    row_blocks = dest_rows // SIDE + 1
    per_step = 2
    steps = DBLK // per_step
    shapes = [
        jax.ShapeDtypeStruct((row_blocks, hi - lo, 2, DBLK, PIX), bf16)
        for lo, hi in spans
        for _ in range(partners)
    ]
    edge_shapes = [
        jax.ShapeDtypeStruct((DBLK, 2, 2 * SIDE, n_rows), bf16),
        jax.ShapeDtypeStruct((DBLK, 2 * SUB, n_rows), bf16),
        jax.ShapeDtypeStruct((DBLK, 2 * SUB, n_rows), bf16),
    ]
    whole = pl.BlockSpec(memory_space=pltpu.VMEM)
    anywhere = pl.BlockSpec(memory_space=pl.ANY)
    own, first, last, *flat = pl.pallas_call(
        functools.partial(interior_kernel, spans, dest_rows, part, per_step),
        in_specs=[pl.BlockSpec(memory_space=pltpu.SMEM)] + [anywhere] * 3,
        out_specs=[whole] * 3 + [anywhere] * len(shapes),
        out_shape=edge_shapes + shapes,
        scratch_shapes=[pltpu.VMEM((partners, *x.shape), bf16) for x in shapes[::partners]]
        + [
            pltpu.VMEM((2, DBLK, n_rows, n_az), bf16),
            pltpu.VMEM((DBLK, n_rows, n_rows), bf16),
            pltpu.VMEM((DBLK, *ak.shape[1:]), bf16),
            pltpu.VMEM((DBLK, n_rows, n_az), bf16),
            pltpu.VMEM((n_az // LANES, (n_rows + 2 * SUB) * 2 * DBLK, LANES), f32),
            pltpu.VMEM((DBLK, 2 * n_rows, n_az), bf16),
            pltpu.SemaphoreType.DMA((steps, 4)),
            pltpu.SemaphoreType.DMA((len(shapes),)),
        ],
        compiler_params=params(),
        cost_estimate=COST,
        name=f"interior_{part}",
    )(me, slc, rk, ak)
    return own, first, last, [flat[s * partners : (s + 1) * partners] for s in range(len(spans))]


def rim_kernel(dest_rows, parts, me_ref, *refs):
    operands, outs, plane = refs[: 4 * parts], refs[4 * parts : -1], refs[-1]
    step, steps = pl.program_id(0), pl.num_programs(0)
    per_step, n_az = operands[0].shape[0], operands[3].shape[2]
    n_rows = operands[0].shape[3]
    n_dates = outs[0].shape[2]
    lines = 2 * n_dates
    row_blocks = outs[0].shape[0]
    eighths = n_rows // 8

    @pl.when(step == 0)
    def _():
        zero = jnp.zeros((lines, LANES), f32)
        plane[:lines, :] = zero
        plane[(eighths + 1) * lines :, :] = zero

    row = lax.broadcasted_iota(jnp.int32, (n_rows, LANES), 0)
    lane = lax.broadcasted_iota(jnp.int32, (n_rows, LANES), 1)
    own = (row % 8) == lane // SIDE
    gather = (
        lax.broadcasted_iota(jnp.int32, (eighths, n_rows), 1) // 8
        == lax.broadcasted_iota(jnp.int32, (eighths, n_rows), 0)
    ).astype(f32).astype(bf16)
    pick_row = lax.broadcasted_iota(jnp.int32, (n_az, LANES), 0)
    pick_col = lax.broadcasted_iota(jnp.int32, (n_az, LANES), 1) % SIDE
    pick = (pick_row == jnp.where(pick_col < 8, pick_col + n_az - 8, pick_col - 8)).astype(f32).astype(bf16)
    zero = jnp.zeros((SUB, LANES), f32)
    items = [(p, i) for p in range(parts) for i in range(per_step)]
    weights = [jnp.dot(operands[4 * p + 3][i], pick, preferred_element_type=f32) for p, i in items]
    moved = []
    for (p, i), w in zip(items, weights):
        edge, left, right, _ = operands[4 * p : 4 * p + 4]
        for c in range(2):
            ends = [
                jnp.concatenate([x, zero] if c == 0 else [zero, x], axis=0)
                for x in (w[:SUB], w[n_az + SUB :])
            ]
            weight = jnp.concatenate([w[SUB : 3 * SUB], w[n_az - SUB : n_az + SUB], *ends], axis=0).astype(bf16)
            value = jnp.concatenate([edge[i, c], left[i], right[i]], axis=0)
            moved.append(lax.dot_general(value, weight, (((0,), (0,)), ((), ())), preferred_element_type=f32))
    moved = [jnp.where(own, x, 0.0).astype(bf16) for x in moved]
    packed = [jnp.dot(gather, x, preferred_element_type=f32) for x in moved]
    for n, (p, i) in enumerate(items):
        for c in range(2):
            line = lines + c * n_dates + p * DBLK + step * per_step + i
            plane[pl.ds(line, eighths, stride=lines), :] = packed[2 * n + c]

    @pl.when(step == steps - 1)
    def _():
        me = me_ref[0]
        for k in range(len(outs)):
            base = (me ^ k) * (dest_rows // 8)
            for j in range(row_blocks):
                for half in range(2):
                    start = pl.multiple_of((base + 2 * j + half) * lines, lines)
                    values = plane[pl.ds(start, lines), :].astype(bf16)
                    for c in range(2):
                        outs[k][j, c, :, half * LANES : (half + 1) * LANES] = values[
                            c * n_dates : (c + 1) * n_dates
                        ]


def rim(me, own, left, right, ak, partners):
    parts = len(own)
    n_rows = own[0].shape[3]
    n_dates = parts * DBLK
    dest_rows = n_rows // partners
    row_blocks = dest_rows // SIDE + 1
    per_step = 2
    steps = DBLK // per_step
    shape = jax.ShapeDtypeStruct((row_blocks, 2, n_dates, PIX), bf16)

    def ak_spec(p):
        return pl.BlockSpec((per_step, *ak.shape[1:]), lambda t, m: (p * steps + t, 0, 0))

    in_specs, operands = [], []
    for p in range(parts):
        in_specs += [
            pl.BlockSpec((per_step, 2, 2 * SIDE, n_rows), lambda t, m: (t, 0, 0, 0)),
            pl.BlockSpec((per_step, 2 * SUB, n_rows), lambda t, m: (t, 0, 0)),
            pl.BlockSpec((per_step, 2 * SUB, n_rows), lambda t, m: (t, 0, 0)),
            ak_spec(p),
        ]
        operands += [own[p], left[p], right[p], ak]
    grid = pltpu.PrefetchScalarGridSpec(
        num_scalar_prefetch=1,
        grid=(steps,),
        in_specs=in_specs,
        out_specs=[pl.BlockSpec(shape.shape, lambda t, m: (0, 0, 0, 0))] * partners,
        scratch_shapes=[pltpu.VMEM(((n_rows // 8 + 2) * 2 * n_dates, LANES), f32)],
    )
    return pl.pallas_call(
        functools.partial(rim_kernel, dest_rows, parts),
        grid_spec=grid,
        out_shape=[shape] * partners,
        compiler_params=params(),
        cost_estimate=COST,
        name="rim",
    )(me, *operands)


def block_moment(pixels):
    n = pixels.shape[0] // 2
    m = lax.dot_general(pixels, pixels, (((1,), (1,)), ((), ())), preferred_element_type=f32)
    return m[:n, :n] + m[n:, n:], m[n:, :n] - m[:n, n:]


def store_coherence(out, index, real, imag):
    n = real.shape[0]
    eye = lax.broadcasted_iota(jnp.int32, (n, n), 0) == lax.broadcasted_iota(jnp.int32, (n, n), 1)
    diagonal = jnp.where(eye, real, 0.0)
    column = lax.rsqrt(jnp.sum(diagonal, axis=1, keepdims=True) + EPS)
    row = lax.rsqrt(jnp.sum(diagonal, axis=0, keepdims=True) + EPS)
    scale = column * row
    out[(*index, 0)] = real * scale
    out[(*index, 1)] = imag * scale


def column_sums(read, scratch, row_blocks, emit):
    before = None
    for j in range(row_blocks):
        read(j, scratch.at[j])
        now = block_moment(scratch[j])
        if before is not None:
            emit(j - 1, before[0] + now[0], before[1] + now[1])
        before = now


def rim_gram_kernel(me_ref, own, before, after, state, result_in, result, out, window, pixels, sem):
    del result_in
    partners, row_blocks, _, n, _ = own.shape
    me = me_ref[0]
    total = n * partners
    lane = lax.broadcasted_iota(jnp.int32, (n, PIX), 1)
    copy = pltpu.make_async_copy(window, result.at[:, 0], sem)
    for end in range(2):

        def read(j, scratch):
            for k in range(partners):
                for c in range(2):
                    left, right = (before, own) if end == 0 else (own, after)
                    value = jnp.where(lane % SIDE < 8, left[k, j, c], right[k, j, c])
                    at = pl.multiple_of(c * total + (me ^ k) * n, SIDE)
                    scratch[pl.ds(at, n), :] = value

        def emit(u, real, imag):
            if end == 0:
                store_coherence(window, (u,), state[u, 0] + real, state[u, 1] + imag)
            else:
                out[u, 0] = real
                out[u, 1] = imag

        column_sums(read, pixels.at[end], row_blocks, emit)
        if end == 0:
            copy.start()
    copy.wait()


def rim_gram(me, own, before, after, state, result):
    partners, row_blocks, _, n, _ = own.shape
    total = n * partners
    whole = pl.BlockSpec(memory_space=pltpu.VMEM)
    anywhere = pl.BlockSpec(memory_space=pl.ANY)
    return pl.pallas_call(
        rim_gram_kernel,
        in_specs=[pl.BlockSpec(memory_space=pltpu.SMEM)] + [whole] * 4 + [anywhere],
        out_specs=[anywhere, whole],
        out_shape=[
            jax.ShapeDtypeStruct(result.shape, f32),
            jax.ShapeDtypeStruct(state.shape, f32),
        ],
        input_output_aliases={5: 0},
        scratch_shapes=[
            pltpu.VMEM(state.shape, f32),
            pltpu.VMEM((2, row_blocks, 2 * total, PIX), bf16),
            pltpu.SemaphoreType.DMA,
        ],
        compiler_params=params(),
        cost_estimate=COST,
        name="rim_gram",
    )(me, own, before, after, state, result)


def gram_kernel(partners, parts, offsets, columns, first, opening, closing, *refs):
    pieces, refs = refs[: partners * parts], refs[partners * parts :]
    if not opening:
        state, end, _, *refs = refs
    result, *refs = refs
    if opening:
        first_out, *refs = refs
    state_out, held, kept, *blocks, stage, pixels, in_sems, out_sems, state_sems = refs
    row_blocks = pieces[0].shape[0]
    me = lax.axis_index("date").astype(jnp.int32)
    total = pixels.shape[1] // 2

    def fetch(column):
        return [
            pltpu.make_async_copy(
                pieces[n].at[:, offsets[n % parts] + column], blocks[n].at[column], in_sems.at[column, n]
            )
            for n in range(partners * parts)
        ]

    def write(window):
        return pltpu.make_async_copy(stage.at[window], result.at[:, first - 1 + window], out_sems.at[window])

    def start(column, carry):
        for copy in fetch(column):
            copy.start()
        return carry

    if not opening:
        state_in = pltpu.make_async_copy(state, held, state_sems.at[0])
        state_in.start()
    lax.fori_loop(0, columns, start, 0)
    if closing:
        end_in = pltpu.make_async_copy(end, kept, state_sems.at[1])
        end_in.start()
    if opening:
        first_copy = pltpu.make_async_copy(kept, first_out, state_sems.at[1])
    else:
        state_in.wait()

    def work(column, carry):
        for copy in fetch(column):
            copy.wait()

        def read(j, scratch):
            for k in range(partners):
                for p in range(parts):
                    for c in range(2):
                        at = pl.multiple_of(c * total + (me ^ k) * (parts * DBLK) + p * DBLK, DBLK)
                        scratch[pl.ds(at, DBLK), :] = blocks[k * parts + p][column, j, c]

        def emit(u, real, imag):
            store_coherence(stage.at[column], (u,), held[u, 0] + real, held[u, 1] + imag)
            held[u, 0] = real
            held[u, 1] = imag

        column_sums(read, pixels, row_blocks, emit)
        if opening:

            @pl.when(column == 0)
            def _():
                kept[...] = held[...]
                first_copy.start()

            pl.when(column > 0)(write(column).start)
        else:
            write(column).start()
        return carry

    lax.fori_loop(0, columns, work, 0)
    if closing:
        end_in.wait()
        for u in range(row_blocks - 1):
            store_coherence(stage.at[columns], (u,), held[u, 0] + kept[u, 0], held[u, 1] + kept[u, 1])
        write(columns).start()
    else:
        state_copy = pltpu.make_async_copy(held, state_out, state_sems.at[0])
        state_copy.start()
    for window in range(1 if opening else 0, columns + (1 if closing else 0)):
        write(window).wait()
    if opening:
        first_copy.wait()
    if not closing:
        state_copy.wait()


def gram(pieces, offsets, columns, first, state, end, result, out_shape, closing):
    partners, parts = len(pieces), len(pieces[0])
    row_blocks = pieces[0][0].shape[0]
    total = out_shape.shape[-1]
    opening = state is None
    sums = jax.ShapeDtypeStruct((row_blocks - 1, 2, total, total), f32)
    anywhere = pl.BlockSpec(memory_space=pl.ANY)
    operands = [x for k in pieces for x in k]
    aliases = {}
    if not opening:
        aliases = {len(operands) + 2: 0}
        operands += [state, end, result]
    n_out = 2 if opening else 1
    return pl.pallas_call(
        functools.partial(gram_kernel, partners, parts, offsets, columns, first, opening, closing),
        in_specs=[anywhere] * len(operands),
        out_specs=[anywhere] * (1 + n_out),
        out_shape=[out_shape] + [sums] * n_out,
        input_output_aliases=aliases,
        scratch_shapes=[pltpu.VMEM(sums.shape, f32)] * 2
        + [pltpu.VMEM((columns, row_blocks, 2, DBLK, PIX), bf16)] * (partners * parts)
        + [
            pltpu.VMEM((columns + (1 if closing else 0), *sums.shape), f32),
            pltpu.VMEM((row_blocks, 2 * total, PIX), bf16),
            pltpu.SemaphoreType.DMA((columns, partners * parts)),
            pltpu.SemaphoreType.DMA((columns + 1,)),
            pltpu.SemaphoreType.DMA((2,)),
        ],
        compiler_params=params(),
        cost_estimate=COST,
        name=f"gram_{first}",
    )(*operands)


def shift(value, axis, by):
    n = lax.axis_size(axis)
    pairs = [(i, i + by) for i in range(n) if 0 <= i + by < n]
    return lax.ppermute(value, axis, pairs)


def exchange(blocks, ahead=None, gates=()):
    n = lax.axis_size("date")
    got = [blocks[0]]
    for k in range(1, n):
        block = blocks[k]
        if ahead is not None:
            block = after(block, ahead[k])
        if k == n - 1 and gates:
            block = after(block, *gates)
        got.append(lax.ppermute(block, "date", [(i, i ^ k) for i in range(n)]))
    return got


def after(value, *others):
    return lax.optimization_barrier((value, *others))[0]


def on_device(slc, range_kernel, azimuth_kernel):
    partners = lax.axis_size("date")
    n_dates, n_rows, n_az = slc.shape[1:]
    total = n_dates * partners
    columns = n_az // SIDE
    me = lax.axis_index("date").astype(jnp.int32).reshape(1)
    parts = n_dates // DBLK
    bounds = [1, 7, 12, columns]
    spans = list(zip(bounds[:-1], bounds[1:]))

    dest_windows = n_rows // partners // SIDE
    out_shape = jax.ShapeDtypeStruct((dest_windows, columns, 2, total, total), f32)

    own, left, right, sent = [], [], [], []
    turn = me
    for part in range(parts):
        part_spans = spans if part == parts - 1 else [(1, columns)]
        edge, first, last, out = interior(turn, slc, range_kernel, azimuth_kernel, part, part_spans, partners)
        turn = after(me, first)
        own.append(edge)
        left.append(shift(last, "strip", 1))
        right.append(shift(first, "strip", -1))
        sent.append(out)
    early = [exchange(s[0]) for s in sent[:-1]]
    rims = jnp.stack(exchange(rim(me, own, left, right, azimuth_kernel, partners)))
    above, below = shift(rims, "strip", 1), shift(rims, "strip", -1)

    def column_gram(s, state, end, result):
        lo, hi = spans[s]
        pieces = [[e[k] for e in early] + [late[s][k]] for k in range(partners)]
        offsets = [lo - 1] * (parts - 1) + [0]
        closing = s == len(spans) - 1
        return gram(pieces, offsets, hi - lo, lo, state, end, result, out_shape, closing)

    late = [exchange(sent[-1][0], early[-1] if early else None)]
    late.append(exchange(sent[-1][1], late[0]))
    result, opening, state = column_gram(0, None, None, None)
    result, end = rim_gram(me, rims, above, below, opening, result)
    for s in range(1, len(spans) - 1):
        result, state = column_gram(s, state, end, result)
        late.append(exchange(sent[-1][s + 1], late[s], gates=(state,)))
    result, state = column_gram(len(spans) - 1, state, end, result)
    return result


def solution(mesh):
    in_specs = (P(None, "date", None, "strip"), P("date", None, None), P("date", None, "strip"))
    out_specs = P("date", "strip", None, None, None)
    return jax.shard_map(on_device, mesh=mesh, in_specs=in_specs, out_specs=out_specs, check_vma=False)
```

```python
import functools

import jax
import jax.numpy as jnp
from jax import lax
from jax.experimental import pallas as pl
from jax.experimental.pallas import tpu as pltpu
from jax.sharding import PartitionSpec as P

HALO = 8
SIDE = 16
PIX = SIDE * SIDE
LANES = 128
SUB = 8
DBLK = 16
EPS = 1e-06
VMEM = 56 * 1024 * 1024
COST = pl.CostEstimate(flops=1, bytes_accessed=1, transcendentals=0)

bf16 = jnp.bfloat16
f32 = jnp.float32


def params():
    return pltpu.CompilerParams(vmem_limit_bytes=VMEM)


def odd_tiles(rows):
    tiles = -(-rows // SUB)
    return (tiles + 1 - tiles % 2) * SUB


def group_masks(shape):
    group = lax.broadcasted_iota(jnp.int32, shape, 1) // SIDE
    return [(group & step) == 0 for step in (1, 2, 4)]


def gather_groups(rows, masks):
    turned = [rows[0]] + [pltpu.roll(rows[r], SIDE * r, 1) for r in range(1, 8)]
    held = [turned[-i % 8] for i in range(8)]
    for step, low in zip((1, 2, 4), masks):
        held = [jnp.where(low, held[i], held[(i - step) % 8]) for i in range(8)]
    return held


def interior_kernel(spans, dest_rows, part, per_step, me_ref, slc_any, rk_any, ak_any, *refs):
    own_ref, first_ref, last_ref, *refs = refs
    *refs, slc_ref, rk_ref, ak_ref, turned, plane, ranged, in_sems, out_sems = refs
    outs, stage = refs[: len(refs) - len(spans)], refs[len(refs) - len(spans) :]
    steps = DBLK // per_step
    n_rows, n_az = slc_ref.shape[2:]
    lines, pitch = 2 * DBLK, odd_tiles(2 * DBLK)
    partners = len(outs) // len(spans)
    row_blocks = outs[0].shape[0]
    halves = plane.shape[0]

    def fetch(step):
        here = pl.ds(step * per_step, per_step)
        there = pl.ds(part * DBLK + step * per_step, per_step)
        return [
            pltpu.make_async_copy(rk_any.at[there], rk_ref.at[here], in_sems.at[step, 0]),
            pltpu.make_async_copy(slc_any.at[0, there], slc_ref.at[0, here], in_sems.at[step, 1]),
            pltpu.make_async_copy(slc_any.at[1, there], slc_ref.at[1, here], in_sems.at[step, 2]),
            pltpu.make_async_copy(ak_any.at[there], ak_ref.at[here], in_sems.at[step, 3]),
        ]

    def start(step, carry):
        for copy in fetch(step):
            copy.start()
        return carry

    def wait(step):
        for copy in fetch(step):
            copy.wait()

    def along_range(step):
        for n in range(per_step):
            i = step * per_step + n
            for c in range(2):
                value = jnp.dot(rk_ref[i], slc_ref[c, i], preferred_element_type=f32)
                ranged[i, c * n_rows : (c + 1) * n_rows, :] = value.astype(bf16)

    def prepare(step):
        for n in range(per_step):
            i = step * per_step + n
            kernel = ak_ref[i].astype(f32)[HALO : HALO + n_rows]
            turned[i] = pltpu.roll(kernel, HALO, 1).astype(bf16)

    def along_azimuth(step):
        for n in range(per_step):
            i = step * per_step + n
            moved = jnp.dot(ranged[i], turned[i], preferred_element_type=f32)
            for c in range(2):
                line = SUB * pitch + c * DBLK + i
                for h in range(halves):
                    plane[h, pl.ds(line, n_rows, stride=pitch), :] = moved[
                        c * n_rows : (c + 1) * n_rows, h * LANES : (h + 1) * LANES
                    ]

    lax.fori_loop(0, steps, start, 0)
    zero = jnp.zeros((SUB * pitch, LANES), f32)
    for h in range(halves):
        plane[h, : SUB * pitch, :] = zero
        plane[h, (SUB + n_rows) * pitch :, :] = zero
    wait(0)
    along_range(0)
    prepare(0)

    def resample(step, carry):
        later = jnp.minimum(step + 1, steps - 1)
        pl.when(step + 1 < steps)(lambda: wait(later))
        along_azimuth(step)
        along_range(later)
        prepare(later)
        return carry

    lax.fori_loop(0, steps, resample, 0)

    me = me_ref[0]
    masks = group_masks((lines, LANES))
    copies = [
        pltpu.make_async_copy(stage[n // partners].at[n % partners], outs[n], out_sems.at[n]) for n in range(len(outs))
    ]

    for k in [*range(1, partners), 0]:
        base = (me ^ k) * dest_rows

        def blocks(j, carry):
            for half in range(2):
                for h in range(halves):
                    rows = []
                    for r in range(8):
                        at = pl.multiple_of((base + j * SIDE + half * 8 + r) * pitch, SUB)
                        rows.append(plane[h, pl.ds(at, lines), :].astype(bf16))
                    cols = gather_groups(rows, masks)
                    for g in range(8):
                        column = h * 8 + g
                        for s, (lo, hi) in enumerate(spans):
                            if lo <= column < hi:
                                for c in range(2):
                                    stage[s][k, j, column - lo, c, :, half * LANES : (half + 1) * LANES] = cols[g][
                                        c * DBLK : (c + 1) * DBLK
                                    ]
            return carry

        lax.fori_loop(0, row_blocks, blocks, 0)
        for s in range(len(spans)):
            copies[s * partners + k].start()

    pick_row = lax.broadcasted_iota(jnp.int32, (2 * SIDE, n_az), 0)
    pick_col = lax.broadcasted_iota(jnp.int32, (2 * SIDE, n_az), 1)
    pick = (pick_col == jnp.where(pick_row < SIDE, pick_row, pick_row + n_az - 2 * SIDE)).astype(f32).astype(bf16)

    def edges(step, carry):
        for n in range(4):
            i = step * 4 + n
            both = lax.dot_general(pick, ranged[i], (((1,), (1,)), ((), ())), preferred_element_type=f32)
            parts = [both[:, c * n_rows : (c + 1) * n_rows] for c in range(2)]
            for c in range(2):
                own_ref[i, c] = parts[c].astype(bf16)
            first_ref[i] = jnp.concatenate([p[:SUB] for p in parts], axis=0).astype(bf16)
            last_ref[i] = jnp.concatenate([p[2 * SIDE - SUB :] for p in parts], axis=0).astype(bf16)
        return carry

    lax.fori_loop(0, DBLK // 4, edges, 0)
    for copy in copies:
        copy.wait()


def interior(me, slc, rk, ak, part, spans, partners):
    n_rows, n_az = slc.shape[2], slc.shape[3]
    dest_rows = n_rows // partners
    row_blocks = dest_rows // SIDE + 1
    per_step = 2
    steps = DBLK // per_step
    shapes = [
        jax.ShapeDtypeStruct((row_blocks, hi - lo, 2, DBLK, PIX), bf16)
        for lo, hi in spans
        for _ in range(partners)
    ]
    edge_shapes = [
        jax.ShapeDtypeStruct((DBLK, 2, 2 * SIDE, n_rows), bf16),
        jax.ShapeDtypeStruct((DBLK, 2 * SUB, n_rows), bf16),
        jax.ShapeDtypeStruct((DBLK, 2 * SUB, n_rows), bf16),
    ]
    whole = pl.BlockSpec(memory_space=pltpu.VMEM)
    anywhere = pl.BlockSpec(memory_space=pl.ANY)
    own, first, last, *flat = pl.pallas_call(
        functools.partial(interior_kernel, spans, dest_rows, part, per_step),
        in_specs=[pl.BlockSpec(memory_space=pltpu.SMEM)] + [anywhere] * 3,
        out_specs=[whole] * 3 + [anywhere] * len(shapes),
        out_shape=edge_shapes + shapes,
        scratch_shapes=[pltpu.VMEM((partners, *x.shape), bf16) for x in shapes[::partners]]
        + [
            pltpu.VMEM((2, DBLK, n_rows, n_az), bf16),
            pltpu.VMEM((DBLK, n_rows, n_rows), bf16),
            pltpu.VMEM((DBLK, *ak.shape[1:]), bf16),
            pltpu.VMEM((DBLK, n_rows, n_az), bf16),
            pltpu.VMEM((n_az // LANES, (n_rows + 2 * SUB) * odd_tiles(2 * DBLK), LANES), f32),
            pltpu.VMEM((DBLK, 2 * n_rows, n_az), bf16),
            pltpu.SemaphoreType.DMA((steps, 4)),
            pltpu.SemaphoreType.DMA((len(shapes),)),
        ],
        compiler_params=params(),
        cost_estimate=COST,
        name=f"interior_{part}",
    )(me, slc, rk, ak)
    return own, first, last, [flat[s * partners : (s + 1) * partners] for s in range(len(spans))]


def rim_kernel(dest_rows, parts, me_ref, *refs):
    operands, outs, plane = refs[: 4 * parts], refs[4 * parts : -1], refs[-1]
    step, steps = pl.program_id(0), pl.num_programs(0)
    per_step, n_az = operands[0].shape[0], operands[3].shape[2]
    n_rows = operands[0].shape[3]
    n_dates = outs[0].shape[2]
    lines, pitch = 2 * n_dates, odd_tiles(2 * n_dates)
    row_blocks = outs[0].shape[0]
    eighths = n_rows // 8

    @pl.when(step == 0)
    def _():
        zero = jnp.zeros((pitch, LANES), f32)
        plane[:pitch, :] = zero
        plane[(eighths + 1) * pitch :, :] = zero

    row = lax.broadcasted_iota(jnp.int32, (n_rows, LANES), 0)
    lane = lax.broadcasted_iota(jnp.int32, (n_rows, LANES), 1)
    own = (row % 8) == lane // SIDE
    gather = (
        lax.broadcasted_iota(jnp.int32, (eighths, n_rows), 1) // 8
        == lax.broadcasted_iota(jnp.int32, (eighths, n_rows), 0)
    ).astype(f32).astype(bf16)
    pick_row = lax.broadcasted_iota(jnp.int32, (n_az, LANES), 0)
    pick_col = lax.broadcasted_iota(jnp.int32, (n_az, LANES), 1) % SIDE
    pick = (pick_row == jnp.where(pick_col < 8, pick_col + n_az - 8, pick_col - 8)).astype(f32).astype(bf16)
    zero = jnp.zeros((SUB, LANES), f32)
    items = [(p, i) for p in range(parts) for i in range(per_step)]
    weights = [jnp.dot(operands[4 * p + 3][i], pick, preferred_element_type=f32) for p, i in items]
    moved = []
    for (p, i), w in zip(items, weights):
        edge, left, right, _ = operands[4 * p : 4 * p + 4]
        for c in range(2):
            ends = [
                jnp.concatenate([x, zero] if c == 0 else [zero, x], axis=0)
                for x in (w[:SUB], w[n_az + SUB :])
            ]
            weight = jnp.concatenate([w[SUB : 3 * SUB], w[n_az - SUB : n_az + SUB], *ends], axis=0).astype(bf16)
            value = jnp.concatenate([edge[i, c], left[i], right[i]], axis=0)
            moved.append(lax.dot_general(value, weight, (((0,), (0,)), ((), ())), preferred_element_type=f32))
    moved = [jnp.where(own, x, 0.0).astype(bf16) for x in moved]
    packed = [jnp.dot(gather, x, preferred_element_type=f32) for x in moved]
    for n, (p, i) in enumerate(items):
        for c in range(2):
            line = pitch + c * n_dates + p * DBLK + step * per_step + i
            plane[pl.ds(line, eighths, stride=pitch), :] = packed[2 * n + c]

    @pl.when(step == steps - 1)
    def _():
        me = me_ref[0]
        for k in range(len(outs)):
            base = (me ^ k) * (dest_rows // 8)
            for j in range(row_blocks):
                for half in range(2):
                    start = pl.multiple_of((base + 2 * j + half) * pitch, SUB)
                    values = plane[pl.ds(start, lines), :].astype(bf16)
                    for c in range(2):
                        outs[k][j, c, :, half * LANES : (half + 1) * LANES] = values[
                            c * n_dates : (c + 1) * n_dates
                        ]


def rim(me, own, left, right, ak, partners):
    parts = len(own)
    n_rows = own[0].shape[3]
    n_dates = parts * DBLK
    dest_rows = n_rows // partners
    row_blocks = dest_rows // SIDE + 1
    per_step = 2
    steps = DBLK // per_step
    shape = jax.ShapeDtypeStruct((row_blocks, 2, n_dates, PIX), bf16)

    def ak_spec(p):
        return pl.BlockSpec((per_step, *ak.shape[1:]), lambda t, m: (p * steps + t, 0, 0))

    in_specs, operands = [], []
    for p in range(parts):
        in_specs += [
            pl.BlockSpec((per_step, 2, 2 * SIDE, n_rows), lambda t, m: (t, 0, 0, 0)),
            pl.BlockSpec((per_step, 2 * SUB, n_rows), lambda t, m: (t, 0, 0)),
            pl.BlockSpec((per_step, 2 * SUB, n_rows), lambda t, m: (t, 0, 0)),
            ak_spec(p),
        ]
        operands += [own[p], left[p], right[p], ak]
    grid = pltpu.PrefetchScalarGridSpec(
        num_scalar_prefetch=1,
        grid=(steps,),
        in_specs=in_specs,
        out_specs=[pl.BlockSpec(shape.shape, lambda t, m: (0, 0, 0, 0))] * partners,
        scratch_shapes=[pltpu.VMEM(((n_rows // 8 + 2) * odd_tiles(2 * n_dates), LANES), f32)],
    )
    return pl.pallas_call(
        functools.partial(rim_kernel, dest_rows, parts),
        grid_spec=grid,
        out_shape=[shape] * partners,
        compiler_params=params(),
        cost_estimate=COST,
        name="rim",
    )(me, *operands)


def block_moment(pixels):
    n = pixels.shape[0] // 2
    m = lax.dot_general(pixels, pixels, (((1,), (1,)), ((), ())), preferred_element_type=f32)
    return m[:n, :n] + m[n:, n:], m[n:, :n] - m[:n, n:]


def store_coherence(out, index, real, imag):
    n = real.shape[0]
    eye = lax.broadcasted_iota(jnp.int32, (n, n), 0) == lax.broadcasted_iota(jnp.int32, (n, n), 1)
    diagonal = jnp.where(eye, real, 0.0)
    column = lax.rsqrt(jnp.sum(diagonal, axis=1, keepdims=True) + EPS)
    row = lax.rsqrt(jnp.sum(diagonal, axis=0, keepdims=True) + EPS)
    scale = column * row
    out[(*index, 0)] = real * scale
    out[(*index, 1)] = imag * scale


def column_sums(read, scratch, row_blocks, emit):
    before = None
    for j in range(row_blocks):
        read(j, scratch.at[j])
        now = block_moment(scratch[j])
        if before is not None:
            emit(j - 1, before[0] + now[0], before[1] + now[1])
        before = now


def rim_gram_kernel(me_ref, own, before, after, state, result_in, result, out, window, pixels, sem):
    del result_in
    partners, row_blocks, _, n, _ = own.shape
    me = me_ref[0]
    total = n * partners
    lane = lax.broadcasted_iota(jnp.int32, (n, PIX), 1)
    copy = pltpu.make_async_copy(window, result.at[:, 0], sem)
    for end in range(2):

        def read(j, scratch):
            for k in range(partners):
                for c in range(2):
                    left, right = (before, own) if end == 0 else (own, after)
                    value = jnp.where(lane % SIDE < 8, left[k, j, c], right[k, j, c])
                    at = pl.multiple_of(c * total + (me ^ k) * n, SIDE)
                    scratch[pl.ds(at, n), :] = value

        def emit(u, real, imag):
            if end == 0:
                store_coherence(window, (u,), state[u, 0] + real, state[u, 1] + imag)
            else:
                out[u, 0] = real
                out[u, 1] = imag

        column_sums(read, pixels.at[end], row_blocks, emit)
        if end == 0:
            copy.start()
    copy.wait()


def rim_gram(me, own, before, after, state, result):
    partners, row_blocks, _, n, _ = own.shape
    total = n * partners
    whole = pl.BlockSpec(memory_space=pltpu.VMEM)
    anywhere = pl.BlockSpec(memory_space=pl.ANY)
    return pl.pallas_call(
        rim_gram_kernel,
        in_specs=[pl.BlockSpec(memory_space=pltpu.SMEM)] + [whole] * 4 + [anywhere],
        out_specs=[anywhere, whole],
        out_shape=[
            jax.ShapeDtypeStruct(result.shape, f32),
            jax.ShapeDtypeStruct(state.shape, f32),
        ],
        input_output_aliases={5: 0},
        scratch_shapes=[
            pltpu.VMEM(state.shape, f32),
            pltpu.VMEM((2, row_blocks, 2 * total, PIX), bf16),
            pltpu.SemaphoreType.DMA,
        ],
        compiler_params=params(),
        cost_estimate=COST,
        name="rim_gram",
    )(me, own, before, after, state, result)


def gram_kernel(partners, parts, offsets, columns, first, opening, closing, *refs):
    pieces, refs = refs[: partners * parts], refs[partners * parts :]
    if not opening:
        state, end, _, *refs = refs
    result, *refs = refs
    if opening:
        first_out, *refs = refs
    state_out, held, kept, *blocks, stage, pixels, in_sems, out_sems, state_sems = refs
    row_blocks = pieces[0].shape[0]
    me = lax.axis_index("date").astype(jnp.int32)
    total = pixels.shape[1] // 2

    def fetch(column):
        return [
            pltpu.make_async_copy(
                pieces[n].at[:, offsets[n % parts] + column], blocks[n].at[column], in_sems.at[column, n]
            )
            for n in range(partners * parts)
        ]

    def write(window):
        return pltpu.make_async_copy(stage.at[window], result.at[:, first - 1 + window], out_sems.at[window])

    def start(column, carry):
        for copy in fetch(column):
            copy.start()
        return carry

    if not opening:
        state_in = pltpu.make_async_copy(state, held, state_sems.at[0])
        state_in.start()
    lax.fori_loop(0, columns, start, 0)
    if closing:
        end_in = pltpu.make_async_copy(end, kept, state_sems.at[1])
        end_in.start()
    if opening:
        first_copy = pltpu.make_async_copy(kept, first_out, state_sems.at[1])
    else:
        state_in.wait()

    def work(column, carry):
        for copy in fetch(column):
            copy.wait()

        def read(j, scratch):
            for k in range(partners):
                for p in range(parts):
                    for c in range(2):
                        at = pl.multiple_of(c * total + (me ^ k) * (parts * DBLK) + p * DBLK, DBLK)
                        scratch[pl.ds(at, DBLK), :] = blocks[k * parts + p][column, j, c]

        def emit(u, real, imag):
            store_coherence(stage.at[column], (u,), held[u, 0] + real, held[u, 1] + imag)
            held[u, 0] = real
            held[u, 1] = imag

        column_sums(read, pixels, row_blocks, emit)
        if opening:

            @pl.when(column == 0)
            def _():
                kept[...] = held[...]
                first_copy.start()

            pl.when(column > 0)(write(column).start)
        else:
            write(column).start()
        return carry

    lax.fori_loop(0, columns, work, 0)
    if closing:
        end_in.wait()
        for u in range(row_blocks - 1):
            store_coherence(stage.at[columns], (u,), held[u, 0] + kept[u, 0], held[u, 1] + kept[u, 1])
        write(columns).start()
    else:
        state_copy = pltpu.make_async_copy(held, state_out, state_sems.at[0])
        state_copy.start()
    for window in range(1 if opening else 0, columns + (1 if closing else 0)):
        write(window).wait()
    if opening:
        first_copy.wait()
    if not closing:
        state_copy.wait()


def gram(pieces, offsets, columns, first, state, end, result, out_shape, closing):
    partners, parts = len(pieces), len(pieces[0])
    row_blocks = pieces[0][0].shape[0]
    total = out_shape.shape[-1]
    opening = state is None
    sums = jax.ShapeDtypeStruct((row_blocks - 1, 2, total, total), f32)
    anywhere = pl.BlockSpec(memory_space=pl.ANY)
    operands = [x for k in pieces for x in k]
    aliases = {}
    if not opening:
        aliases = {len(operands) + 2: 0}
        operands += [state, end, result]
    n_out = 2 if opening else 1
    return pl.pallas_call(
        functools.partial(gram_kernel, partners, parts, offsets, columns, first, opening, closing),
        in_specs=[anywhere] * len(operands),
        out_specs=[anywhere] * (1 + n_out),
        out_shape=[out_shape] + [sums] * n_out,
        input_output_aliases=aliases,
        scratch_shapes=[pltpu.VMEM(sums.shape, f32)] * 2
        + [pltpu.VMEM((columns, row_blocks, 2, DBLK, PIX), bf16)] * (partners * parts)
        + [
            pltpu.VMEM((columns + (1 if closing else 0), *sums.shape), f32),
            pltpu.VMEM((row_blocks, 2 * total, PIX), bf16),
            pltpu.SemaphoreType.DMA((columns, partners * parts)),
            pltpu.SemaphoreType.DMA((columns + 1,)),
            pltpu.SemaphoreType.DMA((2,)),
        ],
        compiler_params=params(),
        cost_estimate=COST,
        name=f"gram_{first}",
    )(*operands)


def shift(value, axis, by):
    n = lax.axis_size(axis)
    pairs = [(i, i + by) for i in range(n) if 0 <= i + by < n]
    return lax.ppermute(value, axis, pairs)


def exchange(blocks, ahead=None, gates=()):
    n = lax.axis_size("date")
    got = [blocks[0]]
    for k in range(1, n):
        block = blocks[k]
        if ahead is not None:
            block = after(block, ahead[k])
        if k == 1 and gates:
            block = after(block, *gates)
        got.append(lax.ppermute(block, "date", [(i, i ^ k) for i in range(n)]))
    return got


def after(value, *others):
    return lax.optimization_barrier((value, *others))[0]


def on_device(slc, range_kernel, azimuth_kernel):
    partners = lax.axis_size("date")
    n_dates, n_rows, n_az = slc.shape[1:]
    total = n_dates * partners
    columns = n_az // SIDE
    me = lax.axis_index("date").astype(jnp.int32).reshape(1)
    parts = n_dates // DBLK
    bounds = [1, 7, 12, columns]
    spans = list(zip(bounds[:-1], bounds[1:]))

    dest_windows = n_rows // partners // SIDE
    out_shape = jax.ShapeDtypeStruct((dest_windows, columns, 2, total, total), f32)

    own, left, right, sent = [], [], [], []
    turn = me
    for part in range(parts):
        part_spans = spans if part == parts - 1 else [(1, columns)]
        edge, first, last, out = interior(turn, slc, range_kernel, azimuth_kernel, part, part_spans, partners)
        turn = after(me, first)
        own.append(edge)
        left.append(shift(last, "strip", 1))
        right.append(shift(first, "strip", -1))
        sent.append(out)
    early = [exchange(s[0]) for s in sent[:-1]]
    rims = jnp.stack(exchange(rim(me, own, left, right, azimuth_kernel, partners)))
    above, below = shift(rims, "strip", 1), shift(rims, "strip", -1)

    def column_gram(s, state, end, result):
        lo, hi = spans[s]
        pieces = [[e[k] for e in early] + [late[s][k]] for k in range(partners)]
        offsets = [lo - 1] * (parts - 1) + [0]
        closing = s == len(spans) - 1
        return gram(pieces, offsets, hi - lo, lo, state, end, result, out_shape, closing)

    late = [exchange(sent[-1][0], early[-1] if early else None)]
    late.append(exchange(sent[-1][1], late[0]))
    result, opening, state = column_gram(0, None, None, None)
    result, end = rim_gram(me, rims, above, below, opening, result)
    for s in range(1, len(spans) - 1):
        result, state = column_gram(s, state, end, result)
        late.append(exchange(sent[-1][s + 1], late[s], gates=(end,)))
    result, state = column_gram(len(spans) - 1, state, end, result)
    return result


def solution(mesh):
    in_specs = (P(None, "date", None, "strip"), P("date", None, None), P("date", None, "strip"))
    out_specs = P("date", "strip", None, None, None)
    return jax.shard_map(on_device, mesh=mesh, in_specs=in_specs, out_specs=out_specs, check_vma=False)
```

```python
import functools

import jax
import jax.numpy as jnp
from jax import lax
from jax.experimental import pallas as pl
from jax.experimental.pallas import tpu as pltpu
from jax.sharding import PartitionSpec as P

HALO = 8
SIDE = 16
PIX = SIDE * SIDE
LANES = 128
SUB = 8
DBLK = 16
EPS = 1e-06
VMEM = 63 * 1024 * 1024
COST = pl.CostEstimate(flops=1, bytes_accessed=1, transcendentals=0)

bf16 = jnp.bfloat16
f32 = jnp.float32


def params():
    return pltpu.CompilerParams(vmem_limit_bytes=VMEM)


def odd_tiles(rows):
    tiles = -(-rows // SUB)
    return (tiles + 1 - tiles % 2) * SUB


def group_masks(shape):
    group = lax.broadcasted_iota(jnp.int32, shape, 1) // SIDE
    return [(group & step) == 0 for step in (1, 2, 4)]


def gather_groups(rows, masks):
    turned = [rows[0]] + [pltpu.roll(rows[r], SIDE * r, 1) for r in range(1, 8)]
    held = [turned[-i % 8] for i in range(8)]
    for step, low in zip((1, 2, 4), masks):
        held = [jnp.where(low, held[i], held[(i - step) % 8]) for i in range(8)]
    return held


def interior_kernel(spans, targets, edged, dest_rows, part, per_step, me_ref, slc_any, rk_any, ak_any, *refs):
    if edged:
        own_ref, first_ref, last_ref, *refs = refs
    *refs, slc_ref, rk_ref, ak_ref, turned, plane, ranged, in_sems, out_sems = refs
    outs, stage = refs[: len(refs) - len(spans)], refs[len(refs) - len(spans) :]
    steps = DBLK // per_step
    n_rows, n_az = slc_ref.shape[2:]
    lines, pitch = 2 * DBLK, odd_tiles(2 * DBLK)
    n_targets = len(targets)
    row_blocks = outs[0].shape[0]
    halves = plane.shape[0]
    me = me_ref[0]
    taken, top = n_rows, 0
    if n_targets == 1:
        taken = min(n_rows, dest_rows + 2 * SIDE)
        top = jnp.clip((me ^ targets[0]) * dest_rows - SIDE, 0, n_rows - taken)
        top = pl.multiple_of(top, SIDE)
    rows_in = pl.ds(top, taken)

    def fetch(step):
        here = pl.ds(step * per_step, per_step)
        there = pl.ds(part * DBLK + step * per_step, per_step)
        return [
            pltpu.make_async_copy(rk_any.at[there, rows_in], rk_ref.at[here, pl.ds(0, taken)], in_sems.at[step, 0]),
            pltpu.make_async_copy(slc_any.at[0, there, rows_in], slc_ref.at[0, here, rows_in], in_sems.at[step, 1]),
            pltpu.make_async_copy(slc_any.at[1, there, rows_in], slc_ref.at[1, here, rows_in], in_sems.at[step, 2]),
            pltpu.make_async_copy(ak_any.at[there], ak_ref.at[here], in_sems.at[step, 3]),
        ]

    def start(step, carry):
        for copy in fetch(step):
            copy.start()
        return carry

    def wait(step):
        for copy in fetch(step):
            copy.wait()

    def along_range(step):
        for n in range(per_step):
            i = step * per_step + n
            for c in range(2):
                value = jnp.dot(rk_ref[i, :taken], slc_ref[c, i], preferred_element_type=f32)
                ranged[i, c * taken : (c + 1) * taken, :] = value.astype(bf16)

    def prepare(step):
        for n in range(per_step):
            i = step * per_step + n
            kernel = ak_ref[i].astype(f32)[HALO : HALO + n_rows]
            turned[i] = pltpu.roll(kernel, HALO, 1).astype(bf16)

    def along_azimuth(step):
        for n in range(per_step):
            i = step * per_step + n
            moved = jnp.dot(ranged[i, : 2 * taken], turned[i], preferred_element_type=f32)
            for c in range(2):
                line = (SUB + top) * pitch + c * DBLK + i
                for h in range(halves):
                    plane[h, pl.ds(line, taken, stride=pitch), :] = moved[
                        c * taken : (c + 1) * taken, h * LANES : (h + 1) * LANES
                    ]

    lax.fori_loop(0, steps, start, 0)
    zero = jnp.zeros((SUB * pitch, LANES), f32)
    for h in range(halves):
        plane[h, : SUB * pitch, :] = zero
        plane[h, (SUB + n_rows) * pitch :, :] = zero
    if taken < n_rows:

        def clear(n, carry):
            at = pl.multiple_of(jnp.where(n * SIDE < top, n * SIDE, n * SIDE + taken), SIDE)
            slc_ref[:, :, pl.ds(at, SIDE), :] = jnp.zeros((2, DBLK, SIDE, n_az), bf16)
            return carry

        lax.fori_loop(0, (n_rows - taken) // SIDE, clear, 0)
    wait(0)
    along_range(0)
    prepare(0)

    def resample(step, carry):
        later = jnp.minimum(step + 1, steps - 1)
        pl.when(step + 1 < steps)(lambda: wait(later))
        along_azimuth(step)
        along_range(later)
        prepare(later)
        return carry

    lax.fori_loop(0, steps, resample, 0)

    masks = group_masks((lines, LANES))
    copies = [
        pltpu.make_async_copy(stage[n // n_targets].at[n % n_targets], outs[n], out_sems.at[n])
        for n in range(len(outs))
    ]

    for t, k in enumerate(targets):
        base = (me ^ k) * dest_rows

        def blocks(j, carry):
            for half in range(2):
                for h in range(halves):
                    rows = []
                    for r in range(8):
                        at = pl.multiple_of((base + j * SIDE + half * 8 + r) * pitch, SUB)
                        rows.append(plane[h, pl.ds(at, lines), :].astype(bf16))
                    cols = gather_groups(rows, masks)
                    for g in range(8):
                        column = h * 8 + g
                        for s, (lo, hi) in enumerate(spans):
                            if lo <= column < hi:
                                for c in range(2):
                                    stage[s][t, j, column - lo, c, :, half * LANES : (half + 1) * LANES] = cols[g][
                                        c * DBLK : (c + 1) * DBLK
                                    ]
            return carry

        lax.fori_loop(0, row_blocks, blocks, 0)
        for s in range(len(spans)):
            copies[s * n_targets + t].start()

    pick_row = lax.broadcasted_iota(jnp.int32, (2 * SIDE, n_az), 0)
    pick_col = lax.broadcasted_iota(jnp.int32, (2 * SIDE, n_az), 1)
    pick = (pick_col == jnp.where(pick_row < SIDE, pick_row, pick_row + n_az - 2 * SIDE)).astype(f32).astype(bf16)

    def edges(step, carry):
        for n in range(4):
            i = step * 4 + n
            both = lax.dot_general(pick, ranged[i], (((1,), (1,)), ((), ())), preferred_element_type=f32)
            parts = [both[:, c * n_rows : (c + 1) * n_rows] for c in range(2)]
            for c in range(2):
                own_ref[i, c] = parts[c].astype(bf16)
            first_ref[i] = jnp.concatenate([p[:SUB] for p in parts], axis=0).astype(bf16)
            last_ref[i] = jnp.concatenate([p[2 * SIDE - SUB :] for p in parts], axis=0).astype(bf16)
        return carry

    if edged:
        lax.fori_loop(0, DBLK // 4, edges, 0)
    for copy in copies:
        copy.wait()


def interior(me, slc, rk, ak, part, spans, targets, edged, partners):
    n_rows, n_az = slc.shape[2], slc.shape[3]
    dest_rows = n_rows // partners
    row_blocks = dest_rows // SIDE + 1
    per_step = 2
    steps = DBLK // per_step
    shapes = [
        jax.ShapeDtypeStruct((row_blocks, hi - lo, 2, DBLK, PIX), bf16)
        for lo, hi in spans
        for _ in targets
    ]
    edge_shapes = [
        jax.ShapeDtypeStruct((DBLK, 2, 2 * SIDE, n_rows), bf16),
        jax.ShapeDtypeStruct((DBLK, 2 * SUB, n_rows), bf16),
        jax.ShapeDtypeStruct((DBLK, 2 * SUB, n_rows), bf16),
    ]
    if not edged:
        edge_shapes = []
    whole = pl.BlockSpec(memory_space=pltpu.VMEM)
    anywhere = pl.BlockSpec(memory_space=pl.ANY)
    outs = pl.pallas_call(
        functools.partial(interior_kernel, spans, targets, edged, dest_rows, part, per_step),
        in_specs=[pl.BlockSpec(memory_space=pltpu.SMEM)] + [anywhere] * 3,
        out_specs=[whole] * len(edge_shapes) + [anywhere] * len(shapes),
        out_shape=edge_shapes + shapes,
        scratch_shapes=[pltpu.VMEM((len(targets), *x.shape), bf16) for x in shapes[:: len(targets)]]
        + [
            pltpu.VMEM((2, DBLK, n_rows, n_az), bf16),
            pltpu.VMEM((DBLK, n_rows, n_rows), bf16),
            pltpu.VMEM((DBLK, *ak.shape[1:]), bf16),
            pltpu.VMEM((DBLK, n_rows, n_az), bf16),
            pltpu.VMEM((n_az // LANES, (n_rows + 2 * SUB) * odd_tiles(2 * DBLK), LANES), f32),
            pltpu.VMEM((DBLK, 2 * n_rows, n_az), bf16),
            pltpu.SemaphoreType.DMA((steps, 4)),
            pltpu.SemaphoreType.DMA((len(shapes),)),
        ],
        compiler_params=params(),
        cost_estimate=COST,
        name=f"interior_{part}_{targets[0]}",
    )(me, slc, rk, ak)
    flat = outs[len(edge_shapes) :]
    return outs[: len(edge_shapes)], [flat[s * len(targets) : (s + 1) * len(targets)] for s in range(len(spans))]


def rim_kernel(dest_rows, parts, me_ref, *refs):
    operands, outs, plane = refs[: 4 * parts], refs[4 * parts : -1], refs[-1]
    step, steps = pl.program_id(0), pl.num_programs(0)
    per_step, n_az = operands[0].shape[0], operands[3].shape[2]
    n_rows = operands[0].shape[3]
    n_dates = outs[0].shape[2]
    lines, pitch = 2 * n_dates, odd_tiles(2 * n_dates)
    row_blocks = outs[0].shape[0]
    eighths = n_rows // 8

    @pl.when(step == 0)
    def _():
        zero = jnp.zeros((pitch, LANES), f32)
        plane[:pitch, :] = zero
        plane[(eighths + 1) * pitch :, :] = zero

    row = lax.broadcasted_iota(jnp.int32, (n_rows, LANES), 0)
    lane = lax.broadcasted_iota(jnp.int32, (n_rows, LANES), 1)
    own = (row % 8) == lane // SIDE
    gather = (
        lax.broadcasted_iota(jnp.int32, (eighths, n_rows), 1) // 8
        == lax.broadcasted_iota(jnp.int32, (eighths, n_rows), 0)
    ).astype(f32).astype(bf16)
    pick_row = lax.broadcasted_iota(jnp.int32, (n_az, LANES), 0)
    pick_col = lax.broadcasted_iota(jnp.int32, (n_az, LANES), 1) % SIDE
    pick = (pick_row == jnp.where(pick_col < 8, pick_col + n_az - 8, pick_col - 8)).astype(f32).astype(bf16)
    zero = jnp.zeros((SUB, LANES), f32)
    items = [(p, i) for p in range(parts) for i in range(per_step)]
    weights = [jnp.dot(operands[4 * p + 3][i], pick, preferred_element_type=f32) for p, i in items]
    moved = []
    for (p, i), w in zip(items, weights):
        edge, left, right, _ = operands[4 * p : 4 * p + 4]
        for c in range(2):
            ends = [
                jnp.concatenate([x, zero] if c == 0 else [zero, x], axis=0)
                for x in (w[:SUB], w[n_az + SUB :])
            ]
            weight = jnp.concatenate([w[SUB : 3 * SUB], w[n_az - SUB : n_az + SUB], *ends], axis=0).astype(bf16)
            value = jnp.concatenate([edge[i, c], left[i], right[i]], axis=0)
            moved.append(lax.dot_general(value, weight, (((0,), (0,)), ((), ())), preferred_element_type=f32))
    moved = [jnp.where(own, x, 0.0).astype(bf16) for x in moved]
    packed = [jnp.dot(gather, x, preferred_element_type=f32) for x in moved]
    for n, (p, i) in enumerate(items):
        for c in range(2):
            line = pitch + c * n_dates + p * DBLK + step * per_step + i
            plane[pl.ds(line, eighths, stride=pitch), :] = packed[2 * n + c]

    @pl.when(step == steps - 1)
    def _():
        me = me_ref[0]
        for k in range(len(outs)):
            base = (me ^ k) * (dest_rows // 8)
            for j in range(row_blocks):
                for half in range(2):
                    start = pl.multiple_of((base + 2 * j + half) * pitch, SUB)
                    values = plane[pl.ds(start, lines), :].astype(bf16)
                    for c in range(2):
                        outs[k][j, c, :, half * LANES : (half + 1) * LANES] = values[
                            c * n_dates : (c + 1) * n_dates
                        ]


def rim(me, own, left, right, ak, partners):
    parts = len(own)
    n_rows = own[0].shape[3]
    n_dates = parts * DBLK
    dest_rows = n_rows // partners
    row_blocks = dest_rows // SIDE + 1
    per_step = 2
    steps = DBLK // per_step
    shape = jax.ShapeDtypeStruct((row_blocks, 2, n_dates, PIX), bf16)

    def ak_spec(p):
        return pl.BlockSpec((per_step, *ak.shape[1:]), lambda t, m: (p * steps + t, 0, 0))

    in_specs, operands = [], []
    for p in range(parts):
        in_specs += [
            pl.BlockSpec((per_step, 2, 2 * SIDE, n_rows), lambda t, m: (t, 0, 0, 0)),
            pl.BlockSpec((per_step, 2 * SUB, n_rows), lambda t, m: (t, 0, 0)),
            pl.BlockSpec((per_step, 2 * SUB, n_rows), lambda t, m: (t, 0, 0)),
            ak_spec(p),
        ]
        operands += [own[p], left[p], right[p], ak]
    grid = pltpu.PrefetchScalarGridSpec(
        num_scalar_prefetch=1,
        grid=(steps,),
        in_specs=in_specs,
        out_specs=[pl.BlockSpec(shape.shape, lambda t, m: (0, 0, 0, 0))] * partners,
        scratch_shapes=[pltpu.VMEM(((n_rows // 8 + 2) * odd_tiles(2 * n_dates), LANES), f32)],
    )
    return pl.pallas_call(
        functools.partial(rim_kernel, dest_rows, parts),
        grid_spec=grid,
        out_shape=[shape] * partners,
        compiler_params=params(),
        cost_estimate=COST,
        name="rim",
    )(me, *operands)


def block_moment(pixels):
    n = pixels.shape[0] // 2
    m = lax.dot_general(pixels, pixels, (((1,), (1,)), ((), ())), preferred_element_type=f32)
    return m[:n, :n] + m[n:, n:], m[n:, :n] - m[:n, n:]


def store_coherence(out, index, real, imag):
    n = real.shape[0]
    eye = lax.broadcasted_iota(jnp.int32, (n, n), 0) == lax.broadcasted_iota(jnp.int32, (n, n), 1)
    diagonal = jnp.where(eye, real, 0.0)
    column = lax.rsqrt(jnp.sum(diagonal, axis=1, keepdims=True) + EPS)
    row = lax.rsqrt(jnp.sum(diagonal, axis=0, keepdims=True) + EPS)
    scale = column * row
    out[(*index, 0)] = real * scale
    out[(*index, 1)] = imag * scale


def column_sums(read, scratch, row_blocks, emit):
    before = None
    for j in range(row_blocks):
        read(j, scratch.at[j])
        now = block_moment(scratch[j])
        if before is not None:
            emit(j - 1, before[0] + now[0], before[1] + now[1])
        before = now


def rim_gram_kernel(me_ref, own, before, after, state, result_in, result, out, window, pixels, sem):
    del result_in
    partners, row_blocks, _, n, _ = own.shape
    me = me_ref[0]
    total = n * partners
    lane = lax.broadcasted_iota(jnp.int32, (n, PIX), 1)
    copy = pltpu.make_async_copy(window, result.at[:, 0], sem)
    for end in range(2):

        def read(j, scratch):
            for k in range(partners):
                for c in range(2):
                    left, right = (before, own) if end == 0 else (own, after)
                    value = jnp.where(lane % SIDE < 8, left[k, j, c], right[k, j, c])
                    at = pl.multiple_of(c * total + (me ^ k) * n, SIDE)
                    scratch[pl.ds(at, n), :] = value

        def emit(u, real, imag):
            if end == 0:
                store_coherence(window, (u,), state[u, 0] + real, state[u, 1] + imag)
            else:
                out[u, 0] = real
                out[u, 1] = imag

        column_sums(read, pixels.at[end], row_blocks, emit)
        if end == 0:
            copy.start()
    copy.wait()


def rim_gram(me, own, before, after, state, result):
    partners, row_blocks, _, n, _ = own.shape
    total = n * partners
    whole = pl.BlockSpec(memory_space=pltpu.VMEM)
    anywhere = pl.BlockSpec(memory_space=pl.ANY)
    return pl.pallas_call(
        rim_gram_kernel,
        in_specs=[pl.BlockSpec(memory_space=pltpu.SMEM)] + [whole] * 4 + [anywhere],
        out_specs=[anywhere, whole],
        out_shape=[
            jax.ShapeDtypeStruct(result.shape, f32),
            jax.ShapeDtypeStruct(state.shape, f32),
        ],
        input_output_aliases={5: 0},
        scratch_shapes=[
            pltpu.VMEM(state.shape, f32),
            pltpu.VMEM((2, row_blocks, 2 * total, PIX), bf16),
            pltpu.SemaphoreType.DMA,
        ],
        compiler_params=params(),
        cost_estimate=COST,
        name="rim_gram",
    )(me, own, before, after, state, result)


def gram_kernel(partners, parts, offsets, columns, first, opening, closing, *refs):
    pieces, refs = refs[: partners * parts], refs[partners * parts :]
    if not opening:
        state, end, _, *refs = refs
    result, *refs = refs
    if opening:
        first_out, *refs = refs
    state_out, held, kept, *blocks, stage, pixels, in_sems, out_sems, state_sems = refs
    row_blocks = pieces[0].shape[0]
    me = lax.axis_index("date").astype(jnp.int32)
    total = pixels.shape[1] // 2

    def fetch(column):
        return [
            pltpu.make_async_copy(
                pieces[n].at[:, offsets[n % parts] + column], blocks[n].at[column], in_sems.at[column, n]
            )
            for n in range(partners * parts)
        ]

    def write(window):
        return pltpu.make_async_copy(stage.at[window], result.at[:, first - 1 + window], out_sems.at[window])

    def start(column, carry):
        for copy in fetch(column):
            copy.start()
        return carry

    if not opening:
        state_in = pltpu.make_async_copy(state, held, state_sems.at[0])
        state_in.start()
    lax.fori_loop(0, columns, start, 0)
    if closing:
        end_in = pltpu.make_async_copy(end, kept, state_sems.at[1])
        end_in.start()
    if opening:
        first_copy = pltpu.make_async_copy(kept, first_out, state_sems.at[1])
    else:
        state_in.wait()

    def work(column, carry):
        for copy in fetch(column):
            copy.wait()

        def read(j, scratch):
            for k in range(partners):
                for p in range(parts):
                    for c in range(2):
                        at = pl.multiple_of(c * total + (me ^ k) * (parts * DBLK) + p * DBLK, DBLK)
                        scratch[pl.ds(at, DBLK), :] = blocks[k * parts + p][column, j, c]

        def emit(u, real, imag):
            store_coherence(stage.at[column], (u,), held[u, 0] + real, held[u, 1] + imag)
            held[u, 0] = real
            held[u, 1] = imag

        column_sums(read, pixels, row_blocks, emit)
        if opening:

            @pl.when(column == 0)
            def _():
                kept[...] = held[...]
                first_copy.start()

            pl.when(column > 0)(write(column).start)
        else:
            write(column).start()
        return carry

    lax.fori_loop(0, columns, work, 0)
    if closing:
        end_in.wait()
        for u in range(row_blocks - 1):
            store_coherence(stage.at[columns], (u,), held[u, 0] + kept[u, 0], held[u, 1] + kept[u, 1])
        write(columns).start()
    else:
        state_copy = pltpu.make_async_copy(held, state_out, state_sems.at[0])
        state_copy.start()
    for window in range(1 if opening else 0, columns + (1 if closing else 0)):
        write(window).wait()
    if opening:
        first_copy.wait()
    if not closing:
        state_copy.wait()


def gram(pieces, offsets, columns, first, state, end, result, out_shape, closing):
    partners, parts = len(pieces), len(pieces[0])
    row_blocks = pieces[0][0].shape[0]
    total = out_shape.shape[-1]
    opening = state is None
    sums = jax.ShapeDtypeStruct((row_blocks - 1, 2, total, total), f32)
    anywhere = pl.BlockSpec(memory_space=pl.ANY)
    operands = [x for k in pieces for x in k]
    aliases = {}
    if not opening:
        aliases = {len(operands) + 2: 0}
        operands += [state, end, result]
    n_out = 2 if opening else 1
    return pl.pallas_call(
        functools.partial(gram_kernel, partners, parts, offsets, columns, first, opening, closing),
        in_specs=[anywhere] * len(operands),
        out_specs=[anywhere] * (1 + n_out),
        out_shape=[out_shape] + [sums] * n_out,
        input_output_aliases=aliases,
        scratch_shapes=[pltpu.VMEM(sums.shape, f32)] * 2
        + [pltpu.VMEM((columns, row_blocks, 2, DBLK, PIX), bf16)] * (partners * parts)
        + [
            pltpu.VMEM((columns + (1 if closing else 0), *sums.shape), f32),
            pltpu.VMEM((row_blocks, 2 * total, PIX), bf16),
            pltpu.SemaphoreType.DMA((columns, partners * parts)),
            pltpu.SemaphoreType.DMA((columns + 1,)),
            pltpu.SemaphoreType.DMA((2,)),
        ],
        compiler_params=params(),
        cost_estimate=COST,
        name=f"gram_{first}",
    )(*operands)


def shift(value, axis, by):
    n = lax.axis_size(axis)
    pairs = [(i, i + by) for i in range(n) if 0 <= i + by < n]
    return lax.ppermute(value, axis, pairs)


def exchange(blocks, ahead=None, gates=()):
    n = lax.axis_size("date")
    got = [blocks[0]]
    for k in range(1, n):
        block = blocks[k]
        if ahead is not None:
            block = after(block, ahead[k])
        if k == 1 and gates:
            block = after(block, *gates)
        got.append(lax.ppermute(block, "date", [(i, i ^ k) for i in range(n)]))
    return got


def after(value, *others):
    return lax.optimization_barrier((value, *others))[0]


def on_device(slc, range_kernel, azimuth_kernel):
    partners = lax.axis_size("date")
    n_dates, n_rows, n_az = slc.shape[1:]
    total = n_dates * partners
    columns = n_az // SIDE
    me = lax.axis_index("date").astype(jnp.int32).reshape(1)
    parts = n_dates // DBLK
    bounds = [1, 7, 13, columns]
    spans = list(zip(bounds[:-1], bounds[1:]))

    dest_windows = n_rows // partners // SIDE
    out_shape = jax.ShapeDtypeStruct((dest_windows, columns, 2, total, total), f32)

    own, left, right, sent = [], [], [], []
    turn = me
    for part in range(parts):
        part_spans = spans if part == parts - 1 else [(1, columns)]
        source = (slc, range_kernel, azimuth_kernel, part, part_spans)
        if part == 0:
            _, lead = interior(turn, *source, [partners - 1], False, partners)
            turn = after(me, lead[0][0])
        targets = [*range(1, partners - 1 if part == 0 else partners), 0]
        (edge, first, last), out = interior(turn, *source, targets, True, partners)
        turn = after(me, first)
        own.append(edge)
        left.append(shift(last, "strip", 1))
        right.append(shift(first, "strip", -1))
        if part == 0:
            out = [[x[-1], *x[:-1], y[0]] for x, y in zip(out, lead)]
        else:
            out = [[x[-1], *x[:-1]] for x in out]
        sent.append(out)
    early = [exchange(s[0]) for s in sent[:-1]]
    lead = [early[-1][-1]] if early else []
    rims = exchange([after(x, *lead) for x in rim(me, own, left, right, azimuth_kernel, partners)])
    first = [*sent[-1][0][:-1], after(sent[-1][0][-1], *rims)]
    late = [exchange(first, early[-1] if early else None)]
    rims = jnp.stack(rims)
    above, below = shift(rims, "strip", 1), shift(rims, "strip", -1)

    def column_gram(s, state, end, result):
        lo, hi = spans[s]
        pieces = [[e[k] for e in early] + [late[s][k]] for k in range(partners)]
        offsets = [lo - 1] * (parts - 1) + [0]
        closing = s == len(spans) - 1
        return gram(pieces, offsets, hi - lo, lo, state, end, result, out_shape, closing)

    late.append(exchange(sent[-1][1], late[0]))
    result, opening, state = column_gram(0, None, None, None)
    result, end = rim_gram(me, rims, above, below, opening, result)
    for s in range(1, len(spans) - 1):
        result, state = column_gram(s, state, end, result)
        late.append(exchange(sent[-1][s + 1], late[s], gates=(end,)))
    result, state = column_gram(len(spans) - 1, state, end, result)
    return result


def solution(mesh):
    in_specs = (P(None, "date", None, "strip"), P("date", None, None), P("date", None, "strip"))
    out_specs = P("date", "strip", None, None, None)
    return jax.shard_map(on_device, mesh=mesh, in_specs=in_specs, out_specs=out_specs, check_vma=False)
```

```python
import functools

import jax
import jax.numpy as jnp
from jax import lax
from jax.experimental import pallas as pl
from jax.experimental.pallas import tpu as pltpu
from jax.sharding import PartitionSpec as P

HALO = 8
SIDE = 16
PIX = SIDE * SIDE
LANES = 128
SUB = 8
DBLK = 16
EPS = 1e-06
VMEM = 62 * 1024 * 1024
COST = pl.CostEstimate(flops=1, bytes_accessed=1, transcendentals=0)

bf16 = jnp.bfloat16
f32 = jnp.float32


def params():
    return pltpu.CompilerParams(vmem_limit_bytes=VMEM)


def odd_tiles(rows):
    tiles = -(-rows // SUB)
    return (tiles + 1 - tiles % 2) * SUB


def group_masks(shape):
    group = lax.broadcasted_iota(jnp.int32, shape, 1) // SIDE
    return [(group & step) == 0 for step in (1, 2, 4)]


def gather_groups(rows, masks):
    turned = [rows[0]] + [pltpu.roll(rows[r], SIDE * r, 1) for r in range(1, 8)]
    held = [turned[-i % 8] for i in range(8)]
    for step, low in zip((1, 2, 4), masks):
        held = [jnp.where(low, held[i], held[(i - step) % 8]) for i in range(8)]
    return held


def interior_kernel(spans, targets, edged, dest_rows, part, per_step, me_ref, slc_any, rk_any, ak_any, *refs):
    if edged:
        own_ref, first_ref, last_ref, *refs = refs
    *refs, slc_ref, rk_ref, ak_ref, turned, plane, ranged, in_sems, out_sems = refs
    outs, stage = refs[: len(refs) - len(spans)], refs[len(refs) - len(spans) :]
    steps = DBLK // per_step
    n_rows, n_az = slc_ref.shape[2:]
    lines, pitch = 2 * DBLK, odd_tiles(2 * DBLK)
    n_targets = len(targets)
    row_blocks = outs[0].shape[0]
    halves = plane.shape[0]
    me = me_ref[0]
    taken, top = n_rows, 0
    if n_targets == 1:
        taken = min(n_rows, dest_rows + 2 * SIDE)
        top = jnp.clip((me ^ targets[0]) * dest_rows - SIDE, 0, n_rows - taken)
        top = pl.multiple_of(top, SIDE)
    rows_in = pl.ds(top, taken)

    def fetch(step):
        here = pl.ds(step * per_step, per_step)
        there = pl.ds(part * DBLK + step * per_step, per_step)
        return [
            pltpu.make_async_copy(rk_any.at[there, rows_in], rk_ref.at[here, pl.ds(0, taken)], in_sems.at[step, 0]),
            pltpu.make_async_copy(slc_any.at[0, there, rows_in], slc_ref.at[0, here, rows_in], in_sems.at[step, 1]),
            pltpu.make_async_copy(slc_any.at[1, there, rows_in], slc_ref.at[1, here, rows_in], in_sems.at[step, 2]),
            pltpu.make_async_copy(ak_any.at[there], ak_ref.at[here], in_sems.at[step, 3]),
        ]

    def start(step, carry):
        for copy in fetch(step):
            copy.start()
        return carry

    def wait(step):
        for copy in fetch(step):
            copy.wait()

    def along_range(step):
        for n in range(per_step):
            i = step * per_step + n
            for c in range(2):
                value = jnp.dot(rk_ref[i, :taken], slc_ref[c, i], preferred_element_type=f32)
                ranged[i, c * taken : (c + 1) * taken, :] = value.astype(bf16)

    def prepare(step):
        for n in range(per_step):
            i = step * per_step + n
            kernel = ak_ref[i].astype(f32)[HALO : HALO + n_rows]
            turned[i] = pltpu.roll(kernel, HALO, 1).astype(bf16)

    def along_azimuth(step):
        for n in range(per_step):
            i = step * per_step + n
            moved = jnp.dot(ranged[i, : 2 * taken], turned[i], preferred_element_type=f32)
            for c in range(2):
                line = (SUB + top) * pitch + c * DBLK + i
                for h in range(halves):
                    plane[h, pl.ds(line, taken, stride=pitch), :] = moved[
                        c * taken : (c + 1) * taken, h * LANES : (h + 1) * LANES
                    ]

    lax.fori_loop(0, steps, start, 0)
    zero = jnp.zeros((SUB * pitch, LANES), f32)
    for h in range(halves):
        plane[h, : SUB * pitch, :] = zero
        plane[h, (SUB + n_rows) * pitch :, :] = zero
    if taken < n_rows:

        def clear(n, carry):
            at = pl.multiple_of(jnp.where(n * SIDE < top, n * SIDE, n * SIDE + taken), SIDE)
            slc_ref[:, :, pl.ds(at, SIDE), :] = jnp.zeros((2, DBLK, SIDE, n_az), bf16)
            return carry

        lax.fori_loop(0, (n_rows - taken) // SIDE, clear, 0)
    wait(0)
    along_range(0)
    prepare(0)

    def resample(step, carry):
        later = jnp.minimum(step + 1, steps - 1)
        pl.when(step + 1 < steps)(lambda: wait(later))
        along_azimuth(step)
        along_range(later)
        prepare(later)
        return carry

    lax.fori_loop(0, steps, resample, 0)

    masks = group_masks((lines, LANES))
    copies = [
        pltpu.make_async_copy(stage[n // n_targets].at[n % n_targets], outs[n], out_sems.at[n])
        for n in range(len(outs))
    ]

    for t, k in enumerate(targets):
        base = (me ^ k) * dest_rows

        def blocks(j, carry):
            for half in range(2):
                for h in range(halves):
                    rows = []
                    for r in range(8):
                        at = pl.multiple_of((base + j * SIDE + half * 8 + r) * pitch, SUB)
                        rows.append(plane[h, pl.ds(at, lines), :].astype(bf16))
                    cols = gather_groups(rows, masks)
                    for g in range(8):
                        column = h * 8 + g
                        for s, (lo, hi) in enumerate(spans):
                            if lo <= column < hi:
                                for c in range(2):
                                    stage[s][t, j, column - lo, c, :, half * LANES : (half + 1) * LANES] = cols[g][
                                        c * DBLK : (c + 1) * DBLK
                                    ]
            return carry

        lax.fori_loop(0, row_blocks, blocks, 0)
        for s in range(len(spans)):
            copies[s * n_targets + t].start()

    pick_row = lax.broadcasted_iota(jnp.int32, (2 * SIDE, n_az), 0)
    pick_col = lax.broadcasted_iota(jnp.int32, (2 * SIDE, n_az), 1)
    pick = (pick_col == jnp.where(pick_row < SIDE, pick_row, pick_row + n_az - 2 * SIDE)).astype(f32).astype(bf16)

    def edges(step, carry):
        for n in range(4):
            i = step * 4 + n
            both = lax.dot_general(pick, ranged[i], (((1,), (1,)), ((), ())), preferred_element_type=f32)
            parts = [both[:, c * n_rows : (c + 1) * n_rows] for c in range(2)]
            for c in range(2):
                own_ref[i, c] = parts[c].astype(bf16)
            first_ref[i] = jnp.concatenate([p[:SUB] for p in parts], axis=0).astype(bf16)
            last_ref[i] = jnp.concatenate([p[2 * SIDE - SUB :] for p in parts], axis=0).astype(bf16)
        return carry

    if edged:
        lax.fori_loop(0, DBLK // 4, edges, 0)
    for copy in copies:
        copy.wait()


def interior(me, slc, rk, ak, part, spans, targets, edged, partners):
    n_rows, n_az = slc.shape[2], slc.shape[3]
    dest_rows = n_rows // partners
    row_blocks = dest_rows // SIDE + 1
    per_step = 2
    steps = DBLK // per_step
    shapes = [
        jax.ShapeDtypeStruct((row_blocks, hi - lo, 2, DBLK, PIX), bf16)
        for lo, hi in spans
        for _ in targets
    ]
    edge_shapes = [
        jax.ShapeDtypeStruct((DBLK, 2, 2 * SIDE, n_rows), bf16),
        jax.ShapeDtypeStruct((DBLK, 2 * SUB, n_rows), bf16),
        jax.ShapeDtypeStruct((DBLK, 2 * SUB, n_rows), bf16),
    ]
    if not edged:
        edge_shapes = []
    whole = pl.BlockSpec(memory_space=pltpu.VMEM)
    anywhere = pl.BlockSpec(memory_space=pl.ANY)
    outs = pl.pallas_call(
        functools.partial(interior_kernel, spans, targets, edged, dest_rows, part, per_step),
        in_specs=[pl.BlockSpec(memory_space=pltpu.SMEM)] + [anywhere] * 3,
        out_specs=[whole] * len(edge_shapes) + [anywhere] * len(shapes),
        out_shape=edge_shapes + shapes,
        scratch_shapes=[pltpu.VMEM((len(targets), *x.shape), bf16) for x in shapes[:: len(targets)]]
        + [
            pltpu.VMEM((2, DBLK, n_rows, n_az), bf16),
            pltpu.VMEM((DBLK, n_rows, n_rows), bf16),
            pltpu.VMEM((DBLK, *ak.shape[1:]), bf16),
            pltpu.VMEM((DBLK, n_rows, n_az), bf16),
            pltpu.VMEM((n_az // LANES, (n_rows + 2 * SUB) * odd_tiles(2 * DBLK), LANES), f32),
            pltpu.VMEM((DBLK, 2 * n_rows, n_az), bf16),
            pltpu.SemaphoreType.DMA((steps, 4)),
            pltpu.SemaphoreType.DMA((len(shapes),)),
        ],
        compiler_params=params(),
        cost_estimate=COST,
        name=f"interior_{part}_{targets[0]}",
    )(me, slc, rk, ak)
    flat = outs[len(edge_shapes) :]
    return outs[: len(edge_shapes)], [flat[s * len(targets) : (s + 1) * len(targets)] for s in range(len(spans))]


def rim_kernel(dest_rows, parts, me_ref, *refs):
    operands, outs, plane = refs[: 4 * parts], refs[4 * parts : -1], refs[-1]
    step, steps = pl.program_id(0), pl.num_programs(0)
    per_step, n_az = operands[0].shape[0], operands[3].shape[2]
    n_rows = operands[0].shape[3]
    n_dates = outs[0].shape[2]
    lines, pitch = 2 * n_dates, odd_tiles(2 * n_dates)
    row_blocks = outs[0].shape[0]
    eighths = n_rows // 8

    @pl.when(step == 0)
    def _():
        zero = jnp.zeros((pitch, LANES), f32)
        plane[:pitch, :] = zero
        plane[(eighths + 1) * pitch :, :] = zero

    row = lax.broadcasted_iota(jnp.int32, (n_rows, LANES), 0)
    lane = lax.broadcasted_iota(jnp.int32, (n_rows, LANES), 1)
    own = (row % 8) == lane // SIDE
    gather = (
        lax.broadcasted_iota(jnp.int32, (eighths, n_rows), 1) // 8
        == lax.broadcasted_iota(jnp.int32, (eighths, n_rows), 0)
    ).astype(f32).astype(bf16)
    pick_row = lax.broadcasted_iota(jnp.int32, (n_az, LANES), 0)
    pick_col = lax.broadcasted_iota(jnp.int32, (n_az, LANES), 1) % SIDE
    pick = (pick_row == jnp.where(pick_col < 8, pick_col + n_az - 8, pick_col - 8)).astype(f32).astype(bf16)
    zero = jnp.zeros((SUB, LANES), f32)
    items = [(p, i) for p in range(parts) for i in range(per_step)]
    weights = [jnp.dot(operands[4 * p + 3][i], pick, preferred_element_type=f32) for p, i in items]
    moved = []
    for (p, i), w in zip(items, weights):
        edge, left, right, _ = operands[4 * p : 4 * p + 4]
        for c in range(2):
            ends = [
                jnp.concatenate([x, zero] if c == 0 else [zero, x], axis=0)
                for x in (w[:SUB], w[n_az + SUB :])
            ]
            weight = jnp.concatenate([w[SUB : 3 * SUB], w[n_az - SUB : n_az + SUB], *ends], axis=0).astype(bf16)
            value = jnp.concatenate([edge[i, c], left[i], right[i]], axis=0)
            moved.append(lax.dot_general(value, weight, (((0,), (0,)), ((), ())), preferred_element_type=f32))
    moved = [jnp.where(own, x, 0.0).astype(bf16) for x in moved]
    packed = [jnp.dot(gather, x, preferred_element_type=f32) for x in moved]
    for n, (p, i) in enumerate(items):
        for c in range(2):
            line = pitch + c * n_dates + p * DBLK + step * per_step + i
            plane[pl.ds(line, eighths, stride=pitch), :] = packed[2 * n + c]

    @pl.when(step == steps - 1)
    def _():
        me = me_ref[0]
        for k in range(len(outs)):
            base = (me ^ k) * (dest_rows // 8)
            for j in range(row_blocks):
                for half in range(2):
                    start = pl.multiple_of((base + 2 * j + half) * pitch, SUB)
                    values = plane[pl.ds(start, lines), :].astype(bf16)
                    for c in range(2):
                        outs[k][j, c, :, half * LANES : (half + 1) * LANES] = values[
                            c * n_dates : (c + 1) * n_dates
                        ]


def rim(me, own, left, right, ak, partners):
    parts = len(own)
    n_rows = own[0].shape[3]
    n_dates = parts * DBLK
    dest_rows = n_rows // partners
    row_blocks = dest_rows // SIDE + 1
    per_step = 2
    steps = DBLK // per_step
    shape = jax.ShapeDtypeStruct((row_blocks, 2, n_dates, PIX), bf16)

    def ak_spec(p):
        return pl.BlockSpec((per_step, *ak.shape[1:]), lambda t, m: (p * steps + t, 0, 0))

    in_specs, operands = [], []
    for p in range(parts):
        in_specs += [
            pl.BlockSpec((per_step, 2, 2 * SIDE, n_rows), lambda t, m: (t, 0, 0, 0)),
            pl.BlockSpec((per_step, 2 * SUB, n_rows), lambda t, m: (t, 0, 0)),
            pl.BlockSpec((per_step, 2 * SUB, n_rows), lambda t, m: (t, 0, 0)),
            ak_spec(p),
        ]
        operands += [own[p], left[p], right[p], ak]
    grid = pltpu.PrefetchScalarGridSpec(
        num_scalar_prefetch=1,
        grid=(steps,),
        in_specs=in_specs,
        out_specs=[pl.BlockSpec(shape.shape, lambda t, m: (0, 0, 0, 0))] * partners,
        scratch_shapes=[pltpu.VMEM(((n_rows // 8 + 2) * odd_tiles(2 * n_dates), LANES), f32)],
    )
    return pl.pallas_call(
        functools.partial(rim_kernel, dest_rows, parts),
        grid_spec=grid,
        out_shape=[shape] * partners,
        compiler_params=params(),
        cost_estimate=COST,
        name="rim",
    )(me, *operands)


def block_moment(pixels):
    n = pixels.shape[0] // 2
    m = lax.dot_general(pixels, pixels, (((1,), (1,)), ((), ())), preferred_element_type=f32)
    return m[:n, :n] + m[n:, n:], m[n:, :n] - m[:n, n:]


def store_coherence(out, index, real, imag):
    n = real.shape[0]
    eye = lax.broadcasted_iota(jnp.int32, (n, n), 0) == lax.broadcasted_iota(jnp.int32, (n, n), 1)
    diagonal = jnp.where(eye, real, 0.0)
    column = lax.rsqrt(jnp.sum(diagonal, axis=1, keepdims=True) + EPS)
    row = lax.rsqrt(jnp.sum(diagonal, axis=0, keepdims=True) + EPS)
    scale = column * row
    out[(*index, 0)] = real * scale
    out[(*index, 1)] = imag * scale


def column_sums(read, scratch, row_blocks, emit):
    before = None
    for j in range(row_blocks):
        read(j, scratch.at[j])
        now = block_moment(scratch[j])
        if before is not None:
            emit(j - 1, before[0] + now[0], before[1] + now[1])
        before = now


def rim_gram_kernel(me_ref, own, before, after, state, result_in, result, out, window, pixels, sem):
    del result_in
    partners, row_blocks, _, n, _ = own.shape
    me = me_ref[0]
    total = n * partners
    lane = lax.broadcasted_iota(jnp.int32, (n, PIX), 1)
    copy = pltpu.make_async_copy(window, result.at[:, 0], sem)
    for end in range(2):

        def read(j, scratch):
            for k in range(partners):
                for c in range(2):
                    left, right = (before, own) if end == 0 else (own, after)
                    value = jnp.where(lane % SIDE < 8, left[k, j, c], right[k, j, c])
                    at = pl.multiple_of(c * total + (me ^ k) * n, SIDE)
                    scratch[pl.ds(at, n), :] = value

        def emit(u, real, imag):
            if end == 0:
                store_coherence(window, (u,), state[u, 0] + real, state[u, 1] + imag)
            else:
                out[u, 0] = real
                out[u, 1] = imag

        column_sums(read, pixels.at[end], row_blocks, emit)
        if end == 0:
            copy.start()
    copy.wait()


def rim_gram(me, own, before, after, state, result):
    partners, row_blocks, _, n, _ = own.shape
    total = n * partners
    whole = pl.BlockSpec(memory_space=pltpu.VMEM)
    anywhere = pl.BlockSpec(memory_space=pl.ANY)
    return pl.pallas_call(
        rim_gram_kernel,
        in_specs=[pl.BlockSpec(memory_space=pltpu.SMEM)] + [whole] * 4 + [anywhere],
        out_specs=[anywhere, whole],
        out_shape=[
            jax.ShapeDtypeStruct(result.shape, f32),
            jax.ShapeDtypeStruct(state.shape, f32),
        ],
        input_output_aliases={5: 0},
        scratch_shapes=[
            pltpu.VMEM(state.shape, f32),
            pltpu.VMEM((2, row_blocks, 2 * total, PIX), bf16),
            pltpu.SemaphoreType.DMA,
        ],
        compiler_params=params(),
        cost_estimate=COST,
        name="rim_gram",
    )(me, own, before, after, state, result)


def gram_kernel(partners, parts, offsets, columns, first, opening, closing, *refs):
    pieces, refs = refs[: partners * parts], refs[partners * parts :]
    if not opening:
        state, end, _, *refs = refs
    result, *refs = refs
    if opening:
        first_out, *refs = refs
    state_out, held, kept, *blocks, stage, pixels, in_sems, out_sems, state_sems = refs
    row_blocks = pieces[0].shape[0]
    me = lax.axis_index("date").astype(jnp.int32)
    total = pixels.shape[1] // 2

    def fetch(column):
        return [
            pltpu.make_async_copy(
                pieces[n].at[:, offsets[n % parts] + column], blocks[n].at[column], in_sems.at[column, n]
            )
            for n in range(partners * parts)
        ]

    def write(window):
        return pltpu.make_async_copy(stage.at[window], result.at[:, first - 1 + window], out_sems.at[window])

    def start(column, carry):
        for copy in fetch(column):
            copy.start()
        return carry

    if not opening:
        state_in = pltpu.make_async_copy(state, held, state_sems.at[0])
        state_in.start()
    lax.fori_loop(0, columns, start, 0)
    if closing:
        end_in = pltpu.make_async_copy(end, kept, state_sems.at[1])
        end_in.start()
    if opening:
        first_copy = pltpu.make_async_copy(kept, first_out, state_sems.at[1])
    else:
        state_in.wait()

    def work(column, carry):
        for copy in fetch(column):
            copy.wait()

        def read(j, scratch):
            for k in range(partners):
                for p in range(parts):
                    for c in range(2):
                        at = pl.multiple_of(c * total + (me ^ k) * (parts * DBLK) + p * DBLK, DBLK)
                        scratch[pl.ds(at, DBLK), :] = blocks[k * parts + p][column, j, c]

        def emit(u, real, imag):
            store_coherence(stage.at[column], (u,), held[u, 0] + real, held[u, 1] + imag)
            held[u, 0] = real
            held[u, 1] = imag

        column_sums(read, pixels, row_blocks, emit)
        if opening:

            @pl.when(column == 0)
            def _():
                kept[...] = held[...]
                first_copy.start()

            pl.when(column > 0)(write(column).start)
        else:
            write(column).start()
        return carry

    lax.fori_loop(0, columns, work, 0)
    if closing:
        end_in.wait()
        for u in range(row_blocks - 1):
            store_coherence(stage.at[columns], (u,), held[u, 0] + kept[u, 0], held[u, 1] + kept[u, 1])
        write(columns).start()
    else:
        state_copy = pltpu.make_async_copy(held, state_out, state_sems.at[0])
        state_copy.start()
    for window in range(1 if opening else 0, columns + (1 if closing else 0)):
        write(window).wait()
    if opening:
        first_copy.wait()
    if not closing:
        state_copy.wait()


def gram(pieces, offsets, columns, first, state, end, result, out_shape, closing):
    partners, parts = len(pieces), len(pieces[0])
    row_blocks = pieces[0][0].shape[0]
    total = out_shape.shape[-1]
    opening = state is None
    sums = jax.ShapeDtypeStruct((row_blocks - 1, 2, total, total), f32)
    anywhere = pl.BlockSpec(memory_space=pl.ANY)
    operands = [x for k in pieces for x in k]
    aliases = {}
    if not opening:
        aliases = {len(operands) + 2: 0}
        operands += [state, end, result]
    n_out = 2 if opening else 1
    return pl.pallas_call(
        functools.partial(gram_kernel, partners, parts, offsets, columns, first, opening, closing),
        in_specs=[anywhere] * len(operands),
        out_specs=[anywhere] * (1 + n_out),
        out_shape=[out_shape] + [sums] * n_out,
        input_output_aliases=aliases,
        scratch_shapes=[pltpu.VMEM(sums.shape, f32)] * 2
        + [pltpu.VMEM((columns, row_blocks, 2, DBLK, PIX), bf16)] * (partners * parts)
        + [
            pltpu.VMEM((columns + (1 if closing else 0), *sums.shape), f32),
            pltpu.VMEM((row_blocks, 2 * total, PIX), bf16),
            pltpu.SemaphoreType.DMA((columns, partners * parts)),
            pltpu.SemaphoreType.DMA((columns + 1,)),
            pltpu.SemaphoreType.DMA((2,)),
        ],
        compiler_params=params(),
        cost_estimate=COST,
        name=f"gram_{first}",
    )(*operands)


def shift(value, axis, by):
    n = lax.axis_size(axis)
    pairs = [(i, i + by) for i in range(n) if 0 <= i + by < n]
    return lax.ppermute(value, axis, pairs)


def exchange(blocks, ahead=None, gates=()):
    n = lax.axis_size("date")
    got = [blocks[0]]
    for k in range(1, n):
        block = blocks[k]
        if ahead is not None:
            block = after(block, ahead[k])
        if k == 1 and gates:
            block = after(block, *gates)
        got.append(lax.ppermute(block, "date", [(i, i ^ k) for i in range(n)]))
    if gates:
        got = got[:1] + [pltpu.with_memory_space_constraint(x, pltpu.VMEM) for x in got[1:]]
    return got


def after(value, *others):
    return lax.optimization_barrier((value, *others))[0]


def on_device(slc, range_kernel, azimuth_kernel):
    partners = lax.axis_size("date")
    n_dates, n_rows, n_az = slc.shape[1:]
    total = n_dates * partners
    columns = n_az // SIDE
    me = lax.axis_index("date").astype(jnp.int32).reshape(1)
    parts = n_dates // DBLK
    bounds = [1, 7, 13, columns]
    spans = list(zip(bounds[:-1], bounds[1:]))

    dest_windows = n_rows // partners // SIDE
    out_shape = jax.ShapeDtypeStruct((dest_windows, columns, 2, total, total), f32)

    own, left, right, sent = [], [], [], []
    turn = me
    for part in range(parts):
        part_spans = spans if part == parts - 1 else [(1, columns)]
        source = (slc, range_kernel, azimuth_kernel, part, part_spans)
        if part == 0:
            _, lead = interior(turn, *source, [partners - 1], False, partners)
            turn = after(me, lead[0][0])
        targets = [*range(1, partners - 1 if part == 0 else partners), 0]
        (edge, first, last), out = interior(turn, *source, targets, True, partners)
        turn = after(me, first)
        own.append(edge)
        left.append(shift(last, "strip", 1))
        right.append(shift(first, "strip", -1))
        if part == 0:
            out = [[x[-1], *x[:-1], y[0]] for x, y in zip(out, lead)]
        else:
            out = [[x[-1], *x[:-1]] for x in out]
        sent.append(out)
    early = [exchange(s[0]) for s in sent[:-1]]
    lead = [early[-1][-1]] if early else []
    rims = exchange([after(x, *lead) for x in rim(me, own, left, right, azimuth_kernel, partners)])
    first = [*sent[-1][0][:-1], after(sent[-1][0][-1], *rims)]
    late = [exchange(first, early[-1] if early else None)]
    rims = jnp.stack(rims)
    above, below = shift(rims, "strip", 1), shift(rims, "strip", -1)

    def column_gram(s, state, end, result):
        lo, hi = spans[s]
        pieces = [[e[k] for e in early] + [late[s][k]] for k in range(partners)]
        offsets = [lo - 1] * (parts - 1) + [0]
        closing = s == len(spans) - 1
        return gram(pieces, offsets, hi - lo, lo, state, end, result, out_shape, closing)

    late.append(exchange(sent[-1][1], late[0]))
    result, opening, state = column_gram(0, None, None, None)
    result, end = rim_gram(me, rims, above, below, opening, result)
    for s in range(1, len(spans) - 1):
        result, state = column_gram(s, state, end, result)
        late.append(exchange(sent[-1][s + 1], late[s], gates=(end,)))
    result, state = column_gram(len(spans) - 1, state, end, result)
    return result


def solution(mesh):
    in_specs = (P(None, "date", None, "strip"), P("date", None, None), P("date", None, "strip"))
    out_specs = P("date", "strip", None, None, None)
    return jax.shard_map(on_device, mesh=mesh, in_specs=in_specs, out_specs=out_specs, check_vma=False)
```

```python
import functools

import jax
import jax.numpy as jnp
from jax import lax
from jax.experimental import pallas as pl
from jax.experimental.pallas import tpu as pltpu
from jax.sharding import PartitionSpec as P

HALO = 8
SIDE = 16
PIX = SIDE * SIDE
LANES = 128
SUB = 8
DBLK = 16
EPS = 1e-06
VMEM = 62 * 1024 * 1024
COST = pl.CostEstimate(flops=1, bytes_accessed=1, transcendentals=0)

bf16 = jnp.bfloat16
f32 = jnp.float32


def params():
    return pltpu.CompilerParams(vmem_limit_bytes=VMEM)


def odd_tiles(rows):
    tiles = -(-rows // SUB)
    return (tiles + 1 - tiles % 2) * SUB


def group_masks(shape):
    group = lax.broadcasted_iota(jnp.int32, shape, 1) // SIDE
    return [(group & step) == 0 for step in (1, 2, 4)]


def gather_groups(rows, masks):
    turned = [rows[0]] + [pltpu.roll(rows[r], SIDE * r, 1) for r in range(1, 8)]
    held = [turned[-i % 8] for i in range(8)]
    for step, low in zip((1, 2, 4), masks):
        held = [jnp.where(low, held[i], held[(i - step) % 8]) for i in range(8)]
    return held


def interior_kernel(spans, targets, edged, dest_rows, part, per_step, me_ref, slc_any, rk_any, ak_any, *refs):
    if edged:
        own_ref, first_ref, last_ref, *refs = refs
    *refs, slc_ref, rk_ref, ak_ref, turned, plane, ranged, in_sems, out_sems = refs
    outs, stage = refs[: len(refs) - len(spans)], refs[len(refs) - len(spans) :]
    steps = DBLK // per_step
    n_rows, n_az = slc_ref.shape[2:]
    lines, pitch = 2 * DBLK, odd_tiles(2 * DBLK)
    n_targets = len(targets)
    row_blocks = outs[0].shape[0]
    halves = plane.shape[0]
    me = me_ref[0]
    taken, top = n_rows, 0
    if n_targets == 1:
        taken = min(n_rows, dest_rows + 2 * SIDE)
        top = jnp.clip((me ^ targets[0]) * dest_rows - SIDE, 0, n_rows - taken)
        top = pl.multiple_of(top, SIDE)
    rows_in = pl.ds(top, taken)

    def fetch(step):
        here = pl.ds(step * per_step, per_step)
        there = pl.ds(part * DBLK + step * per_step, per_step)
        return [
            pltpu.make_async_copy(rk_any.at[there, rows_in], rk_ref.at[here, pl.ds(0, taken)], in_sems.at[step, 0]),
            pltpu.make_async_copy(slc_any.at[0, there, rows_in], slc_ref.at[0, here, rows_in], in_sems.at[step, 1]),
            pltpu.make_async_copy(slc_any.at[1, there, rows_in], slc_ref.at[1, here, rows_in], in_sems.at[step, 2]),
            pltpu.make_async_copy(ak_any.at[there], ak_ref.at[here], in_sems.at[step, 3]),
        ]

    def start(step, carry):
        for copy in fetch(step):
            copy.start()
        return carry

    def wait(step):
        for copy in fetch(step):
            copy.wait()

    def along_range(step):
        for n in range(per_step):
            i = step * per_step + n
            for c in range(2):
                value = jnp.dot(rk_ref[i, :taken], slc_ref[c, i], preferred_element_type=f32)
                ranged[i, c * taken : (c + 1) * taken, :] = value.astype(bf16)

    def prepare(step):
        for n in range(per_step):
            i = step * per_step + n
            kernel = ak_ref[i].astype(f32)[HALO : HALO + n_rows]
            turned[i] = pltpu.roll(kernel, HALO, 1).astype(bf16)

    def along_azimuth(step):
        for n in range(per_step):
            i = step * per_step + n
            moved = jnp.dot(ranged[i, : 2 * taken], turned[i], preferred_element_type=f32)
            for c in range(2):
                line = (SUB + top) * pitch + c * DBLK + i
                for h in range(halves):
                    plane[h, pl.ds(line, taken, stride=pitch), :] = moved[
                        c * taken : (c + 1) * taken, h * LANES : (h + 1) * LANES
                    ]

    lax.fori_loop(0, steps, start, 0)
    zero = jnp.zeros((SUB * pitch, LANES), f32)
    for h in range(halves):
        plane[h, : SUB * pitch, :] = zero
        plane[h, (SUB + n_rows) * pitch :, :] = zero
    if taken < n_rows:

        def clear(n, carry):
            at = pl.multiple_of(jnp.where(n * SIDE < top, n * SIDE, n * SIDE + taken), SIDE)
            slc_ref[:, :, pl.ds(at, SIDE), :] = jnp.zeros((2, DBLK, SIDE, n_az), bf16)
            return carry

        lax.fori_loop(0, (n_rows - taken) // SIDE, clear, 0)
    wait(0)
    along_range(0)
    prepare(0)

    def resample(step, carry):
        later = jnp.minimum(step + 1, steps - 1)
        pl.when(step + 1 < steps)(lambda: wait(later))
        along_azimuth(step)
        along_range(later)
        prepare(later)
        return carry

    lax.fori_loop(0, steps, resample, 0)

    masks = group_masks((lines, LANES))
    def copy_out(n, j):
        return pltpu.make_async_copy(stage[n // n_targets].at[n % n_targets, j], outs[n].at[j], out_sems.at[n])


    for t, k in enumerate(targets):
        base = (me ^ k) * dest_rows

        def blocks(j, carry):
            for half in range(2):
                for h in range(halves):
                    rows = []
                    for r in range(8):
                        at = pl.multiple_of((base + j * SIDE + half * 8 + r) * pitch, SUB)
                        rows.append(plane[h, pl.ds(at, lines), :].astype(bf16))
                    cols = gather_groups(rows, masks)
                    for g in range(8):
                        column = h * 8 + g
                        for s, (lo, hi) in enumerate(spans):
                            if lo <= column < hi:
                                for c in range(2):
                                    stage[s][t, j, column - lo, c, :, half * LANES : (half + 1) * LANES] = cols[g][
                                        c * DBLK : (c + 1) * DBLK
                                    ]
            for s in range(len(spans)):
                copy_out(s * n_targets + t, j).start()
            return carry

        lax.fori_loop(0, row_blocks, blocks, 0)

    pick_row = lax.broadcasted_iota(jnp.int32, (2 * SIDE, n_az), 0)
    pick_col = lax.broadcasted_iota(jnp.int32, (2 * SIDE, n_az), 1)
    pick = (pick_col == jnp.where(pick_row < SIDE, pick_row, pick_row + n_az - 2 * SIDE)).astype(f32).astype(bf16)

    def edges(step, carry):
        for n in range(4):
            i = step * 4 + n
            both = lax.dot_general(pick, ranged[i], (((1,), (1,)), ((), ())), preferred_element_type=f32)
            parts = [both[:, c * n_rows : (c + 1) * n_rows] for c in range(2)]
            for c in range(2):
                own_ref[i, c] = parts[c].astype(bf16)
            first_ref[i] = jnp.concatenate([p[:SUB] for p in parts], axis=0).astype(bf16)
            last_ref[i] = jnp.concatenate([p[2 * SIDE - SUB :] for p in parts], axis=0).astype(bf16)
        return carry

    if edged:
        lax.fori_loop(0, DBLK // 4, edges, 0)
    for n in range(len(outs)):
        pltpu.make_async_copy(stage[n // n_targets].at[n % n_targets], outs[n], out_sems.at[n]).wait()


def interior(me, slc, rk, ak, part, spans, targets, edged, partners):
    n_rows, n_az = slc.shape[2], slc.shape[3]
    dest_rows = n_rows // partners
    row_blocks = dest_rows // SIDE + 1
    per_step = 2
    steps = DBLK // per_step
    shapes = [
        jax.ShapeDtypeStruct((row_blocks, hi - lo, 2, DBLK, PIX), bf16)
        for lo, hi in spans
        for _ in targets
    ]
    edge_shapes = [
        jax.ShapeDtypeStruct((DBLK, 2, 2 * SIDE, n_rows), bf16),
        jax.ShapeDtypeStruct((DBLK, 2 * SUB, n_rows), bf16),
        jax.ShapeDtypeStruct((DBLK, 2 * SUB, n_rows), bf16),
    ]
    if not edged:
        edge_shapes = []
    whole = pl.BlockSpec(memory_space=pltpu.VMEM)
    anywhere = pl.BlockSpec(memory_space=pl.ANY)
    outs = pl.pallas_call(
        functools.partial(interior_kernel, spans, targets, edged, dest_rows, part, per_step),
        in_specs=[pl.BlockSpec(memory_space=pltpu.SMEM)] + [anywhere] * 3,
        out_specs=[whole] * len(edge_shapes) + [anywhere] * len(shapes),
        out_shape=edge_shapes + shapes,
        scratch_shapes=[pltpu.VMEM((len(targets), *x.shape), bf16) for x in shapes[:: len(targets)]]
        + [
            pltpu.VMEM((2, DBLK, n_rows, n_az), bf16),
            pltpu.VMEM((DBLK, n_rows, n_rows), bf16),
            pltpu.VMEM((DBLK, *ak.shape[1:]), bf16),
            pltpu.VMEM((DBLK, n_rows, n_az), bf16),
            pltpu.VMEM((n_az // LANES, (n_rows + 2 * SUB) * odd_tiles(2 * DBLK), LANES), f32),
            pltpu.VMEM((DBLK, 2 * n_rows, n_az), bf16),
            pltpu.SemaphoreType.DMA((steps, 4)),
            pltpu.SemaphoreType.DMA((len(shapes),)),
        ],
        compiler_params=params(),
        cost_estimate=COST,
        name=f"interior_{part}_{targets[0]}",
    )(me, slc, rk, ak)
    flat = outs[len(edge_shapes) :]
    return outs[: len(edge_shapes)], [flat[s * len(targets) : (s + 1) * len(targets)] for s in range(len(spans))]


def rim_kernel(dest_rows, parts, me_ref, *refs):
    operands, outs, plane = refs[: 4 * parts], refs[4 * parts : -1], refs[-1]
    step, steps = pl.program_id(0), pl.num_programs(0)
    per_step, n_az = operands[0].shape[0], operands[3].shape[2]
    n_rows = operands[0].shape[3]
    n_dates = outs[0].shape[2]
    lines, pitch = 2 * n_dates, odd_tiles(2 * n_dates)
    row_blocks = outs[0].shape[0]
    eighths = n_rows // 8

    @pl.when(step == 0)
    def _():
        zero = jnp.zeros((pitch, LANES), f32)
        plane[:pitch, :] = zero
        plane[(eighths + 1) * pitch :, :] = zero

    row = lax.broadcasted_iota(jnp.int32, (n_rows, LANES), 0)
    lane = lax.broadcasted_iota(jnp.int32, (n_rows, LANES), 1)
    own = (row % 8) == lane // SIDE
    gather = (
        lax.broadcasted_iota(jnp.int32, (eighths, n_rows), 1) // 8
        == lax.broadcasted_iota(jnp.int32, (eighths, n_rows), 0)
    ).astype(f32).astype(bf16)
    pick_row = lax.broadcasted_iota(jnp.int32, (n_az, LANES), 0)
    pick_col = lax.broadcasted_iota(jnp.int32, (n_az, LANES), 1) % SIDE
    pick = (pick_row == jnp.where(pick_col < 8, pick_col + n_az - 8, pick_col - 8)).astype(f32).astype(bf16)
    zero = jnp.zeros((SUB, LANES), f32)
    items = [(p, i) for p in range(parts) for i in range(per_step)]
    weights = [jnp.dot(operands[4 * p + 3][i], pick, preferred_element_type=f32) for p, i in items]
    moved = []
    for (p, i), w in zip(items, weights):
        edge, left, right, _ = operands[4 * p : 4 * p + 4]
        for c in range(2):
            ends = [
                jnp.concatenate([x, zero] if c == 0 else [zero, x], axis=0)
                for x in (w[:SUB], w[n_az + SUB :])
            ]
            weight = jnp.concatenate([w[SUB : 3 * SUB], w[n_az - SUB : n_az + SUB], *ends], axis=0).astype(bf16)
            value = jnp.concatenate([edge[i, c], left[i], right[i]], axis=0)
            moved.append(lax.dot_general(value, weight, (((0,), (0,)), ((), ())), preferred_element_type=f32))
    moved = [jnp.where(own, x, 0.0).astype(bf16) for x in moved]
    packed = [jnp.dot(gather, x, preferred_element_type=f32) for x in moved]
    for n, (p, i) in enumerate(items):
        for c in range(2):
            line = pitch + c * n_dates + p * DBLK + step * per_step + i
            plane[pl.ds(line, eighths, stride=pitch), :] = packed[2 * n + c]

    @pl.when(step == steps - 1)
    def _():
        me = me_ref[0]
        for k in range(len(outs)):
            base = (me ^ k) * (dest_rows // 8)
            for j in range(row_blocks):
                for half in range(2):
                    start = pl.multiple_of((base + 2 * j + half) * pitch, SUB)
                    values = plane[pl.ds(start, lines), :].astype(bf16)
                    for c in range(2):
                        outs[k][j, c, :, half * LANES : (half + 1) * LANES] = values[
                            c * n_dates : (c + 1) * n_dates
                        ]


def rim(me, own, left, right, ak, partners):
    parts = len(own)
    n_rows = own[0].shape[3]
    n_dates = parts * DBLK
    dest_rows = n_rows // partners
    row_blocks = dest_rows // SIDE + 1
    per_step = 2
    steps = DBLK // per_step
    shape = jax.ShapeDtypeStruct((row_blocks, 2, n_dates, PIX), bf16)

    def ak_spec(p):
        return pl.BlockSpec((per_step, *ak.shape[1:]), lambda t, m: (p * steps + t, 0, 0))

    in_specs, operands = [], []
    for p in range(parts):
        in_specs += [
            pl.BlockSpec((per_step, 2, 2 * SIDE, n_rows), lambda t, m: (t, 0, 0, 0)),
            pl.BlockSpec((per_step, 2 * SUB, n_rows), lambda t, m: (t, 0, 0)),
            pl.BlockSpec((per_step, 2 * SUB, n_rows), lambda t, m: (t, 0, 0)),
            ak_spec(p),
        ]
        operands += [own[p], left[p], right[p], ak]
    grid = pltpu.PrefetchScalarGridSpec(
        num_scalar_prefetch=1,
        grid=(steps,),
        in_specs=in_specs,
        out_specs=[pl.BlockSpec(shape.shape, lambda t, m: (0, 0, 0, 0))] * partners,
        scratch_shapes=[pltpu.VMEM(((n_rows // 8 + 2) * odd_tiles(2 * n_dates), LANES), f32)],
    )
    return pl.pallas_call(
        functools.partial(rim_kernel, dest_rows, parts),
        grid_spec=grid,
        out_shape=[shape] * partners,
        compiler_params=params(),
        cost_estimate=COST,
        name="rim",
    )(me, *operands)


def block_moment(pixels):
    n = pixels.shape[0] // 2
    m = lax.dot_general(pixels, pixels, (((1,), (1,)), ((), ())), preferred_element_type=f32)
    return m[:n, :n] + m[n:, n:], m[n:, :n] - m[:n, n:]


def store_coherence(out, index, real, imag):
    n = real.shape[0]
    eye = lax.broadcasted_iota(jnp.int32, (n, n), 0) == lax.broadcasted_iota(jnp.int32, (n, n), 1)
    diagonal = jnp.where(eye, real, 0.0)
    column = lax.rsqrt(jnp.sum(diagonal, axis=1, keepdims=True) + EPS)
    row = lax.rsqrt(jnp.sum(diagonal, axis=0, keepdims=True) + EPS)
    scale = column * row
    out[(*index, 0)] = real * scale
    out[(*index, 1)] = imag * scale


def column_sums(read, scratch, row_blocks, emit):
    before = None
    for j in range(row_blocks):
        read(j, scratch.at[j])
        now = block_moment(scratch[j])
        if before is not None:
            emit(j - 1, before[0] + now[0], before[1] + now[1])
        before = now


def rim_gram_kernel(me_ref, own, before, after, state, result_in, result, out, window, pixels, sem):
    del result_in
    partners, row_blocks, _, n, _ = own.shape
    me = me_ref[0]
    total = n * partners
    lane = lax.broadcasted_iota(jnp.int32, (n, PIX), 1)
    copy = pltpu.make_async_copy(window, result.at[:, 0], sem)
    for end in range(2):

        def read(j, scratch):
            for k in range(partners):
                for c in range(2):
                    left, right = (before, own) if end == 0 else (own, after)
                    value = jnp.where(lane % SIDE < 8, left[k, j, c], right[k, j, c])
                    at = pl.multiple_of(c * total + (me ^ k) * n, SIDE)
                    scratch[pl.ds(at, n), :] = value

        def emit(u, real, imag):
            if end == 0:
                store_coherence(window, (u,), state[u, 0] + real, state[u, 1] + imag)
            else:
                out[u, 0] = real
                out[u, 1] = imag

        column_sums(read, pixels.at[end], row_blocks, emit)
        if end == 0:
            copy.start()
    copy.wait()


def rim_gram(me, own, before, after, state, result):
    partners, row_blocks, _, n, _ = own.shape
    total = n * partners
    whole = pl.BlockSpec(memory_space=pltpu.VMEM)
    anywhere = pl.BlockSpec(memory_space=pl.ANY)
    return pl.pallas_call(
        rim_gram_kernel,
        in_specs=[pl.BlockSpec(memory_space=pltpu.SMEM)] + [whole] * 4 + [anywhere],
        out_specs=[anywhere, whole],
        out_shape=[
            jax.ShapeDtypeStruct(result.shape, f32),
            jax.ShapeDtypeStruct(state.shape, f32),
        ],
        input_output_aliases={5: 0},
        scratch_shapes=[
            pltpu.VMEM(state.shape, f32),
            pltpu.VMEM((2, row_blocks, 2 * total, PIX), bf16),
            pltpu.SemaphoreType.DMA,
        ],
        compiler_params=params(),
        cost_estimate=COST,
        name="rim_gram",
    )(me, own, before, after, state, result)


def gram_kernel(partners, parts, offsets, columns, first, opening, closing, *refs):
    pieces, refs = refs[: partners * parts], refs[partners * parts :]
    if not opening:
        state, end, _, *refs = refs
    result, *refs = refs
    if opening:
        first_out, *refs = refs
    state_out, held, kept, *blocks, stage, pixels, in_sems, out_sems, state_sems = refs
    row_blocks = pieces[0].shape[0]
    me = lax.axis_index("date").astype(jnp.int32)
    total = pixels.shape[1] // 2

    placed = [n for n in range(parts, partners * parts) if closing and n % parts == parts - 1]

    def fetch(column):
        return [
            pltpu.make_async_copy(
                pieces[n].at[:, offsets[n % parts] + column], blocks[n].at[column], in_sems.at[column, n]
            )
            for n in range(partners * parts)
            if n not in placed
        ]

    def write(window):
        return pltpu.make_async_copy(stage.at[window], result.at[:, first - 1 + window], out_sems.at[window])

    def start(column, carry):
        for copy in fetch(column):
            copy.start()
        return carry

    if not opening:
        state_in = pltpu.make_async_copy(state, held, state_sems.at[0])
        state_in.start()
    lax.fori_loop(0, columns, start, 0)
    if closing:
        end_in = pltpu.make_async_copy(end, kept, state_sems.at[1])
        end_in.start()
    if opening:
        first_copy = pltpu.make_async_copy(kept, first_out, state_sems.at[1])
    else:
        state_in.wait()

    def work(column, carry):
        for copy in fetch(column):
            copy.wait()

        def read(j, scratch):
            for k in range(partners):
                for p in range(parts):
                    for c in range(2):
                        at = pl.multiple_of(c * total + (me ^ k) * (parts * DBLK) + p * DBLK, DBLK)
                        n = k * parts + p
                        here = pieces[n][j, column, c] if n in placed else blocks[n][column, j, c]
                        scratch[pl.ds(at, DBLK), :] = here

        def emit(u, real, imag):
            store_coherence(stage.at[column], (u,), held[u, 0] + real, held[u, 1] + imag)
            held[u, 0] = real
            held[u, 1] = imag

        column_sums(read, pixels, row_blocks, emit)
        if opening:

            @pl.when(column == 0)
            def _():
                kept[...] = held[...]
                first_copy.start()

            pl.when(column > 0)(write(column).start)
        else:
            write(column).start()
        return carry

    lax.fori_loop(0, columns, work, 0)
    if closing:
        end_in.wait()
        for u in range(row_blocks - 1):
            store_coherence(stage.at[columns], (u,), held[u, 0] + kept[u, 0], held[u, 1] + kept[u, 1])
        write(columns).start()
    else:
        state_copy = pltpu.make_async_copy(held, state_out, state_sems.at[0])
        state_copy.start()
    for window in range(1 if opening else 0, columns + (1 if closing else 0)):
        write(window).wait()
    if opening:
        first_copy.wait()
    if not closing:
        state_copy.wait()


def gram(pieces, offsets, columns, first, state, end, result, out_shape, closing):
    partners, parts = len(pieces), len(pieces[0])
    row_blocks = pieces[0][0].shape[0]
    total = out_shape.shape[-1]
    opening = state is None
    sums = jax.ShapeDtypeStruct((row_blocks - 1, 2, total, total), f32)
    anywhere = pl.BlockSpec(memory_space=pl.ANY)
    operands = [x for k in pieces for x in k]
    aliases = {}
    if not opening:
        aliases = {len(operands) + 2: 0}
        operands += [state, end, result]
    n_out = 2 if opening else 1
    return pl.pallas_call(
        functools.partial(gram_kernel, partners, parts, offsets, columns, first, opening, closing),
        in_specs=[
            pl.BlockSpec(memory_space=pltpu.VMEM)
            if closing and parts <= n < partners * parts and n % parts == parts - 1
            else anywhere
            for n in range(len(operands))
        ],
        out_specs=[anywhere] * (1 + n_out),
        out_shape=[out_shape] + [sums] * n_out,
        input_output_aliases=aliases,
        scratch_shapes=[pltpu.VMEM(sums.shape, f32)] * 2
        + [pltpu.VMEM((columns, row_blocks, 2, DBLK, PIX), bf16)] * (partners * parts)
        + [
            pltpu.VMEM((columns + (1 if closing else 0), *sums.shape), f32),
            pltpu.VMEM((row_blocks, 2 * total, PIX), bf16),
            pltpu.SemaphoreType.DMA((columns, partners * parts)),
            pltpu.SemaphoreType.DMA((columns + 1,)),
            pltpu.SemaphoreType.DMA((2,)),
        ],
        compiler_params=params(),
        cost_estimate=COST,
        name=f"gram_{first}",
    )(*operands)


def shift(value, axis, by):
    n = lax.axis_size(axis)
    pairs = [(i, i + by) for i in range(n) if 0 <= i + by < n]
    return lax.ppermute(value, axis, pairs)


def exchange(blocks, ahead=None, gates=()):
    n = lax.axis_size("date")
    got = [blocks[0]]
    for k in range(1, n):
        block = blocks[k]
        if ahead is not None:
            block = after(block, ahead[k])
        if k == 1 and gates:
            block = after(block, *gates)
        got.append(lax.ppermute(block, "date", [(i, i ^ k) for i in range(n)]))
    if gates:
        got = got[:1] + [pltpu.with_memory_space_constraint(x, pltpu.VMEM) for x in got[1:]]
    return got


def after(value, *others):
    return lax.optimization_barrier((value, *others))[0]


def on_device(slc, range_kernel, azimuth_kernel):
    partners = lax.axis_size("date")
    n_dates, n_rows, n_az = slc.shape[1:]
    total = n_dates * partners
    columns = n_az // SIDE
    me = lax.axis_index("date").astype(jnp.int32).reshape(1)
    parts = n_dates // DBLK
    bounds = [1, 7, 13, columns]
    spans = list(zip(bounds[:-1], bounds[1:]))

    dest_windows = n_rows // partners // SIDE
    out_shape = jax.ShapeDtypeStruct((dest_windows, columns, 2, total, total), f32)

    own, left, right, sent = [], [], [], []
    turn = me
    for part in range(parts):
        part_spans = spans if part == parts - 1 else [(1, columns)]
        source = (slc, range_kernel, azimuth_kernel, part, part_spans)
        if part == 0:
            _, lead = interior(turn, *source, [partners - 1], False, partners)
            turn = after(me, lead[0][0])
        targets = [*range(1, partners - 1 if part == 0 else partners), 0]
        (edge, first, last), out = interior(turn, *source, targets, True, partners)
        turn = after(me, first)
        own.append(edge)
        left.append(shift(last, "strip", 1))
        right.append(shift(first, "strip", -1))
        if part == 0:
            out = [[x[-1], *x[:-1], y[0]] for x, y in zip(out, lead)]
        else:
            out = [[x[-1], *x[:-1]] for x in out]
        sent.append(out)
    early = [exchange(s[0]) for s in sent[:-1]]
    lead = [early[-1][-1]] if early else []
    rims = exchange([after(x, *lead) for x in rim(me, own, left, right, azimuth_kernel, partners)])
    first = [*sent[-1][0][:-1], after(sent[-1][0][-1], *rims)]
    late = [exchange(first, early[-1] if early else None)]
    rims = jnp.stack(rims)
    above, below = shift(rims, "strip", 1), shift(rims, "strip", -1)

    def column_gram(s, state, end, result):
        lo, hi = spans[s]
        pieces = [[e[k] for e in early] + [late[s][k]] for k in range(partners)]
        offsets = [lo - 1] * (parts - 1) + [0]
        closing = s == len(spans) - 1
        return gram(pieces, offsets, hi - lo, lo, state, end, result, out_shape, closing)

    late.append(exchange(sent[-1][1], late[0]))
    result, opening, state = column_gram(0, None, None, None)
    result, end = rim_gram(me, rims, above, below, opening, result)
    for s in range(1, len(spans) - 1):
        result, state = column_gram(s, state, end, result)
        late.append(exchange(sent[-1][s + 1], late[s], gates=(end,)))
    result, state = column_gram(len(spans) - 1, state, end, result)
    return result


def solution(mesh):
    in_specs = (P(None, "date", None, "strip"), P("date", None, None), P("date", None, "strip"))
    out_specs = P("date", "strip", None, None, None)
    return jax.shard_map(on_device, mesh=mesh, in_specs=in_specs, out_specs=out_specs, check_vma=False)
```

```python
import functools

import jax
import jax.numpy as jnp
from jax import lax
from jax.experimental import pallas as pl
from jax.experimental.pallas import tpu as pltpu
from jax.sharding import PartitionSpec as P

HALO = 8
SIDE = 16
PIX = SIDE * SIDE
LANES = 128
SUB = 8
DBLK = 16
EPS = 1e-06
VMEM = 62 * 1024 * 1024
COST = pl.CostEstimate(flops=1, bytes_accessed=1, transcendentals=0)

bf16 = jnp.bfloat16
f32 = jnp.float32


def params():
    return pltpu.CompilerParams(vmem_limit_bytes=VMEM)


def odd_tiles(rows):
    tiles = -(-rows // SUB)
    return (tiles + 1 - tiles % 2) * SUB


def group_masks(shape):
    group = lax.broadcasted_iota(jnp.int32, shape, 1) // SIDE
    return [(group & step) == 0 for step in (1, 2, 4)]


def gather_groups(rows, masks):
    turned = [rows[0]] + [pltpu.roll(rows[r], SIDE * r, 1) for r in range(1, 8)]
    held = [turned[-i % 8] for i in range(8)]
    for step, low in zip((1, 2, 4), masks):
        held = [jnp.where(low, held[i], held[(i - step) % 8]) for i in range(8)]
    return held


def interior_kernel(spans, targets, edged, dest_rows, part, per_step, me_ref, slc_any, rk_any, ak_any, *refs):
    if edged:
        own_ref, first_ref, last_ref, *refs = refs
    *refs, slc_ref, rk_ref, ak_ref, turned, plane, ranged, in_sems, out_sems = refs
    outs, stage = refs[: len(refs) - len(spans)], refs[len(refs) - len(spans) :]
    steps = DBLK // per_step
    n_rows, n_az = slc_ref.shape[2:]
    lines, pitch = 2 * DBLK, odd_tiles(2 * DBLK)
    n_targets = len(targets)
    row_blocks = outs[0].shape[0]
    halves = plane.shape[0]
    me = me_ref[0]
    taken, top = n_rows, 0
    if n_targets == 1:
        taken = min(n_rows, dest_rows + 2 * SIDE)
        top = jnp.clip((me ^ targets[0]) * dest_rows - SIDE, 0, n_rows - taken)
        top = pl.multiple_of(top, SIDE)
    rows_in = pl.ds(top, taken)

    def fetch(step):
        here = pl.ds(step * per_step, per_step)
        there = pl.ds(part * DBLK + step * per_step, per_step)
        return [
            pltpu.make_async_copy(rk_any.at[there, rows_in], rk_ref.at[here, pl.ds(0, taken)], in_sems.at[step, 0]),
            pltpu.make_async_copy(slc_any.at[0, there, rows_in], slc_ref.at[0, here, pl.ds(0, taken)], in_sems.at[step, 1]),
            pltpu.make_async_copy(slc_any.at[1, there, rows_in], slc_ref.at[1, here, pl.ds(0, taken)], in_sems.at[step, 2]),
            pltpu.make_async_copy(ak_any.at[there], ak_ref.at[here], in_sems.at[step, 3]),
        ]

    def start(step, carry):
        for copy in fetch(step):
            copy.start()
        return carry

    def wait(step):
        for copy in fetch(step):
            copy.wait()

    def along_range(step):
        for n in range(per_step):
            i = step * per_step + n
            weights = rk_ref[i, :taken]
            if taken < n_rows:
                weights = pltpu.roll(weights.astype(f32), lax.rem(n_rows - top, n_rows), 1).astype(bf16)[:, :taken]
            for c in range(2):
                value = jnp.dot(weights, slc_ref[c, i, :taken], preferred_element_type=f32)
                ranged[i, c * taken : (c + 1) * taken, :] = value.astype(bf16)

    def prepare(step):
        for n in range(per_step):
            i = step * per_step + n
            kernel = ak_ref[i].astype(f32)[HALO : HALO + n_rows]
            turned[i] = pltpu.roll(kernel, HALO, 1).astype(bf16)

    def along_azimuth(step):
        for n in range(per_step):
            i = step * per_step + n
            moved = jnp.dot(ranged[i, : 2 * taken], turned[i], preferred_element_type=f32)
            for c in range(2):
                line = (SUB + top) * pitch + c * DBLK + i
                for h in range(halves):
                    plane[h, pl.ds(line, taken, stride=pitch), :] = moved[
                        c * taken : (c + 1) * taken, h * LANES : (h + 1) * LANES
                    ]

    lax.fori_loop(0, steps, start, 0)
    zero = jnp.zeros((SUB * pitch, LANES), f32)
    for h in range(halves):
        plane[h, : SUB * pitch, :] = zero
        plane[h, (SUB + n_rows) * pitch :, :] = zero
    wait(0)
    along_range(0)
    prepare(0)

    def resample(step, carry):
        later = jnp.minimum(step + 1, steps - 1)
        pl.when(step + 1 < steps)(lambda: wait(later))
        along_azimuth(step)
        along_range(later)
        prepare(later)
        return carry

    lax.fori_loop(0, steps, resample, 0)

    masks = group_masks((lines, LANES))
    def copy_out(n, j):
        return pltpu.make_async_copy(stage[n // n_targets].at[n % n_targets, j], outs[n].at[j], out_sems.at[n])


    for t, k in enumerate(targets):
        base = (me ^ k) * dest_rows

        def blocks(j, carry):
            for half in range(2):
                for h in range(halves):
                    rows = []
                    for r in range(8):
                        at = pl.multiple_of((base + j * SIDE + half * 8 + r) * pitch, SUB)
                        rows.append(plane[h, pl.ds(at, lines), :].astype(bf16))
                    cols = gather_groups(rows, masks)
                    for g in range(8):
                        column = h * 8 + g
                        for s, (lo, hi) in enumerate(spans):
                            if lo <= column < hi:
                                for c in range(2):
                                    stage[s][t, j, column - lo, c, :, half * LANES : (half + 1) * LANES] = cols[g][
                                        c * DBLK : (c + 1) * DBLK
                                    ]
            for s in range(len(spans)):
                copy_out(s * n_targets + t, j).start()
            return carry

        lax.fori_loop(0, row_blocks, blocks, 0)

    pick_row = lax.broadcasted_iota(jnp.int32, (2 * SIDE, n_az), 0)
    pick_col = lax.broadcasted_iota(jnp.int32, (2 * SIDE, n_az), 1)
    pick = (pick_col == jnp.where(pick_row < SIDE, pick_row, pick_row + n_az - 2 * SIDE)).astype(f32).astype(bf16)

    def edges(step, carry):
        for n in range(4):
            i = step * 4 + n
            both = lax.dot_general(pick, ranged[i], (((1,), (1,)), ((), ())), preferred_element_type=f32)
            parts = [both[:, c * n_rows : (c + 1) * n_rows] for c in range(2)]
            for c in range(2):
                own_ref[i, c] = parts[c].astype(bf16)
            first_ref[i] = jnp.concatenate([p[:SUB] for p in parts], axis=0).astype(bf16)
            last_ref[i] = jnp.concatenate([p[2 * SIDE - SUB :] for p in parts], axis=0).astype(bf16)
        return carry

    if edged:
        lax.fori_loop(0, DBLK // 4, edges, 0)
    for n in range(len(outs)):
        pltpu.make_async_copy(stage[n // n_targets].at[n % n_targets], outs[n], out_sems.at[n]).wait()


def interior(me, slc, rk, ak, part, spans, targets, edged, partners):
    n_rows, n_az = slc.shape[2], slc.shape[3]
    dest_rows = n_rows // partners
    row_blocks = dest_rows // SIDE + 1
    per_step = 2
    steps = DBLK // per_step
    shapes = [
        jax.ShapeDtypeStruct((row_blocks, hi - lo, 2, DBLK, PIX), bf16)
        for lo, hi in spans
        for _ in targets
    ]
    edge_shapes = [
        jax.ShapeDtypeStruct((DBLK, 2, 2 * SIDE, n_rows), bf16),
        jax.ShapeDtypeStruct((DBLK, 2 * SUB, n_rows), bf16),
        jax.ShapeDtypeStruct((DBLK, 2 * SUB, n_rows), bf16),
    ]
    if not edged:
        edge_shapes = []
    whole = pl.BlockSpec(memory_space=pltpu.VMEM)
    anywhere = pl.BlockSpec(memory_space=pl.ANY)
    outs = pl.pallas_call(
        functools.partial(interior_kernel, spans, targets, edged, dest_rows, part, per_step),
        in_specs=[pl.BlockSpec(memory_space=pltpu.SMEM)] + [anywhere] * 3,
        out_specs=[whole] * len(edge_shapes) + [anywhere] * len(shapes),
        out_shape=edge_shapes + shapes,
        scratch_shapes=[pltpu.VMEM((len(targets), *x.shape), bf16) for x in shapes[:: len(targets)]]
        + [
            pltpu.VMEM((2, DBLK, n_rows, n_az), bf16),
            pltpu.VMEM((DBLK, n_rows, n_rows), bf16),
            pltpu.VMEM((DBLK, *ak.shape[1:]), bf16),
            pltpu.VMEM((DBLK, n_rows, n_az), bf16),
            pltpu.VMEM((n_az // LANES, (n_rows + 2 * SUB) * odd_tiles(2 * DBLK), LANES), f32),
            pltpu.VMEM((DBLK, 2 * n_rows, n_az), bf16),
            pltpu.SemaphoreType.DMA((steps, 4)),
            pltpu.SemaphoreType.DMA((len(shapes),)),
        ],
        compiler_params=params(),
        cost_estimate=COST,
        name=f"interior_{part}_{targets[0]}",
    )(me, slc, rk, ak)
    flat = outs[len(edge_shapes) :]
    return outs[: len(edge_shapes)], [flat[s * len(targets) : (s + 1) * len(targets)] for s in range(len(spans))]


def rim_kernel(dest_rows, parts, me_ref, *refs):
    operands, outs, plane = refs[: 4 * parts], refs[4 * parts : -1], refs[-1]
    step, steps = pl.program_id(0), pl.num_programs(0)
    per_step, n_az = operands[0].shape[0], operands[3].shape[2]
    n_rows = operands[0].shape[3]
    n_dates = outs[0].shape[2]
    lines, pitch = 2 * n_dates, odd_tiles(2 * n_dates)
    row_blocks = outs[0].shape[0]
    eighths = n_rows // 8

    @pl.when(step == 0)
    def _():
        zero = jnp.zeros((pitch, LANES), f32)
        plane[:pitch, :] = zero
        plane[(eighths + 1) * pitch :, :] = zero

    row = lax.broadcasted_iota(jnp.int32, (n_rows, LANES), 0)
    lane = lax.broadcasted_iota(jnp.int32, (n_rows, LANES), 1)
    own = (row % 8) == lane // SIDE
    gather = (
        lax.broadcasted_iota(jnp.int32, (eighths, n_rows), 1) // 8
        == lax.broadcasted_iota(jnp.int32, (eighths, n_rows), 0)
    ).astype(f32).astype(bf16)
    pick_row = lax.broadcasted_iota(jnp.int32, (n_az, LANES), 0)
    pick_col = lax.broadcasted_iota(jnp.int32, (n_az, LANES), 1) % SIDE
    pick = (pick_row == jnp.where(pick_col < 8, pick_col + n_az - 8, pick_col - 8)).astype(f32).astype(bf16)
    zero = jnp.zeros((SUB, LANES), f32)
    items = [(p, i) for p in range(parts) for i in range(per_step)]
    weights = [jnp.dot(operands[4 * p + 3][i], pick, preferred_element_type=f32) for p, i in items]
    moved = []
    for (p, i), w in zip(items, weights):
        edge, left, right, _ = operands[4 * p : 4 * p + 4]
        for c in range(2):
            ends = [
                jnp.concatenate([x, zero] if c == 0 else [zero, x], axis=0)
                for x in (w[:SUB], w[n_az + SUB :])
            ]
            weight = jnp.concatenate([w[SUB : 3 * SUB], w[n_az - SUB : n_az + SUB], *ends], axis=0).astype(bf16)
            value = jnp.concatenate([edge[i, c], left[i], right[i]], axis=0)
            moved.append(lax.dot_general(value, weight, (((0,), (0,)), ((), ())), preferred_element_type=f32))
    moved = [jnp.where(own, x, 0.0).astype(bf16) for x in moved]
    packed = [jnp.dot(gather, x, preferred_element_type=f32) for x in moved]
    for n, (p, i) in enumerate(items):
        for c in range(2):
            line = pitch + c * n_dates + p * DBLK + step * per_step + i
            plane[pl.ds(line, eighths, stride=pitch), :] = packed[2 * n + c]

    @pl.when(step == steps - 1)
    def _():
        me = me_ref[0]
        for k in range(len(outs)):
            base = (me ^ k) * (dest_rows // 8)
            for j in range(row_blocks):
                for half in range(2):
                    start = pl.multiple_of((base + 2 * j + half) * pitch, SUB)
                    values = plane[pl.ds(start, lines), :].astype(bf16)
                    for c in range(2):
                        outs[k][j, c, :, half * LANES : (half + 1) * LANES] = values[
                            c * n_dates : (c + 1) * n_dates
                        ]


def rim(me, own, left, right, ak, partners):
    parts = len(own)
    n_rows = own[0].shape[3]
    n_dates = parts * DBLK
    dest_rows = n_rows // partners
    row_blocks = dest_rows // SIDE + 1
    per_step = 2
    steps = DBLK // per_step
    shape = jax.ShapeDtypeStruct((row_blocks, 2, n_dates, PIX), bf16)

    def ak_spec(p):
        return pl.BlockSpec((per_step, *ak.shape[1:]), lambda t, m: (p * steps + t, 0, 0))

    in_specs, operands = [], []
    for p in range(parts):
        in_specs += [
            pl.BlockSpec((per_step, 2, 2 * SIDE, n_rows), lambda t, m: (t, 0, 0, 0)),
            pl.BlockSpec((per_step, 2 * SUB, n_rows), lambda t, m: (t, 0, 0)),
            pl.BlockSpec((per_step, 2 * SUB, n_rows), lambda t, m: (t, 0, 0)),
            ak_spec(p),
        ]
        operands += [own[p], left[p], right[p], ak]
    grid = pltpu.PrefetchScalarGridSpec(
        num_scalar_prefetch=1,
        grid=(steps,),
        in_specs=in_specs,
        out_specs=[pl.BlockSpec(shape.shape, lambda t, m: (0, 0, 0, 0))] * partners,
        scratch_shapes=[pltpu.VMEM(((n_rows // 8 + 2) * odd_tiles(2 * n_dates), LANES), f32)],
    )
    return pl.pallas_call(
        functools.partial(rim_kernel, dest_rows, parts),
        grid_spec=grid,
        out_shape=[shape] * partners,
        compiler_params=params(),
        cost_estimate=COST,
        name="rim",
    )(me, *operands)


def block_moment(pixels):
    n = pixels.shape[0] // 2
    m = lax.dot_general(pixels, pixels, (((1,), (1,)), ((), ())), preferred_element_type=f32)
    return m[:n, :n] + m[n:, n:], m[n:, :n] - m[:n, n:]


def store_coherence(out, index, real, imag):
    n = real.shape[0]
    eye = lax.broadcasted_iota(jnp.int32, (n, n), 0) == lax.broadcasted_iota(jnp.int32, (n, n), 1)
    diagonal = jnp.where(eye, real, 0.0)
    column = lax.rsqrt(jnp.sum(diagonal, axis=1, keepdims=True) + EPS)
    row = lax.rsqrt(jnp.sum(diagonal, axis=0, keepdims=True) + EPS)
    scale = column * row
    out[(*index, 0)] = real * scale
    out[(*index, 1)] = imag * scale


def column_sums(read, scratch, row_blocks, emit):
    before = None
    for j in range(row_blocks):
        read(j, scratch.at[j])
        now = block_moment(scratch[j])
        if before is not None:
            emit(j - 1, before[0] + now[0], before[1] + now[1])
        before = now


def rim_gram_kernel(me_ref, own, before, after, state, result_in, result, out, window, pixels, sem):
    del result_in
    partners, row_blocks, _, n, _ = own.shape
    me = me_ref[0]
    total = n * partners
    lane = lax.broadcasted_iota(jnp.int32, (n, PIX), 1)
    copy = pltpu.make_async_copy(window, result.at[:, 0], sem)
    for end in range(2):

        def read(j, scratch):
            for k in range(partners):
                for c in range(2):
                    left, right = (before, own) if end == 0 else (own, after)
                    value = jnp.where(lane % SIDE < 8, left[k, j, c], right[k, j, c])
                    at = pl.multiple_of(c * total + (me ^ k) * n, SIDE)
                    scratch[pl.ds(at, n), :] = value

        def emit(u, real, imag):
            if end == 0:
                store_coherence(window, (u,), state[u, 0] + real, state[u, 1] + imag)
            else:
                out[u, 0] = real
                out[u, 1] = imag

        column_sums(read, pixels.at[end], row_blocks, emit)
        if end == 0:
            copy.start()
    copy.wait()


def rim_gram(me, own, before, after, state, result):
    partners, row_blocks, _, n, _ = own.shape
    total = n * partners
    whole = pl.BlockSpec(memory_space=pltpu.VMEM)
    anywhere = pl.BlockSpec(memory_space=pl.ANY)
    return pl.pallas_call(
        rim_gram_kernel,
        in_specs=[pl.BlockSpec(memory_space=pltpu.SMEM)] + [whole] * 4 + [anywhere],
        out_specs=[anywhere, whole],
        out_shape=[
            jax.ShapeDtypeStruct(result.shape, f32),
            jax.ShapeDtypeStruct(state.shape, f32),
        ],
        input_output_aliases={5: 0},
        scratch_shapes=[
            pltpu.VMEM(state.shape, f32),
            pltpu.VMEM((2, row_blocks, 2 * total, PIX), bf16),
            pltpu.SemaphoreType.DMA,
        ],
        compiler_params=params(),
        cost_estimate=COST,
        name="rim_gram",
    )(me, own, before, after, state, result)


def gram_kernel(partners, parts, offsets, columns, first, opening, closing, *refs):
    pieces, refs = refs[: partners * parts], refs[partners * parts :]
    if not opening:
        state, end, _, *refs = refs
    result, *refs = refs
    if opening:
        first_out, *refs = refs
    state_out, held, kept, *blocks, stage, pixels, in_sems, out_sems, state_sems = refs
    row_blocks = pieces[0].shape[0]
    me = lax.axis_index("date").astype(jnp.int32)
    total = pixels.shape[1] // 2

    placed = [n for n in range(parts, partners * parts) if closing and n % parts == parts - 1]

    def fetch(column):
        return [
            pltpu.make_async_copy(
                pieces[n].at[:, offsets[n % parts] + column], blocks[n].at[column], in_sems.at[column, n]
            )
            for n in range(partners * parts)
            if n not in placed
        ]

    def write(window):
        return pltpu.make_async_copy(stage.at[window], result.at[:, first - 1 + window], out_sems.at[window])

    def start(column, carry):
        for copy in fetch(column):
            copy.start()
        return carry

    if not opening:
        state_in = pltpu.make_async_copy(state, held, state_sems.at[0])
        state_in.start()
    lax.fori_loop(0, columns, start, 0)
    if closing:
        end_in = pltpu.make_async_copy(end, kept, state_sems.at[1])
        end_in.start()
    if opening:
        first_copy = pltpu.make_async_copy(kept, first_out, state_sems.at[1])
    else:
        state_in.wait()

    def work(column, carry):
        for copy in fetch(column):
            copy.wait()

        def read(j, scratch):
            for k in range(partners):
                for p in range(parts):
                    for c in range(2):
                        at = pl.multiple_of(c * total + (me ^ k) * (parts * DBLK) + p * DBLK, DBLK)
                        n = k * parts + p
                        here = pieces[n][j, column, c] if n in placed else blocks[n][column, j, c]
                        scratch[pl.ds(at, DBLK), :] = here

        def emit(u, real, imag):
            store_coherence(stage.at[column], (u,), held[u, 0] + real, held[u, 1] + imag)
            held[u, 0] = real
            held[u, 1] = imag

        column_sums(read, pixels, row_blocks, emit)
        if opening:

            @pl.when(column == 0)
            def _():
                kept[...] = held[...]
                first_copy.start()

            pl.when(column > 0)(write(column).start)
        else:
            write(column).start()
        return carry

    lax.fori_loop(0, columns, work, 0)
    if closing:
        end_in.wait()
        for u in range(row_blocks - 1):
            store_coherence(stage.at[columns], (u,), held[u, 0] + kept[u, 0], held[u, 1] + kept[u, 1])
        write(columns).start()
    else:
        state_copy = pltpu.make_async_copy(held, state_out, state_sems.at[0])
        state_copy.start()
    for window in range(1 if opening else 0, columns + (1 if closing else 0)):
        write(window).wait()
    if opening:
        first_copy.wait()
    if not closing:
        state_copy.wait()


def gram(pieces, offsets, columns, first, state, end, result, out_shape, closing):
    partners, parts = len(pieces), len(pieces[0])
    row_blocks = pieces[0][0].shape[0]
    total = out_shape.shape[-1]
    opening = state is None
    sums = jax.ShapeDtypeStruct((row_blocks - 1, 2, total, total), f32)
    anywhere = pl.BlockSpec(memory_space=pl.ANY)
    operands = [x for k in pieces for x in k]
    aliases = {}
    if not opening:
        aliases = {len(operands) + 2: 0}
        operands += [state, end, result]
    n_out = 2 if opening else 1
    return pl.pallas_call(
        functools.partial(gram_kernel, partners, parts, offsets, columns, first, opening, closing),
        in_specs=[
            pl.BlockSpec(memory_space=pltpu.VMEM)
            if closing and parts <= n < partners * parts and n % parts == parts - 1
            else anywhere
            for n in range(len(operands))
        ],
        out_specs=[anywhere] * (1 + n_out),
        out_shape=[out_shape] + [sums] * n_out,
        input_output_aliases=aliases,
        scratch_shapes=[pltpu.VMEM(sums.shape, f32)] * 2
        + [pltpu.VMEM((columns, row_blocks, 2, DBLK, PIX), bf16)] * (partners * parts)
        + [
            pltpu.VMEM((columns + (1 if closing else 0), *sums.shape), f32),
            pltpu.VMEM((row_blocks, 2 * total, PIX), bf16),
            pltpu.SemaphoreType.DMA((columns, partners * parts)),
            pltpu.SemaphoreType.DMA((columns + 1,)),
            pltpu.SemaphoreType.DMA((2,)),
        ],
        compiler_params=params(),
        cost_estimate=COST,
        name=f"gram_{first}",
    )(*operands)


def shift(value, axis, by):
    n = lax.axis_size(axis)
    pairs = [(i, i + by) for i in range(n) if 0 <= i + by < n]
    return lax.ppermute(value, axis, pairs)


def exchange(blocks, ahead=None, gates=()):
    n = lax.axis_size("date")
    got = [blocks[0]]
    for k in range(1, n):
        block = blocks[k]
        if ahead is not None:
            block = after(block, ahead[k])
        if k == 1 and gates:
            block = after(block, *gates)
        got.append(lax.ppermute(block, "date", [(i, i ^ k) for i in range(n)]))
    if gates:
        got = got[:1] + [pltpu.with_memory_space_constraint(x, pltpu.VMEM) for x in got[1:]]
    return got


def after(value, *others):
    return lax.optimization_barrier((value, *others))[0]


def on_device(slc, range_kernel, azimuth_kernel):
    partners = lax.axis_size("date")
    n_dates, n_rows, n_az = slc.shape[1:]
    total = n_dates * partners
    columns = n_az // SIDE
    me = lax.axis_index("date").astype(jnp.int32).reshape(1)
    parts = n_dates // DBLK
    bounds = [1, 7, 13, columns]
    spans = list(zip(bounds[:-1], bounds[1:]))

    dest_windows = n_rows // partners // SIDE
    out_shape = jax.ShapeDtypeStruct((dest_windows, columns, 2, total, total), f32)

    own, left, right, sent = [], [], [], []
    turn = me
    for part in range(parts):
        part_spans = spans if part == parts - 1 else [(1, columns)]
        source = (slc, range_kernel, azimuth_kernel, part, part_spans)
        if part == 0:
            _, lead = interior(turn, *source, [partners - 1], False, partners)
            turn = after(me, lead[0][0])
        targets = [*range(1, partners - 1 if part == 0 else partners), 0]
        (edge, first, last), out = interior(turn, *source, targets, True, partners)
        turn = after(me, first)
        own.append(edge)
        left.append(shift(last, "strip", 1))
        right.append(shift(first, "strip", -1))
        if part == 0:
            out = [[x[-1], *x[:-1], y[0]] for x, y in zip(out, lead)]
        else:
            out = [[x[-1], *x[:-1]] for x in out]
        sent.append(out)
    early = [exchange(s[0]) for s in sent[:-1]]
    lead = [early[-1][-1]] if early else []
    rims = exchange([after(x, *lead) for x in rim(me, own, left, right, azimuth_kernel, partners)])
    first = [*sent[-1][0][:-1], after(sent[-1][0][-1], *rims)]
    late = [exchange(first, early[-1] if early else None)]
    rims = jnp.stack(rims)
    above, below = shift(rims, "strip", 1), shift(rims, "strip", -1)

    def column_gram(s, state, end, result):
        lo, hi = spans[s]
        pieces = [[e[k] for e in early] + [late[s][k]] for k in range(partners)]
        offsets = [lo - 1] * (parts - 1) + [0]
        closing = s == len(spans) - 1
        return gram(pieces, offsets, hi - lo, lo, state, end, result, out_shape, closing)

    late.append(exchange(sent[-1][1], late[0]))
    result, opening, state = column_gram(0, None, None, None)
    result, end = rim_gram(me, rims, above, below, opening, result)
    for s in range(1, len(spans) - 1):
        result, state = column_gram(s, state, end, result)
        late.append(exchange(sent[-1][s + 1], late[s], gates=(end,)))
    result, state = column_gram(len(spans) - 1, state, end, result)
    return result


def solution(mesh):
    in_specs = (P(None, "date", None, "strip"), P("date", None, None), P("date", None, "strip"))
    out_specs = P("date", "strip", None, None, None)
    return jax.shard_map(on_device, mesh=mesh, in_specs=in_specs, out_specs=out_specs, check_vma=False)
```

```python
import functools

import jax
import jax.numpy as jnp
from jax import lax
from jax.experimental import pallas as pl
from jax.experimental.pallas import tpu as pltpu
from jax.sharding import PartitionSpec as P

HALO = 8
SIDE = 16
PIX = SIDE * SIDE
LANES = 128
SUB = 8
DBLK = 16
EPS = 1e-06
VMEM = 62 * 1024 * 1024
COST = pl.CostEstimate(flops=1, bytes_accessed=1, transcendentals=0)

bf16 = jnp.bfloat16
f32 = jnp.float32


def params():
    return pltpu.CompilerParams(vmem_limit_bytes=VMEM)


def odd_tiles(rows):
    tiles = -(-rows // SUB)
    return (tiles + 1 - tiles % 2) * SUB


def group_masks(shape):
    group = lax.broadcasted_iota(jnp.int32, shape, 1) // SIDE
    return [(group & step) == 0 for step in (1, 2, 4)]


def gather_groups(rows, masks):
    turned = [rows[0]] + [pltpu.roll(rows[r], SIDE * r, 1) for r in range(1, 8)]
    held = [turned[-i % 8] for i in range(8)]
    for step, low in zip((1, 2, 4), masks):
        held = [jnp.where(low, held[i], held[(i - step) % 8]) for i in range(8)]
    return held


def interior_kernel(spans, targets, edged, dest_rows, part, per_step, me_ref, slc_any, rk_any, ak_any, *refs):
    if edged:
        own_ref, first_ref, last_ref, *refs = refs
    *refs, slc_ref, rk_ref, ak_ref, turned, plane, ranged, in_sems, out_sems = refs
    outs, stage = refs[: len(refs) - len(spans)], refs[len(refs) - len(spans) :]
    steps = DBLK // per_step
    n_rows, n_az = slc_ref.shape[2:]
    lines, pitch = 2 * DBLK, odd_tiles(2 * DBLK)
    n_targets = len(targets)
    row_blocks = outs[0].shape[0]
    halves = plane.shape[0]
    me = me_ref[0]
    taken, top = n_rows, 0
    if n_targets == 1:
        taken = min(n_rows, dest_rows + 2 * SIDE)
        top = jnp.clip((me ^ targets[0]) * dest_rows - SIDE, 0, n_rows - taken)
        top = pl.multiple_of(top, SIDE)
    rows_in = pl.ds(top, taken)

    def fetch(step):
        here = pl.ds(step * per_step, per_step)
        there = pl.ds(part * DBLK + step * per_step, per_step)
        return [
            pltpu.make_async_copy(rk_any.at[there, rows_in], rk_ref.at[here, pl.ds(0, taken)], in_sems.at[step, 0]),
            pltpu.make_async_copy(slc_any.at[0, there, rows_in], slc_ref.at[0, here, pl.ds(0, taken)], in_sems.at[step, 1]),
            pltpu.make_async_copy(slc_any.at[1, there, rows_in], slc_ref.at[1, here, pl.ds(0, taken)], in_sems.at[step, 2]),
            pltpu.make_async_copy(ak_any.at[there], ak_ref.at[here], in_sems.at[step, 3]),
        ]

    def start(step, carry):
        for copy in fetch(step):
            copy.start()
        return carry

    def wait(step):
        for copy in fetch(step):
            copy.wait()

    def along_range(step):
        for n in range(per_step):
            i = step * per_step + n
            weights = rk_ref[i, :taken]
            if taken < n_rows:
                weights = pltpu.roll(weights.astype(f32), lax.rem(n_rows - top, n_rows), 1).astype(bf16)[:, :taken]
            for c in range(2):
                value = jnp.dot(weights, slc_ref[c, i, :taken], preferred_element_type=f32)
                ranged[i, c * taken : (c + 1) * taken, :] = value.astype(bf16)

    def prepare(step):
        for n in range(per_step):
            i = step * per_step + n
            kernel = ak_ref[i].astype(f32)[HALO : HALO + n_rows]
            turned[i] = pltpu.roll(kernel, HALO, 1).astype(bf16)

    def along_azimuth(step):
        for n in range(per_step):
            i = step * per_step + n
            moved = jnp.dot(ranged[i, : 2 * taken], turned[i], preferred_element_type=f32)
            for c in range(2):
                line = (SUB + top) * pitch + c * DBLK + i
                for h in range(halves):
                    plane[h, pl.ds(line, taken, stride=pitch), :] = moved[
                        c * taken : (c + 1) * taken, h * LANES : (h + 1) * LANES
                    ]

    lax.fori_loop(0, steps, start, 0)
    zero = jnp.zeros((SUB * pitch, LANES), f32)
    for h in range(halves):
        plane[h, : SUB * pitch, :] = zero
        plane[h, (SUB + n_rows) * pitch :, :] = zero
    wait(0)
    along_range(0)
    prepare(0)

    def resample(step, carry):
        later = jnp.minimum(step + 1, steps - 1)
        pl.when(step + 1 < steps)(lambda: wait(later))
        along_azimuth(step)
        along_range(later)
        prepare(later)
        return carry

    lax.fori_loop(0, steps, resample, 0)

    masks = group_masks((lines, LANES))
    def copy_out(n, j):
        return pltpu.make_async_copy(stage[n // n_targets].at[n % n_targets, j], outs[n].at[j], out_sems.at[n])


    for t, k in enumerate(targets):
        base = (me ^ k) * dest_rows

        def blocks(j, carry):
            for half in range(2):
                for h in range(halves):
                    rows = []
                    for r in range(8):
                        at = pl.multiple_of((base + j * SIDE + half * 8 + r) * pitch, SUB)
                        rows.append(plane[h, pl.ds(at, lines), :].astype(bf16))
                    cols = gather_groups(rows, masks)
                    for g in range(8):
                        column = h * 8 + g
                        for s, (lo, hi) in enumerate(spans):
                            if lo <= column < hi:
                                for c in range(2):
                                    stage[s][t, j, column - lo, c, :, half * LANES : (half + 1) * LANES] = cols[g][
                                        c * DBLK : (c + 1) * DBLK
                                    ]
            for s in range(len(spans)):
                copy_out(s * n_targets + t, j).start()
            return carry

        lax.fori_loop(0, row_blocks, blocks, 0)

    pick_row = lax.broadcasted_iota(jnp.int32, (2 * SIDE, n_az), 0)
    pick_col = lax.broadcasted_iota(jnp.int32, (2 * SIDE, n_az), 1)
    pick = (pick_col == jnp.where(pick_row < SIDE, pick_row, pick_row + n_az - 2 * SIDE)).astype(f32).astype(bf16)

    def edges(step, carry):
        for n in range(4):
            i = step * 4 + n
            both = lax.dot_general(pick, ranged[i], (((1,), (1,)), ((), ())), preferred_element_type=f32)
            parts = [both[:, c * n_rows : (c + 1) * n_rows] for c in range(2)]
            for c in range(2):
                own_ref[i, c] = parts[c].astype(bf16)
            first_ref[i] = jnp.concatenate([p[:SUB] for p in parts], axis=0).astype(bf16)
            last_ref[i] = jnp.concatenate([p[2 * SIDE - SUB :] for p in parts], axis=0).astype(bf16)
        return carry

    if edged:
        lax.fori_loop(0, DBLK // 4, edges, 0)
    for n in range(len(outs)):
        pltpu.make_async_copy(stage[n // n_targets].at[n % n_targets], outs[n], out_sems.at[n]).wait()


def interior(me, slc, rk, ak, part, spans, targets, edged, partners):
    n_rows, n_az = slc.shape[2], slc.shape[3]
    dest_rows = n_rows // partners
    row_blocks = dest_rows // SIDE + 1
    per_step = 2
    steps = DBLK // per_step
    shapes = [
        jax.ShapeDtypeStruct((row_blocks, hi - lo, 2, DBLK, PIX), bf16)
        for lo, hi in spans
        for _ in targets
    ]
    edge_shapes = [
        jax.ShapeDtypeStruct((DBLK, 2, 2 * SIDE, n_rows), bf16),
        jax.ShapeDtypeStruct((DBLK, 2 * SUB, n_rows), bf16),
        jax.ShapeDtypeStruct((DBLK, 2 * SUB, n_rows), bf16),
    ]
    if not edged:
        edge_shapes = []
    whole = pl.BlockSpec(memory_space=pltpu.VMEM)
    anywhere = pl.BlockSpec(memory_space=pl.ANY)
    outs = pl.pallas_call(
        functools.partial(interior_kernel, spans, targets, edged, dest_rows, part, per_step),
        in_specs=[pl.BlockSpec(memory_space=pltpu.SMEM)] + [anywhere] * 3,
        out_specs=[whole] * len(edge_shapes) + [anywhere] * len(shapes),
        out_shape=edge_shapes + shapes,
        scratch_shapes=[pltpu.VMEM((len(targets), *x.shape), bf16) for x in shapes[:: len(targets)]]
        + [
            pltpu.VMEM((2, DBLK, n_rows, n_az), bf16),
            pltpu.VMEM((DBLK, n_rows, n_rows), bf16),
            pltpu.VMEM((DBLK, *ak.shape[1:]), bf16),
            pltpu.VMEM((DBLK, n_rows, n_az), bf16),
            pltpu.VMEM((n_az // LANES, (n_rows + 2 * SUB) * odd_tiles(2 * DBLK), LANES), f32),
            pltpu.VMEM((DBLK, 2 * n_rows, n_az), bf16),
            pltpu.SemaphoreType.DMA((steps, 4)),
            pltpu.SemaphoreType.DMA((len(shapes),)),
        ],
        compiler_params=params(),
        cost_estimate=COST,
        name=f"interior_{part}_{targets[0]}",
    )(me, slc, rk, ak)
    flat = outs[len(edge_shapes) :]
    return outs[: len(edge_shapes)], [flat[s * len(targets) : (s + 1) * len(targets)] for s in range(len(spans))]


def rim_kernel(dest_rows, parts, me_ref, *refs):
    operands, outs, plane = refs[: 4 * parts], refs[4 * parts : -1], refs[-1]
    step, steps = pl.program_id(0), pl.num_programs(0)
    per_step, n_az = operands[0].shape[0], operands[3].shape[2]
    n_rows = operands[0].shape[3]
    n_dates = outs[0].shape[2]
    lines, pitch = 2 * n_dates, odd_tiles(2 * n_dates)
    row_blocks = outs[0].shape[0]
    eighths = n_rows // 8

    @pl.when(step == 0)
    def _():
        zero = jnp.zeros((pitch, LANES), f32)
        plane[:pitch, :] = zero
        plane[(eighths + 1) * pitch :, :] = zero

    row = lax.broadcasted_iota(jnp.int32, (n_rows, LANES), 0)
    lane = lax.broadcasted_iota(jnp.int32, (n_rows, LANES), 1)
    own = (row % 8) == lane // SIDE
    gather = (
        lax.broadcasted_iota(jnp.int32, (eighths, n_rows), 1) // 8
        == lax.broadcasted_iota(jnp.int32, (eighths, n_rows), 0)
    ).astype(f32).astype(bf16)
    pick_row = lax.broadcasted_iota(jnp.int32, (n_az, LANES), 0)
    pick_col = lax.broadcasted_iota(jnp.int32, (n_az, LANES), 1) % SIDE
    pick = (pick_row == jnp.where(pick_col < 8, pick_col + n_az - 8, pick_col - 8)).astype(f32).astype(bf16)
    zero = jnp.zeros((SUB, LANES), f32)
    items = [(p, i) for p in range(parts) for i in range(per_step)]
    weights = [jnp.dot(operands[4 * p + 3][i], pick, preferred_element_type=f32) for p, i in items]
    moved = []
    for (p, i), w in zip(items, weights):
        edge, left, right, _ = operands[4 * p : 4 * p + 4]
        for c in range(2):
            ends = [
                jnp.concatenate([x, zero] if c == 0 else [zero, x], axis=0)
                for x in (w[:SUB], w[n_az + SUB :])
            ]
            weight = jnp.concatenate([w[SUB : 3 * SUB], w[n_az - SUB : n_az + SUB], *ends], axis=0).astype(bf16)
            value = jnp.concatenate([edge[i, c], left[i], right[i]], axis=0)
            moved.append(lax.dot_general(value, weight, (((0,), (0,)), ((), ())), preferred_element_type=f32))
    moved = [jnp.where(own, x, 0.0).astype(bf16) for x in moved]
    packed = [jnp.dot(gather, x, preferred_element_type=f32) for x in moved]
    for n, (p, i) in enumerate(items):
        for c in range(2):
            line = pitch + c * n_dates + p * DBLK + step * per_step + i
            plane[pl.ds(line, eighths, stride=pitch), :] = packed[2 * n + c]

    @pl.when(step == steps - 1)
    def _():
        me = me_ref[0]
        for k in range(len(outs)):
            base = (me ^ k) * (dest_rows // 8)
            for j in range(row_blocks):
                for half in range(2):
                    start = pl.multiple_of((base + 2 * j + half) * pitch, SUB)
                    values = plane[pl.ds(start, lines), :].astype(bf16)
                    for c in range(2):
                        outs[k][j, c, :, half * LANES : (half + 1) * LANES] = values[
                            c * n_dates : (c + 1) * n_dates
                        ]


def rim(me, own, left, right, ak, partners):
    parts = len(own)
    n_rows = own[0].shape[3]
    n_dates = parts * DBLK
    dest_rows = n_rows // partners
    row_blocks = dest_rows // SIDE + 1
    per_step = 2
    steps = DBLK // per_step
    shape = jax.ShapeDtypeStruct((row_blocks, 2, n_dates, PIX), bf16)

    def ak_spec(p):
        return pl.BlockSpec((per_step, *ak.shape[1:]), lambda t, m: (p * steps + t, 0, 0))

    in_specs, operands = [], []
    for p in range(parts):
        in_specs += [
            pl.BlockSpec((per_step, 2, 2 * SIDE, n_rows), lambda t, m: (t, 0, 0, 0)),
            pl.BlockSpec((per_step, 2 * SUB, n_rows), lambda t, m: (t, 0, 0)),
            pl.BlockSpec((per_step, 2 * SUB, n_rows), lambda t, m: (t, 0, 0)),
            ak_spec(p),
        ]
        operands += [own[p], left[p], right[p], ak]
    grid = pltpu.PrefetchScalarGridSpec(
        num_scalar_prefetch=1,
        grid=(steps,),
        in_specs=in_specs,
        out_specs=[pl.BlockSpec(shape.shape, lambda t, m: (0, 0, 0, 0))] * partners,
        scratch_shapes=[pltpu.VMEM(((n_rows // 8 + 2) * odd_tiles(2 * n_dates), LANES), f32)],
    )
    return pl.pallas_call(
        functools.partial(rim_kernel, dest_rows, parts),
        grid_spec=grid,
        out_shape=[shape] * partners,
        compiler_params=params(),
        cost_estimate=COST,
        name="rim",
    )(me, *operands)


def block_moment(pixels):
    n = pixels.shape[0] // 2
    m = lax.dot_general(pixels, pixels, (((1,), (1,)), ((), ())), preferred_element_type=f32)
    return m[:n, :n] + m[n:, n:], m[n:, :n] - m[:n, n:]


def store_coherence(out, index, real, imag):
    n = real.shape[0]
    eye = lax.broadcasted_iota(jnp.int32, (n, n), 0) == lax.broadcasted_iota(jnp.int32, (n, n), 1)
    diagonal = jnp.where(eye, real, 0.0)
    column = lax.rsqrt(jnp.sum(diagonal, axis=1, keepdims=True) + EPS)
    row = lax.rsqrt(jnp.sum(diagonal, axis=0, keepdims=True) + EPS)
    scale = column * row
    out[(*index, 0)] = real * scale
    out[(*index, 1)] = imag * scale


def column_sums(read, scratch, row_blocks, emit):
    before = None
    for j in range(row_blocks):
        read(j, scratch.at[j])
        now = block_moment(scratch[j])
        if before is not None:
            emit(j - 1, before[0] + now[0], before[1] + now[1])
        before = now


def rim_gram_kernel(me_ref, own, before, after, state, result_in, result, out, window, pixels, sem):
    del result_in
    partners, row_blocks, _, n, _ = own.shape
    me = me_ref[0]
    total = n * partners
    lane = lax.broadcasted_iota(jnp.int32, (n, PIX), 1)
    copy = pltpu.make_async_copy(window, result.at[:, 0], sem)
    for end in range(2):

        def read(j, scratch):
            for k in range(partners):
                for c in range(2):
                    left, right = (before, own) if end == 0 else (own, after)
                    value = jnp.where(lane % SIDE < 8, left[k, j, c], right[k, j, c])
                    at = pl.multiple_of(c * total + (me ^ k) * n, SIDE)
                    scratch[pl.ds(at, n), :] = value

        def emit(u, real, imag):
            if end == 0:
                store_coherence(window, (u,), state[u, 0] + real, state[u, 1] + imag)
            else:
                out[u, 0] = real
                out[u, 1] = imag

        column_sums(read, pixels.at[end], row_blocks, emit)
        if end == 0:
            copy.start()
    copy.wait()


def rim_gram(me, own, before, after, state, result):
    partners, row_blocks, _, n, _ = own.shape
    total = n * partners
    whole = pl.BlockSpec(memory_space=pltpu.VMEM)
    anywhere = pl.BlockSpec(memory_space=pl.ANY)
    return pl.pallas_call(
        rim_gram_kernel,
        in_specs=[pl.BlockSpec(memory_space=pltpu.SMEM)] + [whole] * 4 + [anywhere],
        out_specs=[anywhere, whole],
        out_shape=[
            jax.ShapeDtypeStruct(result.shape, f32),
            jax.ShapeDtypeStruct(state.shape, f32),
        ],
        input_output_aliases={5: 0},
        scratch_shapes=[
            pltpu.VMEM(state.shape, f32),
            pltpu.VMEM((2, row_blocks, 2 * total, PIX), bf16),
            pltpu.SemaphoreType.DMA,
        ],
        compiler_params=params(),
        cost_estimate=COST,
        name="rim_gram",
    )(me, own, before, after, state, result)


def gram_kernel(partners, parts, offsets, columns, first, opening, closing, *refs):
    pieces, refs = refs[: partners * parts], refs[partners * parts :]
    if not opening:
        state, end, _, *refs = refs
    result, *refs = refs
    if opening:
        first_out, *refs = refs
    state_out, held, kept, *blocks, stage, pixels, in_sems, out_sems, state_sems = refs
    row_blocks = pieces[0].shape[0]
    me = lax.axis_index("date").astype(jnp.int32)
    total = pixels.shape[1] // 2

    placed = [n for n in range(parts, partners * parts) if closing and n % parts == parts - 1]

    def fetch(column):
        return [
            pltpu.make_async_copy(
                pieces[n].at[:, offsets[n % parts] + column], blocks[n].at[column], in_sems.at[column, n]
            )
            for n in range(partners * parts)
            if n not in placed
        ]

    def write(window):
        return pltpu.make_async_copy(stage.at[window], result.at[:, first - 1 + window], out_sems.at[window])

    def start(column, carry):
        for copy in fetch(column):
            copy.start()
        return carry

    if not opening:
        state_in = pltpu.make_async_copy(state, held, state_sems.at[0])
        state_in.start()
    lax.fori_loop(0, columns, start, 0)
    if closing:
        end_in = pltpu.make_async_copy(end, kept, state_sems.at[1])
        end_in.start()
    if opening:
        first_copy = pltpu.make_async_copy(kept, first_out, state_sems.at[1])
    else:
        state_in.wait()

    def work(column, carry):
        for copy in fetch(column):
            copy.wait()

        def read(j, scratch):
            for k in range(partners):
                for p in range(parts):
                    for c in range(2):
                        at = pl.multiple_of(c * total + (me ^ k) * (parts * DBLK) + p * DBLK, DBLK)
                        n = k * parts + p
                        here = pieces[n][j, column, c] if n in placed else blocks[n][column, j, c]
                        scratch[pl.ds(at, DBLK), :] = here

        def emit(u, real, imag):
            store_coherence(stage.at[column], (u,), held[u, 0] + real, held[u, 1] + imag)
            held[u, 0] = real
            held[u, 1] = imag

        column_sums(read, pixels, row_blocks, emit)
        if opening:

            @pl.when(column == 0)
            def _():
                kept[...] = held[...]
                first_copy.start()

            pl.when(column > 0)(write(column).start)
        else:
            write(column).start()
        return carry

    lax.fori_loop(0, columns, work, 0)
    if closing:
        end_in.wait()
        for u in range(row_blocks - 1):
            store_coherence(stage.at[columns], (u,), held[u, 0] + kept[u, 0], held[u, 1] + kept[u, 1])
        write(columns).start()
    else:
        state_copy = pltpu.make_async_copy(held, state_out, state_sems.at[0])
        state_copy.start()
    for window in range(1 if opening else 0, columns + (1 if closing else 0)):
        write(window).wait()
    if opening:
        first_copy.wait()
    if not closing:
        state_copy.wait()


def gram(pieces, offsets, columns, first, state, end, result, out_shape, closing):
    partners, parts = len(pieces), len(pieces[0])
    row_blocks = pieces[0][0].shape[0]
    total = out_shape.shape[-1]
    opening = state is None
    sums = jax.ShapeDtypeStruct((row_blocks - 1, 2, total, total), f32)
    anywhere = pl.BlockSpec(memory_space=pl.ANY)
    operands = [x for k in pieces for x in k]
    aliases = {}
    if not opening:
        aliases = {len(operands) + 2: 0}
        operands += [state, end, result]
    n_out = 2 if opening else 1
    return pl.pallas_call(
        functools.partial(gram_kernel, partners, parts, offsets, columns, first, opening, closing),
        in_specs=[
            pl.BlockSpec(memory_space=pltpu.VMEM)
            if closing and parts <= n < partners * parts and n % parts == parts - 1
            else anywhere
            for n in range(len(operands))
        ],
        out_specs=[anywhere] * (1 + n_out),
        out_shape=[out_shape] + [sums] * n_out,
        input_output_aliases=aliases,
        scratch_shapes=[pltpu.VMEM(sums.shape, f32)] * 2
        + [pltpu.VMEM((columns, row_blocks, 2, DBLK, PIX), bf16)] * (partners * parts)
        + [
            pltpu.VMEM((columns + (1 if closing else 0), *sums.shape), f32),
            pltpu.VMEM((row_blocks, 2 * total, PIX), bf16),
            pltpu.SemaphoreType.DMA((columns, partners * parts)),
            pltpu.SemaphoreType.DMA((columns + 1,)),
            pltpu.SemaphoreType.DMA((2,)),
        ],
        compiler_params=params(),
        cost_estimate=COST,
        name=f"gram_{first}",
    )(*operands)


def shift(value, axis, by):
    n = lax.axis_size(axis)
    pairs = [(i, i + by) for i in range(n) if 0 <= i + by < n]
    return lax.ppermute(value, axis, pairs)


def exchange(blocks, ahead=None, gates=()):
    n = lax.axis_size("date")
    got = [blocks[0]]
    for k in range(1, n):
        block = blocks[k]
        if ahead is not None:
            block = after(block, ahead[k])
        if k == 1 and gates:
            block = after(block, *gates)
        got.append(lax.ppermute(block, "date", [(i, i ^ k) for i in range(n)]))
    if gates:
        got = got[:1] + [pltpu.with_memory_space_constraint(x, pltpu.VMEM) for x in got[1:]]
    return got


def after(value, *others):
    return lax.optimization_barrier((value, *others))[0]


def on_device(slc, range_kernel, azimuth_kernel):
    partners = lax.axis_size("date")
    n_dates, n_rows, n_az = slc.shape[1:]
    total = n_dates * partners
    columns = n_az // SIDE
    me = lax.axis_index("date").astype(jnp.int32).reshape(1)
    parts = n_dates // DBLK
    bounds = [1, 6, 13, columns]
    spans = list(zip(bounds[:-1], bounds[1:]))

    dest_windows = n_rows // partners // SIDE
    out_shape = jax.ShapeDtypeStruct((dest_windows, columns, 2, total, total), f32)

    own, left, right, sent = [], [], [], []
    turn = me
    for part in range(parts):
        part_spans = spans if part == parts - 1 else [(1, columns)]
        source = (slc, range_kernel, azimuth_kernel, part, part_spans)
        if part == 0:
            _, lead = interior(turn, *source, [partners - 1], False, partners)
            turn = after(me, lead[0][0])
        targets = [*range(1, partners - 1 if part == 0 else partners), 0]
        (edge, first, last), out = interior(turn, *source, targets, True, partners)
        turn = after(me, first)
        own.append(edge)
        left.append(shift(last, "strip", 1))
        right.append(shift(first, "strip", -1))
        if part == 0:
            out = [[x[-1], *x[:-1], y[0]] for x, y in zip(out, lead)]
        else:
            out = [[x[-1], *x[:-1]] for x in out]
        sent.append(out)
    early = [exchange(s[0]) for s in sent[:-1]]
    lead = [early[-1][-1]] if early else []
    rims = exchange([after(x, *lead) for x in rim(me, own, left, right, azimuth_kernel, partners)])
    first = [*sent[-1][0][:-1], after(sent[-1][0][-1], *rims)]
    late = [exchange(first, early[-1] if early else None)]
    rims = jnp.stack(rims)
    above, below = shift(rims, "strip", 1), shift(rims, "strip", -1)

    def column_gram(s, state, end, result):
        lo, hi = spans[s]
        pieces = [[e[k] for e in early] + [late[s][k]] for k in range(partners)]
        offsets = [lo - 1] * (parts - 1) + [0]
        closing = s == len(spans) - 1
        return gram(pieces, offsets, hi - lo, lo, state, end, result, out_shape, closing)

    late.append(exchange(sent[-1][1], late[0]))
    result, opening, state = column_gram(0, None, None, None)
    result, end = rim_gram(me, rims, above, below, opening, result)
    for s in range(1, len(spans) - 1):
        result, state = column_gram(s, state, end, result)
        late.append(exchange(sent[-1][s + 1], late[s], gates=(end,)))
    result, state = column_gram(len(spans) - 1, state, end, result)
    return result


def solution(mesh):
    in_specs = (P(None, "date", None, "strip"), P("date", None, None), P("date", None, "strip"))
    out_specs = P("date", "strip", None, None, None)
    return jax.shard_map(on_device, mesh=mesh, in_specs=in_specs, out_specs=out_specs, check_vma=False)
```
